32 devices in a mesh: dp: 2 (over core), seq: 16 (over z, y, x).
Axes of the slice: x: 2, y: 2, z: 4, core: 2. Of those that a mesh axis runs over, the one named last changes fastest.
Arguments:
- tokens: bfloat16 [4, 8192, 768], P('dp', 'seq'), may hold values from -6 to 6
- segments: int32 [4, 8192], P('dp'), may hold values from 0 to 15, as said below
- cotangent: bfloat16 [4, 8192, 768], P('dp', 'seq'), may hold values from -6 to 6
- ln1_gain: bfloat16 [768], P(('dp', 'seq')), may hold values from 0.5 to 1.5
- ln1_bias: bfloat16 [768], P(('dp', 'seq')), may hold values from -3 to 3
- w_qkv: bfloat16 [768, 2304], P(('dp', 'seq')), may hold values from -0.21875 to 0.21875
- pool_taps: bfloat16 [5, 1536], P(None, ('dp', 'seq')), may hold values from -2.6875 to 2.6875
- w_out: bfloat16 [768, 768], P(('dp', 'seq')), may hold values from -1.75 to 1.75
- ln2_gain: bfloat16 [768], P(('dp', 'seq')), may hold values from 0.5 to 1.5
- ln2_bias: bfloat16 [768], P(('dp', 'seq')), may hold values from -3 to 3
- w_up: bfloat16 [768, 3072], P(('dp', 'seq')), may hold values from -0.21875 to 0.21875
- w_down: bfloat16 [3072, 768], P(None, ('dp', 'seq')), may hold values from -0.109375 to 0.109375
Outputs:
- output: bfloat16 [4, 8192, 768], P('dp', 'seq')
- input_grad: float32 [4, 8192, 768], P('dp', 'seq')
- grad_ln1_gain: float32 [768], P(('dp', 'seq'))
- grad_ln1_bias: float32 [768], P(('dp', 'seq'))
- grad_w_qkv: float32 [768, 2304], P(('dp', 'seq'))
- grad_pool_taps: float32 [5, 1536], P(None, ('dp', 'seq'))
- grad_w_out: float32 [768, 768], P(('dp', 'seq'))
- grad_ln2_gain: float32 [768], P(('dp', 'seq'))
- grad_ln2_bias: float32 [768], P(('dp', 'seq'))
- grad_w_up: float32 [768, 3072], P(('dp', 'seq'))
- grad_w_down: float32 [3072, 768], P(None, ('dp', 'seq'))
The draws below stay inside these ranges and needn't reach their ends.
Inputs may be any that keep to these rules, and one draw needn't show every extreme that they name: `segments`: within a row the numbers start at 0 and rise by one at the start of each document; in each aligned group of 2 rows one row holds a single document and every other row holds exactly max(16, 2) documents.
All inputs are finite; a program needn't handle non-finite values.
Results may differ from the reference program's by a relative error of at most 0.013.
Values may be sent and summed in bfloat16 or wider, within the bound.
A program may use at most 256 MiB of HBM per device.

```python
import jax
import jax.numpy as jnp
from jax import lax

D = 768
HEADS = 12
HEAD = 64
FF = 3072
MICRO = 2
LOCAL_HALF = 64
POOL_REACH = 256
ROWS = 4
LENGTH = 8192


def draw_segments(key, part):
    key = jax.random.fold_in(key, 7)
    split_keys = jax.random.split(key, 2)
    doc_count = max(LENGTH // 512, 2)
    positions = jnp.arange(LENGTH, dtype=jnp.int32)
    scores = jax.random.randint(split_keys[0], (ROWS, LENGTH), 0, 16384) * LENGTH + positions[None, :]
    scores = jnp.where(positions[None, :] > 0, scores, -1)
    picked_scores, picked_index = lax.top_k(scores, doc_count - 1)
    starts = jnp.sum((picked_index[:, :, None] == positions[None, None, :]).astype(jnp.int32), axis=1)
    chosen = jax.random.randint(split_keys[1], (ROWS // MICRO,), 0, MICRO)
    row_ids = jnp.arange(ROWS, dtype=jnp.int32)
    single = row_ids % MICRO == chosen[row_ids // MICRO]
    starts = jnp.where(single[:, None], 0, starts)
    return jnp.cumsum(starts, axis=1).astype(jnp.int32)


def level_of(stream_key, dims, cuts, smallest, high):
    level, own = 1.0, jax.random.fold_in(stream_key, 6)
    for axis_at, shards_of in cuts:
        steps = jnp.exp(jax.random.uniform(jax.random.fold_in(own, axis_at), (shards_of,), jnp.float32, smallest / len(cuts), high / len(cuts)))
        level = level * jnp.repeat(steps, dims[axis_at] // shards_of).reshape([-1 if axis == axis_at else 1 for axis in range(len(dims))])
    return level


def gaussian(stream_key, shape, deviation, most, cuts=(), kind=jnp.bfloat16):
    factor_of = level_of(stream_key, shape, cuts, -0.22, 0.18) if cuts else 1.0
    values = jax.random.normal(stream_key, shape, jnp.float32) * deviation * factor_of
    return jnp.minimum(jnp.maximum(values, -most), most).astype(kind)


def setup_inputs(seed: int = 0) -> dict:
    key_list = jax.random.split(jax.random.key(seed), 13)
    return {
        "tokens": gaussian(key_list[0], (ROWS, LENGTH, D), 1.0, 6.0, ((0, 2), (1, 16))),
        "segments": draw_segments(jax.random.fold_in(key_list[12], 71), 0),
        "cotangent": gaussian(key_list[2], (ROWS, LENGTH, D), 1.0, 6.0, ((0, 2), (1, 16))),
        "ln1_gain": jnp.clip(1.0 + 0.1 * jax.random.normal(key_list[3], (D,), jnp.float32), 0.5, 1.5).astype(jnp.bfloat16),
        "ln1_bias": gaussian(key_list[4], (D,), 0.3, 3.0, ((0, 32),)),
        "w_qkv": gaussian(key_list[5], (D, 3 * D), D ** -0.5, 0.21875, ((0, 32),)),
        "pool_taps": gaussian(key_list[6], (5, 2 * D), 0.45, 2.6875, ((1, 32),)),
        "w_out": gaussian(key_list[7], (D, D), (D // 64) ** -0.5, 1.75, ((0, 32),)),
        "ln2_gain": jnp.clip(1.0 + 0.1 * jax.random.normal(key_list[8], (D,), jnp.float32), 0.5, 1.5).astype(jnp.bfloat16),
        "ln2_bias": gaussian(key_list[9], (D,), 0.3, 3.0, ((0, 32),)),
        "w_up": gaussian(key_list[10], (D, FF), D ** -0.5, 0.21875, ((0, 32),)),
        "w_down": gaussian(key_list[11], (FF, D), FF ** -0.5, 0.109375, ((1, 32),)),
    }


@jax.custom_vjp
def low(v):
    return lax.optimization_barrier(v.astype(jnp.bfloat16)).astype(jnp.float32)

@jax.custom_vjp
def low_back(v):
    return v

def low_keep(v):
    return (low(v), None)

def low_pass(kept, grad):
    return (grad,)

def back_keep(v):
    return (v, None)

def back_low(kept, grad):
    return (low(grad),)
low.defvjp(low_keep, low_pass)
low_back.defvjp(back_keep, back_low)
highest = lax.Precision.HIGHEST

def layer_norm(inputs, norm_gain, norm_bias):
    middle = lax.optimization_barrier(jnp.mean(inputs, axis=-1, keepdims=True))
    centred = inputs - middle
    spread = lax.optimization_barrier(jnp.mean(centred * centred, axis=-1, keepdims=True))
    return centred * lax.rsqrt(spread + 1e-05) * norm_gain + norm_bias

def pool_row(key_value, pool_taps, segment_row):
    length = key_value.shape[0]
    padded = jnp.pad(key_value, ((2, 2), (0, 0)))
    seg_padded = jnp.pad(segment_row, (2, 2), constant_values=-1)
    anchors = segment_row[0::4]
    pooled = jnp.zeros((length // 4, key_value.shape[1]), jnp.float32)
    for offset in range(5):
        picked = padded[offset:offset + length:4]
        same_doc = (seg_padded[offset:offset + length:4] == anchors).astype(jnp.float32)
        pooled = pooled + pool_taps[offset] * picked * same_doc[:, None]
    return pooled

def attend_block(q_block, k_block, v_block, pk_block, pv_block, seg_query, seg_key, seg_pool):
    block_rows = q_block.shape[0]
    q_index = jnp.arange(block_rows, dtype=jnp.int32)
    k_index = jnp.arange(k_block.shape[0], dtype=jnp.int32)
    p_index = jnp.arange(pk_block.shape[0], dtype=jnp.int32)
    near_mask = (jnp.abs(q_index[:, None] - k_index[None, :] + LOCAL_HALF) <= LOCAL_HALF) & (seg_query[:, None] == seg_key[None, :])
    far_mask = (jnp.abs(4 * p_index[None, :] - POOL_REACH - q_index[:, None]) <= POOL_REACH) & (seg_query[:, None] == seg_pool[None, :])
    score_scale = HEAD ** (-0.5)
    near_scores = low_back(jnp.einsum('qhd,khd->hqk', q_block, k_block, precision=highest) * score_scale)
    far_scores = low_back(jnp.einsum('qhd,khd->hqk', q_block, pk_block, precision=highest) * score_scale)
    near_scores = jnp.where(near_mask[None], near_scores, -1e+30)
    far_scores = jnp.where(far_mask[None], far_scores, -1e+30)
    row_max = jnp.maximum(lax.optimization_barrier(jnp.max(near_scores, axis=2, keepdims=True)), lax.optimization_barrier(jnp.max(far_scores, axis=2, keepdims=True)))
    near_exp = jnp.where(near_mask[None], jnp.exp(near_scores - row_max), 0.0)
    far_exp = jnp.where(far_mask[None], jnp.exp(far_scores - row_max), 0.0)
    row_total = lax.optimization_barrier(jnp.sum(near_exp, axis=2, keepdims=True)) + lax.optimization_barrier(jnp.sum(far_exp, axis=2, keepdims=True))
    near_prob = low(near_exp / row_total)
    far_prob = low(far_exp / row_total)
    mixed_sum = jnp.einsum('hqk,khd->qhd', near_prob, v_block, precision=highest) + jnp.einsum('hqk,khd->qhd', far_prob, pv_block, precision=highest)
    return mixed_sum.reshape(block_rows, D)

def attend_row(queries, keys, values, pooled_keys, pooled_values, segment_row):
    length = queries.shape[0]
    pool_half = POOL_REACH // 4
    block_size = 512
    key_pad = jnp.pad(keys, ((LOCAL_HALF, LOCAL_HALF), (0, 0), (0, 0)))
    value_pad = jnp.pad(values, ((LOCAL_HALF, LOCAL_HALF), (0, 0), (0, 0)))
    pkey_pad = jnp.pad(pooled_keys, ((pool_half, pool_half), (0, 0), (0, 0)))
    pvalue_pad = jnp.pad(pooled_values, ((pool_half, pool_half), (0, 0), (0, 0)))
    seg_token_pad = jnp.pad(segment_row, (LOCAL_HALF, LOCAL_HALF), constant_values=-1)
    anchor_pad = jnp.pad(segment_row[0::4], (pool_half, pool_half), constant_values=-1)

    def one_block(block_index):
        start_row = (block_index * block_size).astype(jnp.int32)
        pool_start = (block_index * (block_size // 4)).astype(jnp.int32)
        q_block = lax.dynamic_slice_in_dim(queries, start_row, block_size, 0)
        k_block = lax.dynamic_slice_in_dim(key_pad, start_row, block_size + 2 * LOCAL_HALF, 0)
        v_block = lax.dynamic_slice_in_dim(value_pad, start_row, block_size + 2 * LOCAL_HALF, 0)
        pk_block = lax.dynamic_slice_in_dim(pkey_pad, pool_start, block_size // 4 + 2 * pool_half, 0)
        pv_block = lax.dynamic_slice_in_dim(pvalue_pad, pool_start, block_size // 4 + 2 * pool_half, 0)
        seg_query = lax.dynamic_slice_in_dim(segment_row, start_row, block_size, 0)
        seg_key = lax.dynamic_slice_in_dim(seg_token_pad, start_row, block_size + 2 * LOCAL_HALF, 0)
        seg_pool = lax.dynamic_slice_in_dim(anchor_pad, pool_start, block_size // 4 + 2 * pool_half, 0)
        return attend_block(q_block, k_block, v_block, pk_block, pv_block, seg_query, seg_key, seg_pool)
    pieces = lax.map(jax.checkpoint(one_block), jnp.arange(length // block_size, dtype=jnp.int32))
    return pieces.reshape(length, D)

def reference(tokens, segments, cotangent, ln1_gain, ln1_bias, w_qkv, pool_taps, w_out, ln2_gain, ln2_bias, w_up, w_down):

    def forward(inputs, gain_one, bias_one, proj_qkv, taps, proj_out, gain_two, bias_two, proj_up, proj_down):
        flat_in = inputs.reshape(-1, D)
        normed = low(layer_norm(flat_in, gain_one, bias_one))
        projected = low(low_back(jnp.dot(normed, proj_qkv, precision=highest)))
        projected = projected.reshape(ROWS, LENGTH, 3 * D)

        def one_row(packed):
            proj_row, segment_row = packed
            queries = proj_row[:, :D].reshape(LENGTH, HEADS, HEAD)
            key_value = proj_row[:, D:]
            pooled = low(pool_row(key_value, taps, segment_row))
            return attend_row(queries, key_value[:, :D].reshape(LENGTH, HEADS, HEAD), key_value[:, D:].reshape(LENGTH, HEADS, HEAD), pooled[:, :D].reshape(LENGTH // 4, HEADS, HEAD), pooled[:, D:].reshape(LENGTH // 4, HEADS, HEAD), segment_row)
        attended = lax.map(one_row, (projected, segments))
        attended = low(low_back(attended.reshape(-1, D)))
        branch = low_back(jnp.dot(attended, proj_out, precision=highest))
        middle = flat_in + branch
        normed_two = low(layer_norm(middle, gain_two, bias_two))
        upward = low_back(jnp.dot(normed_two, proj_up, precision=highest))
        activated = low(jax.nn.gelu(upward))
        result = middle + jnp.dot(activated, proj_down, precision=highest)
        return result.reshape(ROWS, LENGTH, D)
    params = tuple((weight.astype(jnp.float32) for weight in (tokens, ln1_gain, ln1_bias, w_qkv, pool_taps, w_out, ln2_gain, ln2_bias, w_up, w_down)))
    result, pullback = jax.vjp(forward, *params)
    gradients = pullback(cotangent.astype(jnp.float32))
    return (result.astype(jnp.bfloat16), gradients[0], gradients[1], gradients[2], gradients[3], gradients[4], gradients[5], gradients[6], gradients[7], gradients[8], gradients[9])
```

```python
import functools

import jax
import jax.numpy as jnp
from jax import lax
from jax.experimental import pallas as pl
from jax.experimental.pallas import tpu as pltpu
from jax.sharding import PartitionSpec as P

HEADS = 12
HEAD = 64
NEAR = 64
REACH = 256
F32, BF = jnp.float32, jnp.bfloat16
NT = (((1,), (1,)), ((), ()))
TN = (((0,), (0,)), ((), ()))
NN = (((1,), (0,)), ((), ()))
MESH = pl.DeviceIdType.MESH
ANY = pl.BlockSpec(memory_space=pl.ANY)
VM = pl.BlockSpec(memory_space=pltpu.VMEM)
VMEM_LIMIT = 62 * 2**20
UNIT = 384
CLS = 3456
WIDE = 3584
PLACE = {"qkv": (0, 0, 2304), "out": (1, 0, 768), "up": (1, 3, 3072), "down": (1, 15, 3072)}


def dg(a, b, dims):
    return lax.dot_general(a, b, dims, preferred_element_type=F32)


def spot(name, unit):
    first, start, _ = PLACE[name]
    at = start + unit
    return first + at // 9, (at % 9) * UNIT


def units(name):
    return PLACE[name][2] // UNIT


def where_am_i():
    c = lax.axis_index("dp")
    s = lax.axis_index("seq")
    z, col = s // 4, s % 4
    x, y = col % 2, col // 2
    colx, coly, cold = y * 2 + (1 - x), (1 - y) * 2 + x, 3 - col
    return dict(
        c=c, s=s, z=z, col=col, colx=colx, coly=coly, cold=cold,
        px=(c, z * 4 + colx), py=(c, z * 4 + coly), pd=(1 - c, s),
    )


def greet(me, halo):
    bar = pltpu.get_barrier_semaphore()
    who = [me["px"], me["py"], me["pd"]]
    who += [(me["c"], lax.rem(me["z"] + j, 4) * 4 + me["col"]) for j in (1, 2, 3)]
    for dev in who:
        pl.semaphore_signal(bar, inc=1, device_id=dev, device_id_type=MESH)
    count = 6
    if halo:
        last = lax.axis_size("seq") - 1

        @pl.when(me["s"] > 0)
        def _():
            pl.semaphore_signal(bar, inc=1, device_id=(me["c"], me["s"] - 1), device_id_type=MESH)

        @pl.when(me["s"] < last)
        def _():
            pl.semaphore_signal(bar, inc=1, device_id=(me["c"], me["s"] + 1), device_id_type=MESH)

        count = 6 + (me["s"] > 0).astype(jnp.int32) + (me["s"] < last).astype(jnp.int32)
    pl.semaphore_wait(bar, count)


def lane_low():
    return lax.broadcasted_iota(jnp.int32, (128, 128), 1) < HEAD


def pair_rows(v):
    low = lane_low()
    zero = jnp.zeros_like(v)
    return jnp.concatenate([jnp.where(low, v, zero), jnp.where(low, zero, v)], axis=0)


def pair_out(t):
    return jnp.concatenate([t[:HEAD, :128], t[HEAD:, 128:]], axis=0).T


def softmax_block(q2, kn, kf, bias):
    st = jnp.concatenate([dg(kn, q2, NT), dg(kf, q2, NT)], axis=0)
    st = st + jnp.concatenate([bias, bias], axis=1)
    top = jnp.max(st, axis=0, keepdims=True)
    e = jnp.exp(st - top)
    total = jnp.sum(e, axis=0, keepdims=True)
    return e, 1.0 / total


def mask_block(winc, win4, winr, r, b):
    seg_q = winr[r : r + 1, 256 + 128 * b : 384 + 128 * b]
    kk = lax.broadcasted_iota(jnp.int32, (256, 128), 0)
    ii = lax.broadcasted_iota(jnp.int32, (256, 128), 1)
    seg_k = winc[r, 192 + 128 * b : 448 + 128 * b, :]
    near = (jnp.abs(kk - NEAR - ii) <= NEAR) & (seg_k == seg_q)
    pp = lax.broadcasted_iota(jnp.int32, (160, 128), 0)
    qi = lax.broadcasted_iota(jnp.int32, (160, 128), 1)
    seg_p = win4[r, 32 * b : 32 * b + 160, 0:1]
    far = (jnp.abs(4 * pp - REACH - qi) <= REACH) & (seg_p == seg_q)
    return jnp.where(near, 0.0, -1e30), jnp.where(far, 0.0, -1e30)


def fill_masks(winc, win4, winr, bias):
    for r in range(2):
        for b in range(4):
            near, far = mask_block(winc, win4, winr, r, b)
            bias[r * 4 + b, 0:256] = near
            bias[r * 4 + b, 256:416] = far


def head_lanes(h):
    return (
        pl.ds(pl.multiple_of(h * 128, 128), 128),
        pl.ds(pl.multiple_of(768 + h * 128, 128), 128),
    )


def attend(q, kv, pe, bias, att, r, h):
    kl, vl = head_lanes(h)
    for b in range(4):
        n, f, i = slice(b * 128, b * 128 + 256), slice(b * 32, b * 32 + 160), slice(b * 128, b * 128 + 128)
        e, rt = softmax_block(pair_rows(q[r, i, kl]), kv[r, n, kl], pe[r, f, kl], bias[r * 4 + b])
        low = (e * rt).astype(BF)
        values = jnp.concatenate([kv[r, n, vl], pe[r, f, vl]], axis=0)
        att[r, i, kl] = pair_out(dg(values, low, TN)).astype(BF)


def attend_back(q, kv, pe, bias, g, gext, dkv, dpe, r, h):
    kl, vl = head_lanes(h)
    for part in (h, 6 + h):
        dkv[r, part] = jnp.zeros((640, 128), F32)
        dpe[r, part] = jnp.zeros((256, 128), F32)
    for b in range(4):
        n, f, i = slice(b * 128, b * 128 + 256), slice(b * 32, b * 32 + 160), slice(b * 128, b * 128 + 128)
        q2, g2 = pair_rows(q[r, i, kl]), pair_rows(g[r, i, kl])
        kn, vn, kf, vf = kv[r, n, kl], kv[r, n, vl], pe[r, f, kl], pe[r, f, vl]
        e, rt = softmax_block(q2, kn, kf, bias[r * 4 + b])
        p = e * rt
        dp = jnp.concatenate([dg(vn, g2, NT), dg(vf, g2, NT)], axis=0)
        delta = jnp.sum(p * dp, axis=0, keepdims=True)
        ds = (p * (dp - delta)).astype(BF)
        low = p.astype(BF)
        dv, dk = dg(low, g2, NN), dg(ds, q2, NN)
        dkv[r, h, n] += dk[:256]
        dkv[r, 6 + h, n] += dv[:256]
        dpe[r, h, f] += dk[256:]
        dpe[r, 6 + h, f] += dv[256:]
        dqt = dg(jnp.concatenate([kn, kf], axis=0), ds, TN)
        gext[r, 64 + b * 128 : 192 + b * 128, kl] = (pair_out(dqt) * HEAD**-0.5).astype(BF)


def norm_parts(v):
    mean = jnp.mean(v, axis=-1, keepdims=True)
    cen = v - mean
    var = jnp.mean(cen * cen, axis=-1, keepdims=True)
    rs = lax.rsqrt(var + 1e-05)
    return cen * rs, rs


def pack_own(grab, put):
    for name in ("qkv", "out", "up", "down"):
        half = units(name) // 2
        for u in range(units(name)):
            k, lo = spot(name, u)
            put(k, lo, grab(name, 0, 16, u))
        for u in range(half):
            k, lo = spot(name, units(name) + u)
            put(k, lo, jnp.concatenate([grab(name, 16, 24, u), grab(name, 16, 24, u + half)], axis=0))


def unpack(name, got, dst):
    half = units(name) // 2

    def pair(i, carry):
        rows = pl.ds(pl.multiple_of(48 * i, 16), 48)
        for u in range(units(name)):
            k, lo = spot(name, u)
            kt, lt = spot(name, units(name) + u % half)
            cut = slice(0, 8) if u < half else slice(8, 16)
            parts = []
            for j in (0, 1):
                parts.append(got[k, 2 * i + j, :, lo : lo + UNIT])
                parts.append(got[kt, 2 * i + j, :, lt : lt + UNIT][cut])
            dst[rows, u * UNIT : (u + 1) * UNIT] = jnp.concatenate(parts, axis=0)
        return carry

    lax.fori_loop(0, 16, pair, 0)


def spread_small(got, taps, gains):
    lane = lax.broadcasted_iota(jnp.int32, (16, 128), 1)

    def place(width, tiles):
        acc = [jnp.zeros((16, 128), F32) for _ in range(tiles)]
        for s in range(32):
            at, off = divmod(width * s, 128)
            v = jnp.where(lane < width, got[0, s, :, CLS:WIDE].astype(F32), 0.0)
            v = pltpu.roll(v, off, 1) if off else v
            acc[at] = acc[at] + jnp.where(lane >= off, v, 0.0)
            if off + width > 128:
                acc[at + 1] = acc[at + 1] + jnp.where(lane < off, v, 0.0)
        return acc

    for i, v in enumerate(place(48, 12)):
        taps[:, i * 128 : (i + 1) * 128] = v
    for i, v in enumerate(place(24, 6)):
        gains[:, i * 128 : (i + 1) * 128] = v


def front_kernel(
    tok, winc, win4, winr, wq, wo, wu, wd, small,
    o_wq, o_wo, o_wu, o_wd, o_taps, o_gains, o_h1, o_q, o_kv, o_pe, o_att, o_bias,
    G, Wq, Wo, Wu, Wd, taps, gains, xe, h1, q, kv, pe, att, bias, chunk,
    send_x, send_y, send_d, send_z, send_g, recv, hsend, hrecv, local,
):
    me = where_am_i()
    c, s, z, col = me["c"], me["s"], me["z"], me["col"]
    mine = c * 16 + s
    last = lax.axis_size("seq") - 1
    has_left, has_right = s > 0, s < last

    def cols(k):
        return WIDE if isinstance(k, int) and k == 0 else CLS

    def hop(k, slot, to, sem):
        part = G.at[k, slot, :, pl.ds(0, cols(k))]
        return pltpu.make_async_remote_copy(
            src_ref=part, dst_ref=part, send_sem=sem, recv_sem=recv.at[k, slot],
            device_id=to, device_id_type=MESH,
        )

    def to_x(k, at):
        return hop(k, c * 16 + at, me["px"], send_x.at[k, at])

    def to_y(k, at):
        return hop(k, c * 16 + at, me["py"], send_y.at[k, at])

    def to_d(k, at):
        return hop(k, c * 16 + at, me["pd"], send_d.at[k, at])

    def to_z(k, j):
        return hop(k, mine, (c, lax.rem(z + j, 4) * 4 + col), send_z.at[k, j - 1])

    def to_g(k, zz):
        even = lax.rem(zz, 2) == 0
        at = zz * 4 + jnp.where(even, me["colx"], me["coly"])
        to = (c, z * 4 + jnp.where(even, me["coly"], me["colx"]))
        return hop(k, c * 16 + at, to, send_g.at[k, zz])

    def got(k, slot):
        hop(k, slot, me["px"], send_x.at[k, 0]).wait_recv()

    def own(k):
        for j in (1, 2, 3):
            to_z(k, j).start()
        to_x(k, s).start()
        to_y(k, s).start()
        to_d(k, s).start()

    def column(k, j):
        at = lax.rem(z + j, 4) * 4 + col
        got(k, c * 16 + at)
        to_x(k, at).start()
        to_y(k, at).start()
        to_d(k, at).start()

    def plane(k, j):
        zz = lax.rem(z + j, 4)
        got(k, c * 16 + zz * 4 + me["colx"])
        to_d(k, zz * 4 + me["colx"]).start()
        got(k, c * 16 + zz * 4 + me["coly"])
        to_d(k, zz * 4 + me["coly"]).start()
        to_g(k, zz).start()

    def diag(k, j):
        at = lax.rem(z + j, 4) * 4 + me["cold"]
        got(k, c * 16 + at)
        to_d(k, at).start()

    def event(e):
        k, i = e // 11 + 1, lax.rem(e, 11)

        @pl.when(i < 4)
        def _():
            plane(k, i)

        @pl.when((i >= 4) & (i < 7) & (k < 3))
        def _():
            column(k + 1, i - 3)

        @pl.when(i >= 7)
        def _():
            diag(k, i - 7)

    def halo_tok(r, right):
        src = tok.at[r, pl.ds(448 if right else 0, 64)]
        dst = xe.at[r, pl.ds(0 if right else 576, 64)]
        i = r * 2 + int(right)
        return pltpu.make_async_remote_copy(
            src_ref=src, dst_ref=dst, send_sem=hsend.at[i], recv_sem=hrecv.at[i],
            device_id=(c, s + 1 if right else s - 1), device_id_type=MESH,
        )

    def halo_pool(r, right):
        src = pe.at[r, pl.ds(128 if right else 64, 64)]
        dst = pe.at[r, pl.ds(0 if right else 192, 64)]
        i = 4 + r * 2 + int(right)
        return pltpu.make_async_remote_copy(
            src_ref=src, dst_ref=dst, send_sem=hsend.at[i], recv_sem=hrecv.at[i],
            device_id=(c, s + 1 if right else s - 1), device_id_type=MESH,
        )

    def both(make, r, act):
        @pl.when(has_right)
        def _():
            act(make(r, True), True)

        @pl.when(has_left)
        def _():
            act(make(r, False), False)

    def arrived(make, r):
        @pl.when(has_left)
        def _():
            make(r, True).wait_recv()

        @pl.when(has_right)
        def _():
            make(r, False).wait_recv()

    load = [pltpu.make_async_copy(tok.at[r], xe.at[r, pl.ds(64, 512)], local.at[r]) for r in range(2)]
    for copy in load:
        copy.start()
    shares = {"qkv": wq, "out": wo, "up": wu, "down": wd}

    def grab(name, a, b, u):
        return shares[name][a:b, u * UNIT : (u + 1) * UNIT]

    def put(k, lo, v):
        G[k, mine, :, lo : lo + UNIT] = v

    pack_own(grab, put)
    G[0, mine, :, CLS:WIDE] = small[...]

    @pl.when(jnp.logical_not(has_left))
    def _():
        for r in range(2):
            xe[r, 0:64] = jnp.zeros((64, 768), BF)
            pe[r, 0:64] = jnp.zeros((64, 1536), BF)

    @pl.when(jnp.logical_not(has_right))
    def _():
        for r in range(2):
            xe[r, 576:640] = jnp.zeros((64, 768), BF)
            pe[r, 192:256] = jnp.zeros((64, 1536), BF)

    greet(me, True)
    own(0)
    for r in range(2):
        both(halo_tok, r, lambda copy, right: copy.start())
    own(1)
    own(2)
    fill_masks(winc, win4, winr, bias)
    for j in (1, 2, 3):
        column(0, j)
    for j in range(4):
        plane(0, j)
    own(3)
    for j in (1, 2, 3):
        column(1, j)
    for j in range(4):
        diag(0, j)

    def other(k):
        def body(i, carry):
            got(k, (1 - c) * 16 + i)
            return carry

        lax.fori_loop(0, 16, body, 0)

    other(0)
    unpack("qkv", G, Wq)
    spread_small(G, taps, gains)
    outs = [
        pltpu.make_async_copy(a, b, local.at[2 + i])
        for i, (a, b) in enumerate(
            [(Wq, o_wq), (taps, o_taps), (gains, o_gains), (h1, o_h1), (q, o_q), (kv, o_kv), (pe, o_pe),
             (att, o_att), (bias, o_bias), (Wo, o_wo), (Wu, o_wu), (Wd, o_wd)]
        )
    ]
    for i in (0, 1, 2, 8):
        outs[i].start()
    for copy in load:
        copy.wait()
    for r in range(2):
        arrived(halo_tok, r)

    for r in range(2):
        def norm_rows(i, carry):
            rows = pl.ds(pl.multiple_of(i * 128, 128), 128)
            n, _ = norm_parts(xe[r, rows].astype(F32))
            h1[r, rows] = (n * gains[5:6] + gains[6:7]).astype(BF)
            return carry

        lax.fori_loop(0, 5, norm_rows, 0)
    outs[3].start()

    for r in range(2):
        def queries(j, carry):
            lanes = pl.ds(pl.multiple_of(j * 256, 256), 256)
            v = dg(h1[r, 64:576], Wq[:, lanes], NN)
            q[r, :, lanes] = v.astype(BF) * jnp.asarray(HEAD**-0.5, BF)
            return carry

        lax.fori_loop(0, 3, queries, 0)
        anchor = win4[r, 64:192, 0:1]
        same = [
            (win4[r, a : a + 128, f : f + 1] == anchor).astype(F32)
            for a, f in ((63, 2), (63, 3), (64, 0), (64, 1), (64, 2))
        ]

        def keys(j, carry):
            event(r * 6 + j)
            lanes = pl.ds(pl.multiple_of(j * 128, 128), 128)
            from_lanes = pl.ds(pl.multiple_of(768 + j * 256, 256), 256)
            to_lanes = pl.ds(pl.multiple_of(j * 256, 256), 256)
            v = dg(h1[r], Wq[:, from_lanes], NN).astype(BF)
            kv[r, :, to_lanes] = v
            chunk[0] = v[:, :128].astype(F32)
            chunk[1] = v[:, 128:].astype(F32)
            for half in range(2):
                hl = pl.ds(pl.multiple_of(j * 256 + half * 128, 128), 128)
                acc = jnp.zeros((128, 128), F32)
                for t in range(5):
                    acc = acc + taps[t : t + 1, hl] * chunk[half, pl.ds(62 + t, 128, stride=4), :] * same[t]
                pe[r, 64:192, hl] = acc.astype(BF)
            return carry

        lax.fori_loop(0, 6, keys, 0)
        both(halo_pool, r, lambda copy, right: copy.start())
    outs[4].start()
    outs[5].start()
    for r in range(2):
        arrived(halo_pool, r)

        def heads_event(h, carry):
            attend(q, kv, pe, bias, att, r, h)
            base = 12 + (r * 6 + h) * 2

            @pl.when(base < 33)
            def _():
                event(base)

            @pl.when(base + 1 < 33)
            def _():
                event(base + 1)

            return carry

        lax.fori_loop(0, 6, heads_event, 0)
    outs[6].start()
    outs[7].start()
    for k in (1, 2, 3):
        other(k)
    for i, (name, dst) in enumerate((("out", Wo), ("up", Wu), ("down", Wd))):
        unpack(name, G, dst)
        outs[9 + i].start()
    for r in range(2):
        both(halo_tok, r, lambda copy, right: copy.wait_send())
        both(halo_pool, r, lambda copy, right: copy.wait_send())
    for k in range(4):
        def done(i, carry):
            to_x(k, i * 4 + col).wait_send()
            to_y(k, i * 4 + col).wait_send()
            to_g(k, i).wait_send()
            for j in range(4):
                to_d(k, i * 4 + j).wait_send()
            return carry

        lax.fori_loop(0, 4, done, 0)
        for j in (1, 2, 3):
            to_z(k, j).wait_send()
    for copy in outs:
        copy.wait()


def front(tok, winc, win4, winr, wq, wo, wu, wd, small):
    sds = jax.ShapeDtypeStruct
    shapes = [
        ((768, 2304), BF), ((768, 768), BF), ((768, 3072), BF), ((768, 3072), BF),
        ((16, 1536), F32), ((16, 768), F32),
        ((2, 640, 768), BF), ((2, 512, 768), BF), ((2, 640, 1536), BF), ((2, 256, 1536), BF),
        ((2, 512, 768), BF), ((8, 416, 128), F32),
    ]
    scratch = [pltpu.VMEM((4, 32, 16, WIDE), BF)]
    scratch += [pltpu.VMEM(sh, dt) for sh, dt in shapes[:6]]
    scratch += [pltpu.VMEM((2, 640, 768), BF)]
    scratch += [pltpu.VMEM(sh, dt) for sh, dt in shapes[6:]]
    scratch += [pltpu.VMEM((2, 640, 128), F32)]
    dma = pltpu.SemaphoreType.DMA
    scratch += [dma((4, 16)), dma((4, 16)), dma((4, 16)), dma((4, 3)), dma((4, 4)), dma((4, 32)), dma((8,)), dma((8,)), dma((14,))]
    return pl.pallas_call(
        front_kernel,
        out_shape=[sds(sh, dt) for sh, dt in shapes],
        in_specs=[ANY] + [VM] * 8,
        out_specs=[ANY] * len(shapes),
        scratch_shapes=scratch,
        compiler_params=pltpu.CompilerParams(collective_id=0, has_side_effects=True, vmem_limit_bytes=VMEM_LIMIT),
    )(tok, winc, win4, winr, wq, wo, wu, wd, small)


def windows(segments):
    block = 512
    padded = jnp.pad(segments, ((0, 0), (REACH, REACH)), constant_values=-1)
    win = lax.dynamic_slice_in_dim(padded, lax.axis_index("seq") * block, block + 2 * REACH, 1)
    return win[:, :, None], win.reshape(2, 256, 4), win


def small_share(pool_taps, ln1_gain, ln1_bias, ln2_gain, ln2_bias):
    rows = jnp.stack([ln1_gain, ln1_bias, ln2_gain, ln2_bias])
    return jnp.concatenate(
        [jnp.pad(pool_taps, ((0, 0), (0, 80))), jnp.pad(rows, ((0, 7), (0, 104)))], axis=0
    )


def gelu_both(u):
    a, b = 0.7978845608028654, 0.044715
    sq = u * u
    t = jnp.tanh(a * u * (1.0 + b * sq))
    half = 0.5 + 0.5 * t
    grad = half + 0.5 * u * (1.0 - t * t) * (a + (3.0 * a * b) * sq)
    return u * half, grad


def pack_pair(lo, hi):
    return jnp.concatenate([lo, hi], axis=0).astype(BF)


def middle_kernel(
    tok, att, dy, wo, wu, wd, gains,
    o_out, o_gmid, o_gatt, o_ffn, o_sout, o_sums,
    Tok, Att, Dy, Wo, Wu, Wd, mid, h2, DyT, H2T, y, gh2, act, gu, dw, gb, S, Sout, outv, sems,
):
    def copy(i, a, b):
        return pltpu.make_async_copy(a, b, sems.at[i])

    loads = [
        copy(i, a, b)
        for i, (a, b) in enumerate([(tok, Tok), (att, Att), (wo, Wo), (dy, Dy), (wu, Wu), (wd, Wd)])
    ]
    for ld in loads:
        ld.start()
    for ld in loads[:3]:
        ld.wait()

    def first(i, carry):
        rows = pl.ds(pl.multiple_of(i * 128, 128), 128)
        v = Tok[rows].astype(F32) + dg(Att[rows], Wo[...], NN)
        mid[rows] = v
        n, _ = norm_parts(v)
        h2[rows] = (n * gains[7:8] + gains[8:9]).astype(BF)
        return carry

    lax.fori_loop(0, 8, first, 0)
    loads[3].wait()

    def flip(i, carry):
        rows = pl.ds(pl.multiple_of(i * 128, 128), 128)
        for j in range(3):
            DyT[j * 256 : j * 256 + 256, rows] = Dy[rows, j * 256 : j * 256 + 256].T
            H2T[j * 256 : j * 256 + 256, rows] = h2[rows, j * 256 : j * 256 + 256].T
        return carry

    lax.fori_loop(0, 8, flip, 0)
    loads[4].wait()
    loads[5].wait()

    def chunk(j, carry):
        lanes = [pl.ds(pl.multiple_of(j * 256 + h * 1536, 256), 256) for h in range(2)]

        def elementwise(m, c):
            rows = pl.ds(pl.multiple_of(m * 256, 256), 256)
            for h in range(2):
                u = dg(h2[rows], Wu[:, lanes[h]], NN)
                ga = dg(Dy[rows], Wd[:, lanes[h]], NN)
                a, da = gelu_both(u)
                act[rows, h * 256 : h * 256 + 256] = a.astype(BF)
                gu[rows, h * 256 : h * 256 + 256] = (ga * da).astype(BF)
            return c

        lax.fori_loop(0, 4, elementwise, 0)

        def sums(m, c):
            rows = pl.ds(pl.multiple_of(m * 256, 256), 256)
            yy = dg(act[rows, 0:256], Wd[:, lanes[0]], NT) + dg(act[rows, 256:512], Wd[:, lanes[1]], NT)
            gg = dg(gu[rows, 0:256], Wu[:, lanes[0]], NT) + dg(gu[rows, 256:512], Wu[:, lanes[1]], NT)

            @pl.when(j == 0)
            def _():
                y[rows] = yy
                gh2[rows] = gg

            @pl.when(j > 0)
            def _():
                y[rows] += yy
                gh2[rows] += gg

            return c

        lax.fori_loop(0, 4, sums, 0)
        for which, (left, right) in enumerate(((H2T, gu), (DyT, act))):
            def grads(m, c):
                rows = pl.ds(pl.multiple_of(m * 256, 256), 256)
                dw[rows, 0:512] = dg(left[rows], right[...], NN)
                return c

            lax.fori_loop(0, 3, grads, 0)
            base = lax.rem(j, 2) * 1536 + which * 768

            def share(s, c):
                r0 = pl.multiple_of(s * 24, 8)
                at = lambda q: pl.ds(pl.multiple_of(base + q * 256, 256), 256)
                S[j // 2, s, :, at(0)] = dw[pl.ds(r0, 16), 0:256].astype(BF)
                S[j // 2, s, :, at(1)] = dw[pl.ds(r0, 16), 256:512].astype(BF)
                tail = pl.ds(pl.multiple_of(r0 + 16, 8), 8)
                S[j // 2, s, :, at(2)] = pack_pair(dw[tail, 0:256], dw[tail, 256:512])
                return c

            lax.fori_loop(0, 32, share, 0)
        return carry

    lax.fori_loop(0, 6, chunk, 0)
    store = [copy(6, S, o_ffn)]
    store[0].start()

    def last(i, carry):
        rows = pl.ds(pl.multiple_of(i * 128, 128), 128)
        v = mid[rows]
        outv[rows] = (v + y[rows]).astype(BF)
        n, rs = norm_parts(v)
        g = gh2[rows]
        e = g * gains[7:8]
        gm = Dy[rows].astype(F32) + rs * (
            e - jnp.mean(e, axis=-1, keepdims=True) - n * jnp.mean(e * n, axis=-1, keepdims=True)
        )
        y[rows] = gm
        gb[rows] = gm.astype(BF)
        a, b = carry
        return a + jnp.sum((g * n).reshape(16, 8, 768), axis=0), b + jnp.sum(g.reshape(16, 8, 768), axis=0)

    zero = jnp.zeros((8, 768), F32)
    a, b = lax.fori_loop(0, 8, last, (zero, zero))
    o_sums[0:1] = jnp.sum(a, axis=0, keepdims=True)
    o_sums[1:2] = jnp.sum(b, axis=0, keepdims=True)
    o_sums[2:8] = jnp.zeros((6, 768), F32)
    store += [copy(7, outv, o_out), copy(8, y, o_gmid)]
    for st in store[1:]:
        st.start()

    def flip_att(i, carry):
        rows = pl.ds(pl.multiple_of(i * 128, 128), 128)
        for j in range(3):
            DyT[j * 256 : j * 256 + 256, rows] = Att[rows, j * 256 : j * 256 + 256].T
        return carry

    lax.fori_loop(0, 8, flip_att, 0)

    def back(m, c):
        rows = pl.ds(pl.multiple_of(m * 256, 256), 256)
        h2[rows] = dg(gb[rows], Wo[...], NT).astype(BF)
        return c

    lax.fori_loop(0, 4, back, 0)
    store.append(copy(9, h2, o_gatt))
    store[-1].start()

    def grads_out(m, c):
        rows = pl.ds(pl.multiple_of(m * 256, 256), 256)
        dw[rows] = dg(DyT[rows], gb[...], NN)
        return c

    lax.fori_loop(0, 3, grads_out, 0)

    def share_out(s, c):
        r0 = pl.multiple_of(s * 24, 8)
        Sout[s, :, 0:768] = dw[pl.ds(r0, 16)].astype(BF)
        tail = pl.ds(pl.multiple_of(r0 + 16, 8), 8)
        Sout[s, :, 768:1152] = pack_pair(dw[tail, 0:384], dw[tail, 384:768])
        return c

    lax.fori_loop(0, 32, share_out, 0)
    store.append(copy(10, Sout, o_sout))
    store[-1].start()
    for st in store:
        st.wait()


def middle_part(tok, att, dy, wo, wu, wd, gains):
    sds = jax.ShapeDtypeStruct
    n = 1024
    vm = pltpu.VMEM
    big = lambda dt: vm((n, 768), dt)
    return pl.pallas_call(
        middle_kernel,
        out_shape=[
            sds((n, 768), BF), sds((n, 768), F32), sds((n, 768), BF), sds((3, 32, 16, 3072), BF),
            sds((32, 16, 1152), BF), sds((8, 768), F32),
        ],
        in_specs=[ANY] * 6 + [VM],
        out_specs=[ANY] * 5 + [VM],
        scratch_shapes=[
            big(BF), big(BF), big(BF), vm((768, 768), BF), vm((768, 3072), BF), vm((768, 3072), BF),
            big(F32), big(BF), vm((768, n), BF), vm((768, n), BF), big(F32), big(F32),
            vm((n, 512), BF), vm((n, 512), BF), vm((768, 768), F32), big(BF),
            vm((3, 32, 16, 3072), BF), vm((32, 16, 1152), BF), big(BF),
            pltpu.SemaphoreType.DMA((11,)),
        ],
        compiler_params=pltpu.CompilerParams(vmem_limit_bytes=VMEM_LIMIT),
    )(tok, att, dy, wo, wu, wd, gains)


def pick_small(tg, lg, put):
    lane = lax.broadcasted_iota(jnp.int32, (16, 128), 1)

    def part(src, width, s):
        at, off = divmod(width * s, 128)
        v = src[:, at * 128 : at * 128 + 128]
        v = pltpu.roll(v, 128 - off, 1) if off else v
        if off + width > 128:
            w = pltpu.roll(src[:, at * 128 + 128 : at * 128 + 256], 128 - off, 1)
            v = jnp.where(lane < 128 - off, v, w)
        return jnp.where(lane < width, v, 0.0)

    for s in range(32):
        put(s, (part(tg, 48, s) + part(lg, 24, s)).astype(BF))


def back_kernel(
    sffn, sout, q_in, kv_in, pe_in, bias_in, gatt_in, gmid_in, h1_in, tok_in, wq_in,
    taps, gains, win4, sums2,
    o_in, o_wq, o_wo, o_wu, o_wd, o_small,
    Sf, So, Sq, Ss, Rf, Ro, Rq, Rs, gext, pstage, precv, hstage, hrecv, tg, lg,
    send, recv, psend, prsem, local,
):
    me = where_am_i()
    c, s, z, col = me["c"], me["s"], me["z"], me["col"]
    has_left, has_right = s > 0, s < lax.axis_size("seq") - 1

    def copy(i, a, b):
        return pltpu.make_async_copy(a, b, local.at[i])

    def cls(k):
        if k < 3:
            return Sf.at[k], Rf.at[k]
        if k == 3:
            return So, Ro
        if k == 4:
            return Sq.at[pl.ds(c * 16, 16)], Rq
        return Ss.at[pl.ds(c * 16, 16)], Rs

    def other(k):
        start = (1 - c) * 16
        if k < 3:
            return sffn.at[k, pl.ds(start, 16)]
        if k == 3:
            return sout.at[pl.ds(start, 16)]
        return (Sq if k == 4 else Ss).at[pl.ds(start, 16)]

    def remote(k, src, slot, i, to):
        return pltpu.make_async_remote_copy(
            src_ref=src, dst_ref=slot, send_sem=send.at[k, i], recv_sem=recv.at[k, i],
            device_id=to, device_id_type=MESH,
        )

    def swap(k):
        return remote(k, other(k), cls(k)[1].at[pl.ds(0, 16)], 0, me["pd"])

    def step_g(k, zz):
        S, R = cls(k)
        to = me["px"] if zz % 2 == 0 else me["py"]
        return remote(k, S.at[zz * 4 + me["cold"]], R.at[16 + zz], 1 + zz, to)

    def step_x(k, zz):
        S, R = cls(k)
        return remote(k, S.at[zz * 4 + me["colx"]], R.at[20 + zz], 5 + zz, me["px"])

    def step_y(k, zz):
        S, R = cls(k)
        return remote(k, S.at[zz * 4 + me["coly"]], R.at[24 + zz], 9 + zz, me["py"])

    def step_z(k, j):
        S, R = cls(k)
        zz = lax.rem(z + j, 4)
        return remote(k, S.at[zz * 4 + col], R.at[27 + j], 12 + j, (c, zz * 4 + col))

    def add(k, at, slots):
        S, R = cls(k)
        v = S[at].astype(F32) + R[at].astype(F32)
        for slot in slots:
            v = v + R[slot].astype(F32)
        return v

    def begin(k):
        swap(k).start()

    def do_g(k, zz):
        if zz == 0:
            swap(k).wait_recv()
        at = zz * 4 + me["cold"]
        cls(k)[0][at] = add(k, at, []).astype(BF)
        step_g(k, zz).start()

    def do_p(k, zz):
        step_g(k, zz).wait_recv()
        even = zz % 2 == 0
        for at, step, has in ((zz * 4 + me["colx"], step_x, not even), (zz * 4 + me["coly"], step_y, even)):
            cls(k)[0][at] = add(k, at, [16 + zz] if has else []).astype(BF)
            step(k, zz).start()

    def arrive(k, zz):
        S, R = cls(k)
        remote(k, S.at[0], R.at[20 + zz], 5 + zz, me["px"]).wait_recv()
        remote(k, S.at[0], R.at[24 + zz], 9 + zz, me["py"]).wait_recv()

    def do_c(k, j):
        zz = lax.rem(z + j, 4)
        arrive(k, zz)
        at = zz * 4 + col
        cls(k)[0][at] = add(k, at, [20 + zz, 24 + zz]).astype(BF)
        step_z(k, j).start()

    def total(k):
        arrive(k, z)
        for j in (1, 2, 3):
            step_z(k, j).wait_recv()
        return add(k, z * 4 + col, [20 + z, 24 + z, 28, 29, 30])

    def drain(k):
        swap(k).wait_send()
        for zz in range(4):
            step_g(k, zz).wait_send()
            step_x(k, zz).wait_send()
            step_y(k, zz).wait_send()
        for j in (1, 2, 3):
            step_z(k, j).wait_send()

    def finish(k):
        v = total(k)
        if k < 3:
            for i in range(2):
                for ref, base in ((o_wu, i * 1536), (o_wd, i * 1536 + 768)):
                    lo, hi = (2 * k + i) * 256, 1536 + (2 * k + i) * 256
                    ref[0:16, lo : lo + 256] = v[:, base : base + 256]
                    ref[0:16, hi : hi + 256] = v[:, base + 256 : base + 512]
                    ref[16:24, lo : lo + 256] = v[0:8, base + 512 : base + 768]
                    ref[16:24, hi : hi + 256] = v[8:16, base + 512 : base + 768]
        elif k < 5:
            ref = o_wo if k == 3 else o_wq
            n = 768 if k == 3 else 2304
            ref[0:16] = v[:, :n]
            ref[16:24, : n // 2] = v[0:8, n:]
            ref[16:24, n // 2 :] = v[8:16, n:]
        else:
            o_small[...] = v
        drain(k)

    def halo(src, dst, r, right, base):
        i = base + r * 2 + int(right)
        return pltpu.make_async_remote_copy(
            src_ref=src.at[r, int(right)], dst_ref=dst.at[r, int(right)],
            send_sem=psend.at[i], recv_sem=prsem.at[i],
            device_id=(c, s + 1 if right else s - 1), device_id_type=MESH,
        )

    def both(src, dst, r, base, act):
        @pl.when(has_right)
        def _():
            act(halo(src, dst, r, True, base))

        @pl.when(has_left)
        def _():
            act(halo(src, dst, r, False, base))

    def arrived(src, dst, r, base):
        @pl.when(has_left)
        def _():
            halo(src, dst, r, True, base).wait_recv()

        @pl.when(has_right)
        def _():
            halo(src, dst, r, False, base).wait_recv()

    mine = [copy(k, sffn.at[k, pl.ds(c * 16, 16)], Sf.at[k]) for k in range(3)]
    mine.append(copy(3, sout.at[pl.ds(c * 16, 16)], So))

    def attention(q, kv, pe, bias, gatt, dkv, dpe, chunk):
        loads = [
            copy(4 + i, a, b)
            for i, (a, b) in enumerate(
                [(q_in, q), (kv_in, kv), (pe_in, pe), (bias_in, bias), (gatt_in, gatt)]
            )
        ]
        for ld in loads + mine:
            ld.start()
        for r in range(2):
            gext[r, 0:64, 0:768] = jnp.zeros((64, 768), BF)
            gext[r, 576:640, 0:768] = jnp.zeros((64, 768), BF)

        @pl.when(jnp.logical_not(has_left))
        def _():
            precv[:, 1] = jnp.zeros((2, 64, 1536), BF)
            hrecv[:, 1] = jnp.zeros((2, 64, 768), BF)

        @pl.when(jnp.logical_not(has_right))
        def _():
            precv[:, 0] = jnp.zeros((2, 64, 1536), BF)
            hrecv[:, 0] = jnp.zeros((2, 64, 768), BF)

        tg[...] = jnp.zeros((16, 1536), F32)
        lg[...] = jnp.zeros((16, 768), F32)
        greet(me, True)
        for k in range(4):
            begin(k)
        for ld in loads + mine:
            ld.wait()
        blocks = [
            (do_g, 0), (do_g, 1), (do_p, 0), (do_g, 2), (do_p, 1), (do_c, 0),
            (do_g, 3), (do_p, 2), (do_c, 1), (do_p, 3), (do_c, 2), (do_c, 3),
        ]
        for r in range(2):
            def heads(h, carry):
                attend_back(q, kv, pe, bias, gatt, gext, dkv, dpe, r, h)
                for i, (fn, k) in enumerate(blocks):
                    @pl.when(r * 6 + h == i)
                    def _():
                        for j in (1, 2, 3) if fn is do_c else (0, 1, 2, 3):
                            fn(k, j)

                return carry

            lax.fori_loop(0, 6, heads, 0)
            for t in range(12):
                lanes = slice(t * 128, t * 128 + 128)
                pstage[r, 0, :, lanes] = dpe[r, t, 0:64].astype(BF)
                pstage[r, 1, :, lanes] = dpe[r, t, 192:256].astype(BF)
            both(pstage, precv, r, 0, lambda cp: cp.start())

        for r in range(2):
            anchor = win4[r, 64:192, 0:1]
            same = [
                (win4[r, a : a + 128, f : f + 1] == anchor).astype(F32)
                for a, f in ((63, 2), (63, 3), (64, 0), (64, 1), (64, 2))
            ]
            arrived(pstage, precv, r, 0)

            def pool_back(t, carry):
                lanes = pl.ds(pl.multiple_of(t * 128, 128), 128)
                low = dpe[r, t, 64:128] + precv[r, 1, :, lanes].astype(F32)
                high = dpe[r, t, 128:192] + precv[r, 0, :, lanes].astype(F32)
                gp = jnp.concatenate([low, high], axis=0)
                chunk[...] = kv[r, :, lanes].astype(F32)
                for i in range(5):
                    at = pl.ds(62 + i, 128, stride=4)
                    gm = gp * same[i]
                    tg[i : i + 1, lanes] += jnp.sum(gm * chunk[at, :], axis=0, keepdims=True)
                    dkv[r, t, at, :] += gm * taps[i : i + 1, lanes]
                out_lanes = pl.ds(pl.multiple_of(768 + t * 128, 128), 128)
                gext[r, :, out_lanes] = dkv[r, t].astype(BF)
                return carry

            lax.fori_loop(0, 12, pool_back, 0)

    vm = pltpu.VMEM
    pl.run_scoped(
        attention,
        vm((2, 512, 768), BF), vm((2, 640, 1536), BF), vm((2, 256, 1536), BF), vm((8, 416, 128), F32),
        vm((2, 512, 768), BF), vm((2, 12, 640, 128), F32), vm((2, 12, 256, 128), F32), vm((640, 128), F32),
    )

    def projection(h1, h1t, wq, tok, gmid, gh, dw):
        loads = [
            copy(9 + i, a, b)
            for i, (a, b) in enumerate([(h1_in, h1), (wq_in, wq), (tok_in, tok), (gmid_in, gmid)])
        ]
        for ld in loads:
            ld.start()
        loads[0].wait()
        for r in range(2):
            def flip(i, carry):
                rows = pl.ds(pl.multiple_of(i * 128, 128), 128)
                for j in range(3):
                    h1t[r, j * 256 : j * 256 + 256, rows] = h1[r, rows, j * 256 : j * 256 + 256].T
                return carry

            lax.fori_loop(0, 5, flip, 0)

        def grads(j, carry):
            lanes = pl.ds(pl.multiple_of(j * 256, 256), 256)
            dw[:, lanes] = dg(h1t[0], gext[0, :, lanes], NN) + dg(h1t[1], gext[1, :, lanes], NN)
            return carry

        lax.fori_loop(0, 9, grads, 0)

        def share(i, carry):
            r0 = pl.multiple_of(i * 24, 8)
            Sq[i, :, 0:2304] = dw[pl.ds(r0, 16)].astype(BF)
            tail = pl.ds(pl.multiple_of(r0 + 16, 8), 8)
            Sq[i, :, 2304:3456] = pack_pair(dw[tail, 0:1152], dw[tail, 1152:2304])
            return carry

        lax.fori_loop(0, 32, share, 0)
        begin(4)
        for k in range(4):
            finish(k)
        for ld in loads[1:]:
            ld.wait()
        for r in range(2):
            def rows_back(i, carry):
                rows = pl.ds(pl.multiple_of(i * 128, 128), 128)
                gh[r, rows] = dg(gext[r, rows], wq[...], NT)
                return carry

            lax.fori_loop(0, 5, rows_back, 0)
            hstage[r, 0] = gh[r, 0:64].astype(BF)
            hstage[r, 1] = gh[r, 576:640].astype(BF)
            both(hstage, hrecv, r, 4, lambda cp: cp.start())
            for zz in range(4):
                (do_g if r == 0 else do_p)(4, zz)
        for r in range(2):
            arrived(hstage, hrecv, r, 4)
            gh[r, 64:128] += hrecv[r, 1].astype(F32)
            gh[r, 512:576] += hrecv[r, 0].astype(F32)
        zero = jnp.zeros((8, 768), F32)
        acc = (zero, zero)
        for r in range(2):
            def rows_norm(i, carry):
                rows = pl.ds(pl.multiple_of(i * 128, 128), 128)
                n, rs = norm_parts(tok[r, rows].astype(F32))
                g = gh[r, pl.ds(pl.multiple_of(i * 128 + 64, 64), 128)]
                e = g * gains[5:6]
                gmid[r, rows] += rs * (
                    e - jnp.mean(e, axis=-1, keepdims=True) - n * jnp.mean(e * n, axis=-1, keepdims=True)
                )
                a, b = carry
                return a + jnp.sum((g * n).reshape(16, 8, 768), axis=0), b + jnp.sum(g.reshape(16, 8, 768), axis=0)

            acc = lax.fori_loop(0, 4, rows_norm, acc)
        out = copy(13, gmid, o_in)
        out.start()
        lg[5:6] = jnp.sum(acc[0], axis=0, keepdims=True)
        lg[6:7] = jnp.sum(acc[1], axis=0, keepdims=True)
        lg[7:9] = sums2[0:2]

        def put(i, v):
            Ss[i] = v

        pick_small(tg, lg, put)
        begin(5)
        for j in (1, 2, 3):
            do_c(4, j)
        for zz in range(4):
            do_g(5, zz)
        for zz in range(4):
            do_p(5, zz)
        for j in (1, 2, 3):
            do_c(5, j)
        finish(4)
        finish(5)
        out.wait()

    pl.run_scoped(
        projection,
        vm((2, 640, 768), BF), vm((2, 768, 640), BF), vm((768, 2304), BF), vm((2, 512, 768), BF),
        vm((2, 512, 768), F32), vm((2, 640, 768), F32), vm((768, 2304), F32),
    )
    for r in range(2):
        both(pstage, precv, r, 0, lambda cp: cp.wait_send())
        both(hstage, hrecv, r, 4, lambda cp: cp.wait_send())


def back_part(sffn, sout, q, kv, pe, bias, gatt, gmid, h1, tok, wq, taps, gains, win4, sums2):
    sds = jax.ShapeDtypeStruct
    vm, dma = pltpu.VMEM, pltpu.SemaphoreType.DMA
    return pl.pallas_call(
        back_kernel,
        out_shape=[
            sds((2, 512, 768), F32), sds((24, 2304), F32), sds((24, 768), F32), sds((24, 3072), F32),
            sds((24, 3072), F32), sds((16, 128), F32),
        ],
        in_specs=[ANY] * 11 + [VM] * 4,
        out_specs=[ANY] + [VM] * 5,
        scratch_shapes=[
            vm((3, 16, 16, 3072), BF), vm((16, 16, 1152), BF), vm((32, 16, 3456), BF), vm((32, 16, 128), BF),
            vm((3, 31, 16, 3072), BF), vm((31, 16, 1152), BF), vm((31, 16, 3456), BF), vm((31, 16, 128), BF),
            vm((2, 640, 2304), BF),
            vm((2, 2, 64, 1536), BF), vm((2, 2, 64, 1536), BF), vm((2, 2, 64, 768), BF), vm((2, 2, 64, 768), BF),
            vm((16, 1536), F32), vm((16, 768), F32),
            dma((6, 16)), dma((6, 16)), dma((8,)), dma((8,)), dma((14,)),
        ],
        compiler_params=pltpu.CompilerParams(collective_id=1, has_side_effects=True, vmem_limit_bytes=VMEM_LIMIT),
    )(sffn, sout, q, kv, pe, bias, gatt, gmid, h1, tok, wq, taps, gains, win4, sums2)


def with_halo(x, sides, width):
    for axis, dim in sides:
        size, length = (lax.axis_size(axis), x.shape[dim])
        up = [(i, (i + 1) % size) for i in range(size - 1)]
        down = [(j, i) for i, j in up]
        last = lax.slice_in_dim(x, length - width, length, axis=dim)
        first = lax.slice_in_dim(x, 0, width, axis=dim)
        before = lax.ppermute(last, axis, up)
        after = lax.ppermute(first, axis, down)
        x = jnp.concatenate([before, x, after], axis=dim)
    return x


def layer_norm(inputs, norm_gain, norm_bias):
    middle = jnp.mean(inputs, axis=-1, keepdims=True)
    centred = inputs - middle
    spread = jnp.mean(centred * centred, axis=-1, keepdims=True)
    return centred * lax.rsqrt(spread + 1e-05) * norm_gain + norm_bias


def pool_local(extended, taps_in, seg_window):
    block_rows = extended.shape[0] - 2 * NEAR
    anchors = seg_window[REACH : REACH + block_rows : 4]
    pooled = jnp.zeros((block_rows // 4, extended.shape[1]), jnp.float32)
    for offset in range(5):
        start_row = NEAR - 2 + offset
        picked = extended[start_row : start_row + block_rows : 4]
        seg_start = REACH - 2 + offset
        same_doc = (seg_window[seg_start : seg_start + block_rows : 4] == anchors).astype(
            jnp.float32
        )
        pooled = pooled + taps_in[offset] * picked * same_doc[:, None]
    return pooled


def window_masks(seg_window, block_rows):
    seg_query = seg_window[REACH : REACH + block_rows]
    seg_key = seg_window[REACH - NEAR : REACH + block_rows + NEAR]
    seg_pool = seg_window[0 : block_rows + 2 * REACH : 4]
    q_index = jnp.arange(block_rows, dtype=jnp.int32)
    k_index = jnp.arange(seg_key.shape[0], dtype=jnp.int32)
    p_index = jnp.arange(seg_pool.shape[0], dtype=jnp.int32)
    near_mask = (jnp.abs(q_index[:, None] - k_index[None, :] + NEAR) <= NEAR) & (
        seg_query[:, None] == seg_key[None, :]
    )
    far_mask = (jnp.abs(4 * p_index[None, :] - REACH - q_index[:, None]) <= REACH) & (
        seg_query[:, None] == seg_pool[None, :]
    )
    return (near_mask, far_mask)


def scores_of(queries, near_keys, far_keys, near_mask, far_mask):
    score_scale = HEAD ** (-0.5)
    near_scores = (
        jnp.einsum("qhd,khd->hqk", queries, near_keys, preferred_element_type=jnp.float32)
        * score_scale
    )
    far_scores = (
        jnp.einsum("qhd,khd->hqk", queries, far_keys, preferred_element_type=jnp.float32)
        * score_scale
    )
    return (
        jnp.where(near_mask[None], near_scores, -1e30),
        jnp.where(far_mask[None], far_scores, -1e30),
    )


def normalise(near_scores, far_scores, near_mask, far_mask, row_max, row_total):
    near_prob = jnp.where(near_mask[None], jnp.exp(near_scores - row_max), 0.0) / row_total
    far_prob = jnp.where(far_mask[None], jnp.exp(far_scores - row_max), 0.0) / row_total
    return (near_prob, far_prob)


def add_rims(middle_part, rim_values, rim_width):
    extra = middle_part.shape[0] - rim_width
    return (
        middle_part
        + jnp.pad(rim_values[:rim_width], ((0, extra), (0, 0)))
        + jnp.pad(rim_values[-rim_width:], ((extra, 0), (0, 0)))
    )


def shards(
    tokens,
    segments,
    cotangent,
    ln1_gain,
    ln1_bias,
    w_qkv,
    pool_taps,
    w_out,
    ln2_gain,
    ln2_bias,
    w_up,
    w_down,
):
    block_rows = tokens.shape[1]
    model_width = tokens.shape[2]
    pool_half = REACH // 4
    score_scale = HEAD ** (-0.5)
    offset_tokens = lax.axis_index("seq") * block_rows
    outputs = []
    input_grads = []
    summed = None
    for micro_step in range(tokens.shape[0]):
        gathered = (
            lax.all_gather(ln1_gain, ("dp", "seq"), axis=0, tiled=True),
            lax.all_gather(ln1_bias, ("dp", "seq"), axis=0, tiled=True),
            lax.all_gather(w_qkv, ("dp", "seq"), axis=0, tiled=True),
            lax.all_gather(pool_taps, ("dp", "seq"), axis=1, tiled=True),
            lax.all_gather(w_out, ("dp", "seq"), axis=0, tiled=True),
            lax.all_gather(ln2_gain, ("dp", "seq"), axis=0, tiled=True),
            lax.all_gather(ln2_bias, ("dp", "seq"), axis=0, tiled=True),
            lax.all_gather(w_up, ("dp", "seq"), axis=0, tiled=True),
            lax.all_gather(w_down, ("dp", "seq"), axis=1, tiled=True),
        )
        gain_one, bias_one, proj_qkv, taps, proj_out, gain_two, bias_two, proj_up, proj_down = (
            gathered
        )
        seg_row = segments[micro_step]
        seg_padded = jnp.pad(seg_row, (REACH, REACH), constant_values=-1)
        seg_window = lax.dynamic_slice_in_dim(
            seg_padded, offset_tokens, block_rows + 2 * REACH, 0
        )
        near_mask, far_mask = window_masks(seg_window, block_rows)
        inputs = tokens[micro_step].astype(jnp.float32)
        gain_float = gain_one.astype(jnp.float32)
        bias_float = bias_one.astype(jnp.float32)
        gain_second = gain_two.astype(jnp.float32)
        bias_second = bias_two.astype(jnp.float32)
        normed = layer_norm(inputs, gain_float, bias_float).astype(jnp.bfloat16)
        projected = jnp.dot(normed, proj_qkv, preferred_element_type=jnp.float32).astype(
            jnp.bfloat16
        )
        queries = projected[:, :model_width].reshape(block_rows, HEADS, HEAD)
        key_value = projected[:, model_width:]
        extended = with_halo(key_value, (("seq", 0),), NEAR)
        ext_float = extended.astype(jnp.float32)
        taps_float = taps.astype(jnp.float32)
        pooled = pool_local(ext_float, taps_float, seg_window).astype(jnp.bfloat16)
        pool_ext = with_halo(pooled, (("seq", 0),), pool_half)
        near_keys = extended[:, :model_width].reshape(-1, HEADS, HEAD)
        near_values = extended[:, model_width:].reshape(-1, HEADS, HEAD)
        far_keys = pool_ext[:, :model_width].reshape(-1, HEADS, HEAD)
        far_values = pool_ext[:, model_width:].reshape(-1, HEADS, HEAD)
        near_scores, far_scores = scores_of(queries, near_keys, far_keys, near_mask, far_mask)
        row_max = jnp.maximum(
            jnp.max(near_scores, axis=2, keepdims=True), jnp.max(far_scores, axis=2, keepdims=True)
        )
        near_exp = jnp.where(near_mask[None], jnp.exp(near_scores - row_max), 0.0)
        far_exp = jnp.where(far_mask[None], jnp.exp(far_scores - row_max), 0.0)
        row_total = jnp.sum(near_exp, axis=2, keepdims=True) + jnp.sum(
            far_exp, axis=2, keepdims=True
        )
        near_low = (near_exp / row_total).astype(jnp.bfloat16)
        far_low = (far_exp / row_total).astype(jnp.bfloat16)
        mixed_sum = jnp.einsum(
            "hqk,khd->qhd", near_low, near_values, preferred_element_type=jnp.float32
        ) + jnp.einsum("hqk,khd->qhd", far_low, far_values, preferred_element_type=jnp.float32)
        attended = mixed_sum.reshape(block_rows, model_width).astype(jnp.bfloat16)
        branch = jnp.dot(attended, proj_out, preferred_element_type=jnp.float32)
        middle = inputs + branch
        normed_two = layer_norm(middle, gain_second, bias_second).astype(jnp.bfloat16)
        upward = jnp.dot(normed_two, proj_up, preferred_element_type=jnp.float32)
        activated = jax.nn.gelu(upward).astype(jnp.bfloat16)
        result = middle + jnp.dot(activated, proj_down, preferred_element_type=jnp.float32)
        outputs.append(result.astype(jnp.bfloat16))
        regathered = (
            lax.all_gather(ln1_gain, ("dp", "seq"), axis=0, tiled=True),
            lax.all_gather(ln1_bias, ("dp", "seq"), axis=0, tiled=True),
            lax.all_gather(w_qkv, ("dp", "seq"), axis=0, tiled=True),
            lax.all_gather(pool_taps, ("dp", "seq"), axis=1, tiled=True),
            lax.all_gather(w_out, ("dp", "seq"), axis=0, tiled=True),
            lax.all_gather(ln2_gain, ("dp", "seq"), axis=0, tiled=True),
            lax.all_gather(ln2_bias, ("dp", "seq"), axis=0, tiled=True),
            lax.all_gather(w_up, ("dp", "seq"), axis=0, tiled=True),
            lax.all_gather(w_down, ("dp", "seq"), axis=1, tiled=True),
        )
        back_qkv = regathered[2]
        back_out = regathered[4]
        back_up = regathered[7]
        back_down = regathered[8]
        grad_out = cotangent[micro_step]
        grad_act = jnp.dot(grad_out, back_down.T, preferred_element_type=jnp.float32)
        grad_down = jnp.dot(activated.T, grad_out, preferred_element_type=jnp.float32)
        gelu_value, gelu_back = jax.vjp(jax.nn.gelu, upward)
        grad_upin = gelu_back(grad_act)[0].astype(jnp.bfloat16)
        grad_upw = jnp.dot(normed_two.T, grad_upin, preferred_element_type=jnp.float32)
        grad_normed_two = jnp.dot(grad_upin, back_up.T, preferred_element_type=jnp.float32)
        norm_value_two, norm_back_two = jax.vjp(layer_norm, middle, gain_second, bias_second)
        grad_mid_part, grad_gain_two, grad_bias_two = norm_back_two(grad_normed_two)
        grad_middle = grad_out.astype(jnp.float32) + grad_mid_part
        grad_branch = grad_middle.astype(jnp.bfloat16)
        grad_outw = jnp.dot(attended.T, grad_branch, preferred_element_type=jnp.float32)
        grad_mixed = (
            jnp.dot(grad_branch, back_out.T, preferred_element_type=jnp.float32)
            .astype(jnp.bfloat16)
            .reshape(block_rows, HEADS, HEAD)
        )
        near_scores, far_scores = scores_of(queries, near_keys, far_keys, near_mask, far_mask)
        near_prob, far_prob = normalise(
            near_scores, far_scores, near_mask, far_mask, row_max, row_total
        )
        near_low = near_prob.astype(jnp.bfloat16)
        far_low = far_prob.astype(jnp.bfloat16)
        grad_near_values = jnp.einsum(
            "hqk,qhd->khd", near_low, grad_mixed, preferred_element_type=jnp.float32
        )
        grad_far_values = jnp.einsum(
            "hqk,qhd->khd", far_low, grad_mixed, preferred_element_type=jnp.float32
        )
        grad_near_prob = jnp.einsum(
            "qhd,khd->hqk", grad_mixed, near_values, preferred_element_type=jnp.float32
        )
        grad_far_prob = jnp.einsum(
            "qhd,khd->hqk", grad_mixed, far_values, preferred_element_type=jnp.float32
        )
        row_delta = jnp.sum(near_prob * grad_near_prob, axis=2, keepdims=True) + jnp.sum(
            far_prob * grad_far_prob, axis=2, keepdims=True
        )
        grad_near_scores = (near_prob * (grad_near_prob - row_delta)).astype(jnp.bfloat16)
        grad_far_scores = (far_prob * (grad_far_prob - row_delta)).astype(jnp.bfloat16)
        grad_queries = (
            jnp.einsum(
                "hqk,khd->qhd", grad_near_scores, near_keys, preferred_element_type=jnp.float32
            )
            + jnp.einsum(
                "hqk,khd->qhd", grad_far_scores, far_keys, preferred_element_type=jnp.float32
            )
        ) * score_scale
        grad_near_keys = (
            jnp.einsum(
                "hqk,qhd->khd", grad_near_scores, queries, preferred_element_type=jnp.float32
            )
            * score_scale
        )
        grad_far_keys = (
            jnp.einsum("hqk,qhd->khd", grad_far_scores, queries, preferred_element_type=jnp.float32)
            * score_scale
        )
        grad_extended = jnp.concatenate(
            [grad_near_keys.reshape(-1, model_width), grad_near_values.reshape(-1, model_width)],
            axis=1,
        )
        grad_pool_ext = jnp.concatenate(
            [grad_far_keys.reshape(-1, model_width), grad_far_values.reshape(-1, model_width)],
            axis=1,
        )
        pool_edges = jnp.concatenate(
            [grad_pool_ext[:pool_half], grad_pool_ext[-pool_half:]], axis=0
        )
        pool_returned = with_halo(pool_edges.astype(jnp.bfloat16), (("seq", 0),), pool_half).astype(
            pool_edges.dtype
        )
        grad_pooled = add_rims(grad_pool_ext[pool_half:-pool_half], pool_returned, pool_half)
        pool_value, pool_back = jax.vjp(
            lambda ext_in, taps_part: pool_local(ext_in, taps_part, seg_window),
            ext_float,
            taps_float,
        )
        grad_ext_pool, grad_taps = pool_back(grad_pooled)
        grad_extended = grad_extended + grad_ext_pool
        token_edges = jnp.concatenate(
            [grad_extended[:NEAR], grad_extended[-NEAR:]], axis=0
        )
        token_returned = with_halo(
            token_edges.astype(jnp.bfloat16), (("seq", 0),), NEAR
        ).astype(token_edges.dtype)
        grad_kv = add_rims(grad_extended[NEAR:-NEAR], token_returned, NEAR)
        grad_projected = jnp.concatenate(
            [grad_queries.reshape(block_rows, model_width), grad_kv], axis=1
        ).astype(jnp.bfloat16)
        grad_qkvw = jnp.dot(normed.T, grad_projected, preferred_element_type=jnp.float32)
        grad_normed = jnp.dot(grad_projected, back_qkv.T, preferred_element_type=jnp.float32)
        norm_value_one, norm_back_one = jax.vjp(layer_norm, inputs, gain_float, bias_float)
        grad_in_part, grad_gain_one, grad_bias_one = norm_back_one(grad_normed)
        input_grads.append(grad_middle + grad_in_part)
        shares = (
            lax.psum_scatter(grad_gain_one, ("dp", "seq"), scatter_dimension=0, tiled=True),
            lax.psum_scatter(grad_bias_one, ("dp", "seq"), scatter_dimension=0, tiled=True),
            lax.psum_scatter(grad_qkvw, ("dp", "seq"), scatter_dimension=0, tiled=True),
            lax.psum_scatter(grad_taps, ("dp", "seq"), scatter_dimension=1, tiled=True),
            lax.psum_scatter(grad_outw, ("dp", "seq"), scatter_dimension=0, tiled=True),
            lax.psum_scatter(grad_gain_two, ("dp", "seq"), scatter_dimension=0, tiled=True),
            lax.psum_scatter(grad_bias_two, ("dp", "seq"), scatter_dimension=0, tiled=True),
            lax.psum_scatter(grad_upw, ("dp", "seq"), scatter_dimension=0, tiled=True),
            lax.psum_scatter(grad_down, ("dp", "seq"), scatter_dimension=1, tiled=True),
        )
        if summed is None:
            summed = shares
        else:
            summed = jax.tree.map(jnp.add, summed, shares)
    return (
        jnp.stack(outputs),
        jnp.stack(input_grads),
        summed[0],
        summed[1],
        summed[2],
        summed[3],
        summed[4],
        summed[5],
        summed[6],
        summed[7],
        summed[8],
    )


def chained(
    tokens, segments, cotangent, ln1_gain, ln1_bias, w_qkv, pool_taps, w_out, ln2_gain, ln2_bias, w_up, w_down,
):
    winc, win4, winr = windows(segments)
    small = small_share(pool_taps, ln1_gain, ln1_bias, ln2_gain, ln2_bias)
    wq, wo, wu, wd, taps, gains, h1, q, kv, pe, att, bias = front(
        tokens, winc, win4, winr, w_qkv, w_out, w_up, w_down.T, small
    )
    flat = (1024, 768)
    out, gmid, gatt, sffn, sout, sums2 = middle_part(
        tokens.reshape(flat), att.reshape(flat), cotangent.reshape(flat), wo, wu, wd, gains
    )
    split = (2, 512, 768)
    g_in, g_wq, g_wo, g_wu, g_wd, g_small = back_part(
        sffn, sout, q, kv, pe, bias, gatt.reshape(split), gmid.reshape(split), h1, tokens, wq, taps, gains, win4, sums2
    )
    return (
        out.reshape(split), g_in, g_small[5, :24], g_small[6, :24], g_wq, g_small[0:5, :48], g_wo,
        g_small[7, :24], g_small[8, :24], g_wu, g_wd.T,
    )


def solution(mesh):
    both = ("dp", "seq")
    row, tok, first, second = P(both), P("dp", "seq", None), P(both, None), P(None, both)
    small_mesh = mesh.shape["dp"] == 2 and mesh.shape["seq"] == 16
    return jax.shard_map(
        chained if small_mesh else shards,
        mesh=mesh,
        in_specs=(tok, P("dp", None), tok, row, row, first, second, first, row, row, first, second),
        out_specs=(tok, tok, row, row, first, second, first, row, row, first, second),
        check_vma=False,
    )
```

```python
import functools

import jax
import jax.numpy as jnp
from jax import lax
from jax.experimental import pallas as pl
from jax.experimental.pallas import tpu as pltpu
from jax.sharding import PartitionSpec as P

HEADS = 12
HEAD = 64
NEAR = 64
REACH = 256
F32, BF = jnp.float32, jnp.bfloat16
NT = (((1,), (1,)), ((), ()))
TN = (((0,), (0,)), ((), ()))
NN = (((1,), (0,)), ((), ()))
MESH = pl.DeviceIdType.MESH
ANY = pl.BlockSpec(memory_space=pl.ANY)
VM = pl.BlockSpec(memory_space=pltpu.VMEM)
VMEM_LIMIT = 62 * 2**20
UNIT = 384
CLS = 3456
WIDE = 3584
PLACE = {"qkv": (0, 0, 2304), "out": (1, 0, 768), "up": (1, 3, 3072), "down": (1, 15, 3072)}


def dg(a, b, dims):
    return lax.dot_general(a, b, dims, preferred_element_type=F32)


def spot(name, unit):
    first, start, _ = PLACE[name]
    at = start + unit
    return first + at // 9, (at % 9) * UNIT


def units(name):
    return PLACE[name][2] // UNIT


def where_am_i():
    c = lax.axis_index("dp")
    s = lax.axis_index("seq")
    z, col = s // 4, s % 4
    x, y = col % 2, col // 2
    colx, coly, cold = y * 2 + (1 - x), (1 - y) * 2 + x, 3 - col
    return dict(
        c=c, s=s, z=z, col=col, colx=colx, coly=coly, cold=cold,
        px=(c, z * 4 + colx), py=(c, z * 4 + coly), pd=(1 - c, s),
    )


def greet(me, halo):
    bar = pltpu.get_barrier_semaphore()
    who = [me["px"], me["py"], me["pd"]]
    who += [(me["c"], lax.rem(me["z"] + j, 4) * 4 + me["col"]) for j in (1, 2, 3)]
    for dev in who:
        pl.semaphore_signal(bar, inc=1, device_id=dev, device_id_type=MESH)
    count = 6
    if halo:
        last = lax.axis_size("seq") - 1

        @pl.when(me["s"] > 0)
        def _():
            pl.semaphore_signal(bar, inc=1, device_id=(me["c"], me["s"] - 1), device_id_type=MESH)

        @pl.when(me["s"] < last)
        def _():
            pl.semaphore_signal(bar, inc=1, device_id=(me["c"], me["s"] + 1), device_id_type=MESH)

        count = 6 + (me["s"] > 0).astype(jnp.int32) + (me["s"] < last).astype(jnp.int32)
    pl.semaphore_wait(bar, count)


def lane_low():
    return lax.broadcasted_iota(jnp.int32, (128, 128), 1) < HEAD


def pair_rows(v):
    low = lane_low()
    zero = jnp.zeros_like(v)
    return jnp.concatenate([jnp.where(low, v, zero), jnp.where(low, zero, v)], axis=0)


def pair_out(t):
    return jnp.concatenate([t[:HEAD, :128], t[HEAD:, 128:]], axis=0).T


def softmax_block(q2, kn, kf, bias):
    st = jnp.concatenate([dg(kn, q2, NT), dg(kf, q2, NT)], axis=0)
    st = st + jnp.concatenate([bias, bias], axis=1)
    top = jnp.max(st, axis=0, keepdims=True)
    e = jnp.exp(st - top)
    total = jnp.sum(e, axis=0, keepdims=True)
    return e, 1.0 / total


def mask_block(winc, win4, winr, r, b):
    seg_q = winr[r : r + 1, 256 + 128 * b : 384 + 128 * b]
    kk = lax.broadcasted_iota(jnp.int32, (256, 128), 0)
    ii = lax.broadcasted_iota(jnp.int32, (256, 128), 1)
    seg_k = winc[r, 192 + 128 * b : 448 + 128 * b, :]
    near = (jnp.abs(kk - NEAR - ii) <= NEAR) & (seg_k == seg_q)
    pp = lax.broadcasted_iota(jnp.int32, (160, 128), 0)
    qi = lax.broadcasted_iota(jnp.int32, (160, 128), 1)
    seg_p = win4[r, 32 * b : 32 * b + 160, 0:1]
    far = (jnp.abs(4 * pp - REACH - qi) <= REACH) & (seg_p == seg_q)
    return jnp.where(near, 0.0, -1e30), jnp.where(far, 0.0, -1e30)


def fill_masks(winc, win4, winr, bias):
    for r in range(2):
        for b in range(4):
            near, far = mask_block(winc, win4, winr, r, b)
            bias[r * 4 + b, 0:256] = near
            bias[r * 4 + b, 256:416] = far


def head_lanes(h):
    return (
        pl.ds(pl.multiple_of(h * 128, 128), 128),
        pl.ds(pl.multiple_of(768 + h * 128, 128), 128),
    )


def attend(q, kv, pe, bias, att, r, h):
    kl, vl = head_lanes(h)
    for b in range(4):
        n, f, i = slice(b * 128, b * 128 + 256), slice(b * 32, b * 32 + 160), slice(b * 128, b * 128 + 128)
        e, rt = softmax_block(pair_rows(q[r, i, kl]), kv[r, n, kl], pe[r, f, kl], bias[r * 4 + b])
        low = (e * rt).astype(BF)
        values = jnp.concatenate([kv[r, n, vl], pe[r, f, vl]], axis=0)
        att[r, i, kl] = pair_out(dg(values, low, TN)).astype(BF)


def attend_back(q, kv, pe, bias, g, gext, dkv, dpe, r, h):
    kl, vl = head_lanes(h)
    for part in (h, 6 + h):
        dkv[r, part] = jnp.zeros((640, 128), F32)
        dpe[r, part] = jnp.zeros((256, 128), F32)
    for b in range(4):
        n, f, i = slice(b * 128, b * 128 + 256), slice(b * 32, b * 32 + 160), slice(b * 128, b * 128 + 128)
        q2, g2 = pair_rows(q[r, i, kl]), pair_rows(g[r * 512 + b * 128 : r * 512 + b * 128 + 128, kl])
        kn, vn, kf, vf = kv[r, n, kl], kv[r, n, vl], pe[r, f, kl], pe[r, f, vl]
        e, rt = softmax_block(q2, kn, kf, bias[r * 4 + b])
        p = e * rt
        dp = jnp.concatenate([dg(vn, g2, NT), dg(vf, g2, NT)], axis=0)
        delta = jnp.sum(p * dp, axis=0, keepdims=True)
        ds = (p * (dp - delta)).astype(BF)
        low = p.astype(BF)
        dv, dk = dg(low, g2, NN), dg(ds, q2, NN)
        dkv[r, h, n] += dk[:256]
        dkv[r, 6 + h, n] += dv[:256]
        dpe[r, h, f] += dk[256:]
        dpe[r, 6 + h, f] += dv[256:]
        dqt = dg(jnp.concatenate([kn, kf], axis=0), ds, TN)
        gext[r * 640 + 64 + b * 128 : r * 640 + 192 + b * 128, kl] = (pair_out(dqt) * HEAD**-0.5).astype(BF)


def norm_parts(v):
    mean = jnp.mean(v, axis=-1, keepdims=True)
    cen = v - mean
    var = jnp.mean(cen * cen, axis=-1, keepdims=True)
    rs = lax.rsqrt(var + 1e-05)
    return cen * rs, rs


def pack_own(grab, put):
    for name in ("qkv", "out", "up", "down"):
        half = units(name) // 2
        for u in range(units(name)):
            k, lo = spot(name, u)
            put(k, lo, grab(name, 0, 16, u))
        for u in range(half):
            k, lo = spot(name, units(name) + u)
            put(k, lo, jnp.concatenate([grab(name, 16, 24, u), grab(name, 16, 24, u + half)], axis=0))


def hidden_place(n):
    half, r = divmod(n, 1536)
    return (r // 256) * 512 + half * 256 + r % 256


def unpack(name, got, dst):
    half = units(name) // 2

    def pair(p, carry):
        rows = pl.ds(pl.multiple_of(48 * p, 16), 48)
        for u in range(units(name)):
            k, lo = spot(name, u)
            kt, lt = spot(name, units(name) + u % half)
            cut = slice(0, 8) if u < half else slice(8, 16)
            hidden = name in ("up", "down")
            for i in range(0, UNIT, 128) if hidden else (0,):
                n = 128 if hidden else UNIT
                to = hidden_place(u * UNIT + i) if hidden else u * UNIT
                parts = []
                for j in (0, 1):
                    parts.append(got[k, 2 * p + j, :, lo + i : lo + i + n])
                    parts.append(got[kt, 2 * p + j, :, lt + i : lt + i + n][cut])
                dst[rows, to : to + n] = jnp.concatenate(parts, axis=0)
        return carry

    lax.fori_loop(0, 16, pair, 0)


def spread_small(got, taps, gains):
    lane = lax.broadcasted_iota(jnp.int32, (16, 128), 1)

    def place(width, tiles):
        acc = [jnp.zeros((16, 128), F32) for _ in range(tiles)]
        for s in range(32):
            at, off = divmod(width * s, 128)
            v = jnp.where(lane < width, got[0, s, :, CLS:WIDE].astype(F32), 0.0)
            v = pltpu.roll(v, off, 1) if off else v
            acc[at] = acc[at] + jnp.where(lane >= off, v, 0.0)
            if off + width > 128:
                acc[at + 1] = acc[at + 1] + jnp.where(lane < off, v, 0.0)
        return acc

    for i, v in enumerate(place(48, 12)):
        taps[:, i * 128 : (i + 1) * 128] = v
    for i, v in enumerate(place(24, 6)):
        gains[:, i * 128 : (i + 1) * 128] = v


def front_kernel(
    tok, winc, win4, winr, wq, wo, wu, wd, small,
    o_wq, o_wo, o_wu, o_wd, o_taps, o_gains, o_h1, o_q, o_kv, o_pe, o_att, o_bias,
    G, Wq, Wo, Wu, Wd, taps, gains, xe, h1, q, kv, pe, att, bias, chunk,
    send_x, send_y, send_d, send_z, send_g, recv, hsend, hrecv, local,
):
    me = where_am_i()
    c, s, z, col = me["c"], me["s"], me["z"], me["col"]
    mine = c * 16 + s
    last = lax.axis_size("seq") - 1
    has_left, has_right = s > 0, s < last

    def cols(k):
        return WIDE if isinstance(k, int) and k == 0 else CLS

    def hop(k, slot, to, sem):
        part = G.at[k, slot, :, pl.ds(0, cols(k))]
        return pltpu.make_async_remote_copy(
            src_ref=part, dst_ref=part, send_sem=sem, recv_sem=recv.at[k, slot],
            device_id=to, device_id_type=MESH,
        )

    def to_x(k, at):
        return hop(k, c * 16 + at, me["px"], send_x.at[k, at])

    def to_y(k, at):
        return hop(k, c * 16 + at, me["py"], send_y.at[k, at])

    def to_d(k, at):
        return hop(k, c * 16 + at, me["pd"], send_d.at[k, at])

    def to_z(k, j):
        return hop(k, mine, (c, lax.rem(z + j, 4) * 4 + col), send_z.at[k, j - 1])

    def to_g(k, zz):
        even = lax.rem(zz, 2) == 0
        at = zz * 4 + jnp.where(even, me["colx"], me["coly"])
        to = (c, z * 4 + jnp.where(even, me["coly"], me["colx"]))
        return hop(k, c * 16 + at, to, send_g.at[k, zz])

    def got(k, slot):
        hop(k, slot, me["px"], send_x.at[k, 0]).wait_recv()

    def own(k):
        for j in (1, 2, 3):
            to_z(k, j).start()
        to_x(k, s).start()
        to_y(k, s).start()
        to_d(k, s).start()

    def column(k, j):
        at = lax.rem(z + j, 4) * 4 + col
        got(k, c * 16 + at)
        to_x(k, at).start()
        to_y(k, at).start()
        to_d(k, at).start()

    def plane(k, j):
        zz = lax.rem(z + j, 4)
        got(k, c * 16 + zz * 4 + me["colx"])
        to_d(k, zz * 4 + me["colx"]).start()
        got(k, c * 16 + zz * 4 + me["coly"])
        to_d(k, zz * 4 + me["coly"]).start()
        to_g(k, zz).start()

    def diag(k, j):
        at = lax.rem(z + j, 4) * 4 + me["cold"]
        got(k, c * 16 + at)
        to_d(k, at).start()

    def event(e):
        k, i = e // 11 + 1, lax.rem(e, 11)

        @pl.when(i < 4)
        def _():
            plane(k, i)

        @pl.when((i >= 4) & (i < 7) & (k < 3))
        def _():
            column(k + 1, i - 3)

        @pl.when(i >= 7)
        def _():
            diag(k, i - 7)

    def halo_tok(r, right):
        src = tok.at[r, pl.ds(448 if right else 0, 64)]
        dst = xe.at[r, pl.ds(0 if right else 576, 64)]
        i = r * 2 + int(right)
        return pltpu.make_async_remote_copy(
            src_ref=src, dst_ref=dst, send_sem=hsend.at[i], recv_sem=hrecv.at[i],
            device_id=(c, s + 1 if right else s - 1), device_id_type=MESH,
        )

    def halo_pool(r, right):
        src = pe.at[r, pl.ds(128 if right else 64, 64)]
        dst = pe.at[r, pl.ds(0 if right else 192, 64)]
        i = 4 + r * 2 + int(right)
        return pltpu.make_async_remote_copy(
            src_ref=src, dst_ref=dst, send_sem=hsend.at[i], recv_sem=hrecv.at[i],
            device_id=(c, s + 1 if right else s - 1), device_id_type=MESH,
        )

    def both(make, r, act):
        @pl.when(has_right)
        def _():
            act(make(r, True), True)

        @pl.when(has_left)
        def _():
            act(make(r, False), False)

    def arrived(make, r):
        @pl.when(has_left)
        def _():
            make(r, True).wait_recv()

        @pl.when(has_right)
        def _():
            make(r, False).wait_recv()

    load = [pltpu.make_async_copy(tok.at[r], xe.at[r, pl.ds(64, 512)], local.at[r]) for r in range(2)]
    for copy in load:
        copy.start()
    shares = {"qkv": wq, "out": wo, "up": wu, "down": wd}

    def grab(name, a, b, u):
        return shares[name][a:b, u * UNIT : (u + 1) * UNIT]

    def put(k, lo, v):
        G[k, mine, :, lo : lo + UNIT] = v

    pack_own(grab, put)
    G[0, mine, :, CLS:WIDE] = small[...]

    @pl.when(jnp.logical_not(has_left))
    def _():
        for r in range(2):
            xe[r, 0:64] = jnp.zeros((64, 768), BF)
            pe[r, 0:64] = jnp.zeros((64, 1536), BF)

    @pl.when(jnp.logical_not(has_right))
    def _():
        for r in range(2):
            xe[r, 576:640] = jnp.zeros((64, 768), BF)
            pe[r, 192:256] = jnp.zeros((64, 1536), BF)

    greet(me, True)
    own(0)
    for r in range(2):
        both(halo_tok, r, lambda copy, right: copy.start())
    own(1)
    own(2)
    fill_masks(winc, win4, winr, bias)
    for j in (1, 2, 3):
        column(0, j)
    for j in range(4):
        plane(0, j)
    own(3)
    for j in (1, 2, 3):
        column(1, j)
    for j in range(4):
        diag(0, j)

    def other(k):
        def body(i, carry):
            got(k, (1 - c) * 16 + i)
            return carry

        lax.fori_loop(0, 16, body, 0)

    other(0)
    unpack("qkv", G, Wq)
    spread_small(G, taps, gains)
    outs = [
        pltpu.make_async_copy(a, b, local.at[2 + i])
        for i, (a, b) in enumerate(
            [(Wq, o_wq), (taps, o_taps), (gains, o_gains), (h1, o_h1), (q, o_q), (kv, o_kv), (pe, o_pe),
             (att, o_att), (bias, o_bias), (Wo, o_wo), (Wu, o_wu), (Wd, o_wd)]
        )
    ]
    for i in (0, 1, 2, 8):
        outs[i].start()
    for copy in load:
        copy.wait()
    for r in range(2):
        arrived(halo_tok, r)

    for r in range(2):
        def norm_rows(i, carry):
            rows = pl.ds(pl.multiple_of(i * 128, 128), 128)
            n, _ = norm_parts(xe[r, rows].astype(F32))
            h1[r, rows] = (n * gains[5:6] + gains[6:7]).astype(BF)
            return carry

        lax.fori_loop(0, 5, norm_rows, 0)
    outs[3].start()

    for r in range(2):
        def queries(j, carry):
            lanes = pl.ds(pl.multiple_of(j * 256, 256), 256)
            v = dg(h1[r, 64:576], Wq[:, lanes], NN)
            q[r, :, lanes] = v.astype(BF) * jnp.asarray(HEAD**-0.5, BF)
            return carry

        lax.fori_loop(0, 3, queries, 0)
        anchor = win4[r, 64:192, 0:1]
        same = [
            (win4[r, a : a + 128, f : f + 1] == anchor).astype(F32)
            for a, f in ((63, 2), (63, 3), (64, 0), (64, 1), (64, 2))
        ]

        def keys(j, carry):
            event(r * 6 + j)
            lanes = pl.ds(pl.multiple_of(j * 128, 128), 128)
            from_lanes = pl.ds(pl.multiple_of(768 + j * 256, 256), 256)
            to_lanes = pl.ds(pl.multiple_of(j * 256, 256), 256)
            v = dg(h1[r], Wq[:, from_lanes], NN).astype(BF)
            kv[r, :, to_lanes] = v
            chunk[0] = v[:, :128].astype(F32)
            chunk[1] = v[:, 128:].astype(F32)
            for half in range(2):
                hl = pl.ds(pl.multiple_of(j * 256 + half * 128, 128), 128)
                acc = jnp.zeros((128, 128), F32)
                for t in range(5):
                    acc = acc + taps[t : t + 1, hl] * chunk[half, pl.ds(62 + t, 128, stride=4), :] * same[t]
                pe[r, 64:192, hl] = acc.astype(BF)
            return carry

        lax.fori_loop(0, 6, keys, 0)
        both(halo_pool, r, lambda copy, right: copy.start())
    outs[4].start()
    outs[5].start()
    for r in range(2):
        arrived(halo_pool, r)

        def heads_event(h, carry):
            attend(q, kv, pe, bias, att, r, h)
            base = 12 + (r * 6 + h) * 2

            @pl.when(base < 33)
            def _():
                event(base)

            @pl.when(base + 1 < 33)
            def _():
                event(base + 1)

            return carry

        lax.fori_loop(0, 6, heads_event, 0)
    outs[6].start()
    outs[7].start()
    for k in (1, 2, 3):
        other(k)
    for i, (name, dst) in enumerate((("out", Wo), ("up", Wu), ("down", Wd))):
        unpack(name, G, dst)
        outs[9 + i].start()
    for r in range(2):
        both(halo_tok, r, lambda copy, right: copy.wait_send())
        both(halo_pool, r, lambda copy, right: copy.wait_send())
    for k in range(4):
        def done(i, carry):
            to_x(k, i * 4 + col).wait_send()
            to_y(k, i * 4 + col).wait_send()
            to_g(k, i).wait_send()
            for j in range(4):
                to_d(k, i * 4 + j).wait_send()
            return carry

        lax.fori_loop(0, 4, done, 0)
        for j in (1, 2, 3):
            to_z(k, j).wait_send()
    for copy in outs:
        copy.wait()


def front(tok, winc, win4, winr, wq, wo, wu, wd, small):
    sds = jax.ShapeDtypeStruct
    shapes = [
        ((768, 2304), BF), ((768, 768), BF), ((768, 3072), BF), ((768, 3072), BF),
        ((16, 1536), F32), ((16, 768), F32),
        ((2, 640, 768), BF), ((2, 512, 768), BF), ((2, 640, 1536), BF), ((2, 256, 1536), BF),
        ((2, 512, 768), BF), ((8, 416, 128), F32),
    ]
    scratch = [pltpu.VMEM((4, 32, 16, WIDE), BF)]
    scratch += [pltpu.VMEM(sh, dt) for sh, dt in shapes[:6]]
    scratch += [pltpu.VMEM((2, 640, 768), BF)]
    scratch += [pltpu.VMEM(sh, dt) for sh, dt in shapes[6:]]
    scratch += [pltpu.VMEM((2, 640, 128), F32)]
    dma = pltpu.SemaphoreType.DMA
    scratch += [dma((4, 16)), dma((4, 16)), dma((4, 16)), dma((4, 3)), dma((4, 4)), dma((4, 32)), dma((8,)), dma((8,)), dma((14,))]
    return pl.pallas_call(
        front_kernel,
        out_shape=[sds(sh, dt) for sh, dt in shapes],
        in_specs=[ANY] + [VM] * 8,
        out_specs=[ANY] * len(shapes),
        scratch_shapes=scratch,
        compiler_params=pltpu.CompilerParams(collective_id=0, has_side_effects=True, vmem_limit_bytes=VMEM_LIMIT),
    )(tok, winc, win4, winr, wq, wo, wu, wd, small)


def windows(segments):
    block = 512
    padded = jnp.pad(segments, ((0, 0), (REACH, REACH)), constant_values=-1)
    win = lax.dynamic_slice_in_dim(padded, lax.axis_index("seq") * block, block + 2 * REACH, 1)
    return win[:, :, None], win.reshape(2, 256, 4), win


def small_share(pool_taps, ln1_gain, ln1_bias, ln2_gain, ln2_bias):
    rows = jnp.stack([ln1_gain, ln1_bias, ln2_gain, ln2_bias])
    return jnp.concatenate(
        [jnp.pad(pool_taps, ((0, 0), (0, 80))), jnp.pad(rows, ((0, 7), (0, 104)))], axis=0
    )


def gelu_both(u):
    a, b = 0.7978845608028654, 0.044715
    sq = u * u
    t = jnp.tanh(a * u * (1.0 + b * sq))
    half = 0.5 + 0.5 * t
    grad = half + 0.5 * u * (1.0 - t * t) * (a + (3.0 * a * b) * sq)
    return u * half, grad


def pack_pair(lo, hi):
    return jnp.concatenate([lo, hi], axis=0).astype(BF)


def pick_small(tg, lg, put):
    lane = lax.broadcasted_iota(jnp.int32, (16, 128), 1)

    def part(src, width, s):
        at, off = divmod(width * s, 128)
        v = src[:, at * 128 : at * 128 + 128]
        v = pltpu.roll(v, 128 - off, 1) if off else v
        if off + width > 128:
            w = pltpu.roll(src[:, at * 128 + 128 : at * 128 + 256], 128 - off, 1)
            v = jnp.where(lane < 128 - off, v, w)
        return jnp.where(lane < width, v, 0.0)

    for s in range(32):
        put(s, (part(tg, 48, s) + part(lg, 24, s)).astype(BF))


def back_kernel(
    tok_in, att_in, dy_in, wo_in, wu_in, wd_in,
    q_in, kv_in, pe_in, bias_in, h1_in, wq_in, taps, gains, win4,
    o_out, o_gmid, o_in, o_wq, o_wo, o_wu, o_wd, o_small,
    Sf, So, Ss, Rf, Ro, Rq, Rs, gatt, pstage, precv, hstage, hrecv, tg, lg,
    send, recv, psend, prsem, local,
):
    me = where_am_i()
    c, s, z, col = me["c"], me["s"], me["z"], me["col"]
    has_left, has_right = s > 0, s < lax.axis_size("seq") - 1

    def copy(i, a, b):
        return pltpu.make_async_copy(a, b, local.at[i])

    late = []

    def cls(k):
        if k < 3:
            return Sf.at[k, pl.ds(c * 16, 16)], Rf.at[k]
        if k == 3:
            return So.at[pl.ds(c * 16, 16)], Ro
        if k == 4:
            return late[0].at[pl.ds(c * 16, 16)], Rq
        return Ss.at[pl.ds(c * 16, 16)], Rs

    def other(k):
        start = (1 - c) * 16
        if k < 3:
            return Sf.at[k, pl.ds(start, 16)]
        return (So, late[0] if late else None, Ss)[k - 3].at[pl.ds(start, 16)]

    def remote(k, src, slot, i, to):
        return pltpu.make_async_remote_copy(
            src_ref=src, dst_ref=slot, send_sem=send.at[k, i], recv_sem=recv.at[k, i],
            device_id=to, device_id_type=MESH,
        )

    def swap(k):
        return remote(k, other(k), cls(k)[1].at[pl.ds(0, 16)], 0, me["pd"])

    def step_g(k, zz):
        S, R = cls(k)
        to = me["px"] if zz % 2 == 0 else me["py"]
        return remote(k, S.at[zz * 4 + me["cold"]], R.at[16 + zz], 1 + zz, to)

    def step_x(k, zz):
        S, R = cls(k)
        return remote(k, S.at[zz * 4 + me["colx"]], R.at[20 + zz], 5 + zz, me["px"])

    def step_y(k, zz):
        S, R = cls(k)
        return remote(k, S.at[zz * 4 + me["coly"]], R.at[24 + zz], 9 + zz, me["py"])

    def step_z(k, j):
        S, R = cls(k)
        zz = lax.rem(z + j, 4)
        return remote(k, S.at[zz * 4 + col], R.at[27 + j], 12 + j, (c, zz * 4 + col))

    def add(k, at, slots):
        S, R = cls(k)
        v = S[at].astype(F32) + R[at].astype(F32)
        for slot in slots:
            v = v + R[slot].astype(F32)
        return v

    def begin(k):
        swap(k).start()

    def do_g(k, zz):
        if zz == 0:
            swap(k).wait_recv()
        at = zz * 4 + me["cold"]
        cls(k)[0][at] = add(k, at, []).astype(BF)
        step_g(k, zz).start()

    def do_p(k, zz):
        step_g(k, zz).wait_recv()
        even = zz % 2 == 0
        for at, step, has in ((zz * 4 + me["colx"], step_x, not even), (zz * 4 + me["coly"], step_y, even)):
            cls(k)[0][at] = add(k, at, [16 + zz] if has else []).astype(BF)
            step(k, zz).start()

    def arrive(k, zz):
        S, R = cls(k)
        remote(k, S.at[0], R.at[20 + zz], 5 + zz, me["px"]).wait_recv()
        remote(k, S.at[0], R.at[24 + zz], 9 + zz, me["py"]).wait_recv()

    def do_c(k, j):
        zz = lax.rem(z + j, 4)
        arrive(k, zz)
        at = zz * 4 + col
        cls(k)[0][at] = add(k, at, [20 + zz, 24 + zz]).astype(BF)
        step_z(k, j).start()

    def total(k):
        arrive(k, z)
        for j in (1, 2, 3):
            step_z(k, j).wait_recv()
        return add(k, z * 4 + col, [20 + z, 24 + z, 28, 29, 30])

    def drain(k):
        swap(k).wait_send()
        for zz in range(4):
            step_g(k, zz).wait_send()
            step_x(k, zz).wait_send()
            step_y(k, zz).wait_send()
        for j in (1, 2, 3):
            step_z(k, j).wait_send()

    def finish(k):
        v = total(k)
        if k < 3:
            for i in range(2):
                for ref, base in ((o_wu, i * 1536), (o_wd, i * 1536 + 768)):
                    lo, hi = (2 * k + i) * 256, 1536 + (2 * k + i) * 256
                    ref[0:16, lo : lo + 256] = v[:, base : base + 256]
                    ref[0:16, hi : hi + 256] = v[:, base + 256 : base + 512]
                    ref[16:24, lo : lo + 256] = v[0:8, base + 512 : base + 768]
                    ref[16:24, hi : hi + 256] = v[8:16, base + 512 : base + 768]
        elif k < 5:
            ref = o_wo if k == 3 else o_wq
            for i in range(1 if k == 3 else 3):
                at, frm = i * 768, i * 1152
                ref[0:16, at : at + 768] = v[:, frm : frm + 768]
                ref[16:24, at : at + 384] = v[0:8, frm + 768 : frm + 1152]
                ref[16:24, at + 384 : at + 768] = v[8:16, frm + 768 : frm + 1152]
        else:
            o_small[...] = v
        drain(k)

    def halo(src, dst, r, right, base):
        i = base + r * 2 + int(right)
        return pltpu.make_async_remote_copy(
            src_ref=src.at[r, int(right)], dst_ref=dst.at[r, int(right)],
            send_sem=psend.at[i], recv_sem=prsem.at[i],
            device_id=(c, s + 1 if right else s - 1), device_id_type=MESH,
        )

    def both(src, dst, r, base, act):
        @pl.when(has_right)
        def _():
            act(halo(src, dst, r, True, base))

        @pl.when(has_left)
        def _():
            act(halo(src, dst, r, False, base))

    def arrived(src, dst, r, base):
        @pl.when(has_left)
        def _():
            halo(src, dst, r, True, base).wait_recv()

        @pl.when(has_right)
        def _():
            halo(src, dst, r, False, base).wait_recv()

    @pl.when(jnp.logical_not(has_left))
    def _():
        precv[:, 1] = jnp.zeros((2, 64, 1536), BF)
        hrecv[:, 1] = jnp.zeros((2, 64, 768), BF)

    @pl.when(jnp.logical_not(has_right))
    def _():
        precv[:, 0] = jnp.zeros((2, 64, 1536), BF)
        hrecv[:, 0] = jnp.zeros((2, 64, 768), BF)

    tg[...] = jnp.zeros((16, 1536), F32)
    lg[...] = jnp.zeros((16, 768), F32)
    greet(me, True)

    def run(plan, at):
        for i, todo in plan.items():
            @pl.when(at == i)
            def _():
                for fn, k in todo:
                    if fn is begin:
                        begin(k)
                    else:
                        for j in (1, 2, 3) if fn is do_c else (0, 1, 2, 3):
                            fn(k, j)

    def feed_forward(Tok, Att, Dy, Wo, Wu, Wd, mid, h2, DyT, H2T, y, gh2, act, gu):
        loads = [
            copy(i, a, b)
            for i, (a, b) in enumerate(
                [(tok_in, Tok), (att_in, Att), (wo_in, Wo), (dy_in, Dy), (wu_in, Wu), (wd_in, Wd)]
            )
        ]
        for ld in loads:
            ld.start()
        y[...] = jnp.zeros((1024, 768), F32)
        gh2[...] = jnp.zeros((1024, 768), F32)
        for ld in loads[:3]:
            ld.wait()
        mid[...] = dg(Att[...], Wo[...], NN)

        def first(i, carry):
            rows = pl.ds(pl.multiple_of(i * 128, 128), 128)
            v = Tok[rows].astype(F32) + mid[rows]
            mid[rows] = v
            n, _ = norm_parts(v)
            h2[rows] = (n * gains[7:8] + gains[8:9]).astype(BF)
            return carry

        lax.fori_loop(0, 8, first, 0)
        loads[3].wait()

        def flip(i, carry):
            rows = pl.ds(pl.multiple_of(i * 128, 128), 128)
            for j in range(3):
                cols = slice(j * 256, j * 256 + 256)
                DyT[cols, rows] = Dy[rows, cols].T
                H2T[cols, rows] = h2[rows, cols].T
            return carry

        lax.fori_loop(0, 8, flip, 0)
        loads[4].wait()
        loads[5].wait()
        plan = {
            5: [(begin, 0)], 6: [(do_g, 0)], 8: [(do_p, 0)], 9: [(do_c, 0)],
            11: [(begin, 1)], 12: [(do_g, 1)], 14: [(do_p, 1)], 15: [(do_c, 1)], 17: [(begin, 2)],
        }

        def chunk(j, carry):
            lanes = [pl.ds(pl.multiple_of(j * 512 + h * 256, 256), 256) for h in range(2)]
            whole = pl.ds(pl.multiple_of(j * 512, 512), 512)
            for m in range(2):
                rows = slice(m * 512, m * 512 + 512)
                for h in range(2):
                    u = dg(h2[rows], Wu[:, lanes[h]], NN)
                    ga = dg(Dy[rows], Wd[:, lanes[h]], NN)
                    a, da = gelu_both(u)
                    act[rows, h * 256 : h * 256 + 256] = a.astype(BF)
                    gu[rows, h * 256 : h * 256 + 256] = (ga * da).astype(BF)
            run(plan, j * 3)
            y[...] += dg(act[...], Wd[:, whole], NT)
            gh2[...] += dg(gu[...], Wu[:, whole], NT)
            run(plan, j * 3 + 1)
            for which, (left, right) in enumerate(((H2T, gu), (DyT, act))):
                base = lax.rem(j, 2) * 1536 + which * 768
                at = [pl.ds(pl.multiple_of(base + i * 256, 256), 256) for i in range(3)]
                dws = dg(left[...], right[...], NN)
                for i in range(32):
                    head, tail = dws[i * 24 : i * 24 + 16].astype(BF), dws[i * 24 + 16 : i * 24 + 24]
                    Sf[j // 2, i, :, at[0]] = head[:, 0:256]
                    Sf[j // 2, i, :, at[1]] = head[:, 256:512]
                    Sf[j // 2, i, :, at[2]] = pack_pair(tail[:, 0:256], tail[:, 256:512])
            run(plan, j * 3 + 2)
            return carry

        lax.fori_loop(0, 6, chunk, 0)

        def last(i, carry):
            rows = pl.ds(pl.multiple_of(i * 128, 128), 128)
            v = mid[rows]
            Tok[rows] = (v + y[rows]).astype(BF)
            n, rs = norm_parts(v)
            g = gh2[rows]
            e = g * gains[7:8]
            gm = Dy[rows].astype(F32) + rs * (
                e - jnp.mean(e, axis=-1, keepdims=True) - n * jnp.mean(e * n, axis=-1, keepdims=True)
            )
            y[rows] = gm
            h2[rows] = gm.astype(BF)
            a, b = carry
            return a + jnp.sum((g * n).reshape(16, 8, 768), axis=0), b + jnp.sum(g.reshape(16, 8, 768), axis=0)

        zero = jnp.zeros((8, 768), F32)
        a, b = lax.fori_loop(0, 8, last, (zero, zero))
        lg[7:8] = jnp.sum(a, axis=0, keepdims=True)
        lg[8:9] = jnp.sum(b, axis=0, keepdims=True)
        store = [copy(6, Tok, o_out), copy(7, y, o_gmid)]
        for st in store:
            st.start()

        def flip_att(i, carry):
            rows = pl.ds(pl.multiple_of(i * 128, 128), 128)
            for j in range(3):
                DyT[j * 256 : j * 256 + 256, rows] = Att[rows, j * 256 : j * 256 + 256].T
            return carry

        lax.fori_loop(0, 8, flip_att, 0)
        gatt[...] = dg(h2[...], Wo[...], NT).astype(BF)
        dws = dg(DyT[...], h2[...], NN)
        for i in range(32):
            tail = dws[i * 24 + 16 : i * 24 + 24]
            So[i, :, 0:768] = dws[i * 24 : i * 24 + 16].astype(BF)
            So[i, :, 768:1152] = pack_pair(tail[:, 0:384], tail[:, 384:768])
        begin(3)
        for st in store:
            st.wait()

    def attention(gext, q, kv, pe, bias, dkv, dpe, chunk):
        loads = [
            copy(4 + i, a, b)
            for i, (a, b) in enumerate([(q_in, q), (kv_in, kv), (pe_in, pe), (bias_in, bias)])
        ]
        for ld in loads:
            ld.start()
        for r in range(2):
            gext[r * 640 : r * 640 + 64, 0:768] = jnp.zeros((64, 768), BF)
            gext[r * 640 + 576 : r * 640 + 640, 0:768] = jnp.zeros((64, 768), BF)
        for ld in loads:
            ld.wait()
        plan = {
            0: [(do_g, 2)], 1: [(do_g, 3)], 2: [(do_p, 2)], 3: [(do_p, 3)], 4: [(do_c, 2)], 5: [(do_c, 3)],
        }
        for r in range(2):
            def heads(h, carry):
                attend_back(q, kv, pe, bias, gatt, gext, dkv, dpe, r, h)
                if r == 0:
                    run(plan, h)
                return carry

            lax.fori_loop(0, 6, heads, 0)
            for t in range(12):
                lanes = slice(t * 128, t * 128 + 128)
                pstage[r, 0, :, lanes] = dpe[r, t, 0:64].astype(BF)
                pstage[r, 1, :, lanes] = dpe[r, t, 192:256].astype(BF)
            both(pstage, precv, r, 0, lambda cp: cp.start())

        for r in range(2):
            anchor = win4[r, 64:192, 0:1]
            same = [
                (win4[r, a : a + 128, f : f + 1] == anchor).astype(F32)
                for a, f in ((63, 2), (63, 3), (64, 0), (64, 1), (64, 2))
            ]
            arrived(pstage, precv, r, 0)

            def pool_back(t, carry):
                lanes = pl.ds(pl.multiple_of(t * 128, 128), 128)
                low = dpe[r, t, 64:128] + precv[r, 1, :, lanes].astype(F32)
                high = dpe[r, t, 128:192] + precv[r, 0, :, lanes].astype(F32)
                gp = jnp.concatenate([low, high], axis=0)
                chunk[...] = kv[r, :, lanes].astype(F32)
                for i in range(5):
                    at = pl.ds(62 + i, 128, stride=4)
                    gm = gp * same[i]
                    tg[i : i + 1, lanes] += jnp.sum(gm * chunk[at, :], axis=0, keepdims=True)
                    dkv[r, t, at, :] += gm * taps[i : i + 1, lanes]
                out_lanes = pl.ds(pl.multiple_of(768 + t * 128, 128), 128)
                gext[r * 640 : r * 640 + 640, out_lanes] = dkv[r, t].astype(BF)
                return carry

            lax.fori_loop(0, 12, pool_back, 0)

    def projection(gext, h1, h1t, wq, tok, gmid, gh, Sq):
        late.append(Sq)
        loads = [
            copy(9 + i, a, b)
            for i, (a, b) in enumerate([(h1_in, h1), (wq_in, wq), (tok_in, tok), (o_gmid, gmid)])
        ]
        for ld in loads:
            ld.start()
        loads[0].wait()
        for r in range(2):
            def flip(i, carry):
                rows = pl.ds(pl.multiple_of(i * 128, 128), 128)
                for j in range(3):
                    to = pl.ds(pl.multiple_of(r * 640 + i * 128, 128), 128)
                    h1t[j * 256 : j * 256 + 256, to] = h1[r, rows, j * 256 : j * 256 + 256].T
                return carry

            lax.fori_loop(0, 5, flip, 0)

        for j in range(3):
            dws = dg(h1t[...], gext[:, j * 768 : j * 768 + 768], NN)
            for i in range(32):
                tail = dws[i * 24 + 16 : i * 24 + 24]
                Sq[i, :, j * 1152 : j * 1152 + 768] = dws[i * 24 : i * 24 + 16].astype(BF)
                Sq[i, :, j * 1152 + 768 : j * 1152 + 1152] = pack_pair(tail[:, 0:384], tail[:, 384:768])
        begin(4)
        for k in range(4):
            finish(k)
        for ld in loads[1:]:
            ld.wait()
        for r in range(2):
            gh[r] = dg(gext[r * 640 : r * 640 + 640], wq[...], NT)
            hstage[r, 0] = gh[r, 0:64].astype(BF)
            hstage[r, 1] = gh[r, 576:640].astype(BF)
            both(hstage, hrecv, r, 4, lambda cp: cp.start())
            for zz in range(4):
                (do_g if r == 0 else do_p)(4, zz)
        for r in range(2):
            arrived(hstage, hrecv, r, 4)
            gh[r, 64:128] += hrecv[r, 1].astype(F32)
            gh[r, 512:576] += hrecv[r, 0].astype(F32)
        zero = jnp.zeros((8, 768), F32)
        acc = (zero, zero)
        for r in range(2):
            def rows_norm(i, carry):
                flat = pl.ds(pl.multiple_of(r * 512 + i * 128, 128), 128)
                n, rs = norm_parts(tok[flat].astype(F32))
                g = gh[r, pl.ds(pl.multiple_of(i * 128 + 64, 64), 128)]
                e = g * gains[5:6]
                gmid[flat] += rs * (
                    e - jnp.mean(e, axis=-1, keepdims=True) - n * jnp.mean(e * n, axis=-1, keepdims=True)
                )
                a, b = carry
                return a + jnp.sum((g * n).reshape(16, 8, 768), axis=0), b + jnp.sum(g.reshape(16, 8, 768), axis=0)

            acc = lax.fori_loop(0, 4, rows_norm, acc)
        out = copy(13, gmid, o_in)
        out.start()
        lg[5:6] = jnp.sum(acc[0], axis=0, keepdims=True)
        lg[6:7] = jnp.sum(acc[1], axis=0, keepdims=True)

        def put(i, v):
            Ss[i] = v

        pick_small(tg, lg, put)
        begin(5)
        for j in (1, 2, 3):
            do_c(4, j)
        for zz in range(4):
            do_g(5, zz)
        for zz in range(4):
            do_p(5, zz)
        for j in (1, 2, 3):
            do_c(5, j)
        finish(4)
        finish(5)
        out.wait()

    vm = pltpu.VMEM
    tall, wide = (lambda dt: vm((1024, 768), dt)), (lambda dt: vm((768, 1024), dt))
    pl.run_scoped(
        feed_forward,
        tall(BF), tall(BF), tall(BF), vm((768, 768), BF), vm((768, 3072), BF), vm((768, 3072), BF),
        tall(F32), tall(BF), wide(BF), wide(BF), tall(F32), tall(F32), vm((1024, 512), BF), vm((1024, 512), BF),
    )

    def rest(gext):
        pl.run_scoped(
            functools.partial(attention, gext),
            vm((2, 512, 768), BF), vm((2, 640, 1536), BF), vm((2, 256, 1536), BF), vm((8, 416, 128), F32),
            vm((2, 12, 640, 128), F32), vm((2, 12, 256, 128), F32), vm((640, 128), F32),
        )
        pl.run_scoped(
            functools.partial(projection, gext),
            vm((2, 640, 768), BF), vm((768, 1280), BF), vm((768, 2304), BF), tall(BF),
            tall(F32), vm((2, 640, 768), F32), vm((32, 16, 3456), BF),
        )

    pl.run_scoped(rest, vm((1280, 2304), BF))
    for r in range(2):
        both(pstage, precv, r, 0, lambda cp: cp.wait_send())
        both(hstage, hrecv, r, 4, lambda cp: cp.wait_send())


def back_part(*args):
    sds = jax.ShapeDtypeStruct
    vm, dma = pltpu.VMEM, pltpu.SemaphoreType.DMA
    return pl.pallas_call(
        back_kernel,
        out_shape=[
            sds((1024, 768), BF), sds((1024, 768), F32), sds((1024, 768), F32),
            sds((24, 2304), F32), sds((24, 768), F32), sds((24, 3072), F32), sds((24, 3072), F32), sds((16, 128), F32),
        ],
        in_specs=[ANY] * 12 + [VM] * 3,
        out_specs=[ANY] * 3 + [VM] * 5,
        scratch_shapes=[
            vm((3, 32, 16, 3072), BF), vm((32, 16, 1152), BF), vm((32, 16, 128), BF),
            vm((3, 31, 16, 3072), BF), vm((31, 16, 1152), BF), vm((31, 16, 3456), BF), vm((31, 16, 128), BF),
            vm((1024, 768), BF),
            vm((2, 2, 64, 1536), BF), vm((2, 2, 64, 1536), BF), vm((2, 2, 64, 768), BF), vm((2, 2, 64, 768), BF),
            vm((16, 1536), F32), vm((16, 768), F32),
            dma((6, 16)), dma((6, 16)), dma((8,)), dma((8,)), dma((14,)),
        ],
        compiler_params=pltpu.CompilerParams(collective_id=1, has_side_effects=True, vmem_limit_bytes=VMEM_LIMIT),
    )(*args)


def with_halo(x, sides, width):
    for axis, dim in sides:
        size, length = (lax.axis_size(axis), x.shape[dim])
        up = [(i, (i + 1) % size) for i in range(size - 1)]
        down = [(j, i) for i, j in up]
        last = lax.slice_in_dim(x, length - width, length, axis=dim)
        first = lax.slice_in_dim(x, 0, width, axis=dim)
        before = lax.ppermute(last, axis, up)
        after = lax.ppermute(first, axis, down)
        x = jnp.concatenate([before, x, after], axis=dim)
    return x


def layer_norm(inputs, norm_gain, norm_bias):
    middle = jnp.mean(inputs, axis=-1, keepdims=True)
    centred = inputs - middle
    spread = jnp.mean(centred * centred, axis=-1, keepdims=True)
    return centred * lax.rsqrt(spread + 1e-05) * norm_gain + norm_bias


def pool_local(extended, taps_in, seg_window):
    block_rows = extended.shape[0] - 2 * NEAR
    anchors = seg_window[REACH : REACH + block_rows : 4]
    pooled = jnp.zeros((block_rows // 4, extended.shape[1]), jnp.float32)
    for offset in range(5):
        start_row = NEAR - 2 + offset
        picked = extended[start_row : start_row + block_rows : 4]
        seg_start = REACH - 2 + offset
        same_doc = (seg_window[seg_start : seg_start + block_rows : 4] == anchors).astype(
            jnp.float32
        )
        pooled = pooled + taps_in[offset] * picked * same_doc[:, None]
    return pooled


def window_masks(seg_window, block_rows):
    seg_query = seg_window[REACH : REACH + block_rows]
    seg_key = seg_window[REACH - NEAR : REACH + block_rows + NEAR]
    seg_pool = seg_window[0 : block_rows + 2 * REACH : 4]
    q_index = jnp.arange(block_rows, dtype=jnp.int32)
    k_index = jnp.arange(seg_key.shape[0], dtype=jnp.int32)
    p_index = jnp.arange(seg_pool.shape[0], dtype=jnp.int32)
    near_mask = (jnp.abs(q_index[:, None] - k_index[None, :] + NEAR) <= NEAR) & (
        seg_query[:, None] == seg_key[None, :]
    )
    far_mask = (jnp.abs(4 * p_index[None, :] - REACH - q_index[:, None]) <= REACH) & (
        seg_query[:, None] == seg_pool[None, :]
    )
    return (near_mask, far_mask)


def scores_of(queries, near_keys, far_keys, near_mask, far_mask):
    score_scale = HEAD ** (-0.5)
    near_scores = (
        jnp.einsum("qhd,khd->hqk", queries, near_keys, preferred_element_type=jnp.float32)
        * score_scale
    )
    far_scores = (
        jnp.einsum("qhd,khd->hqk", queries, far_keys, preferred_element_type=jnp.float32)
        * score_scale
    )
    return (
        jnp.where(near_mask[None], near_scores, -1e30),
        jnp.where(far_mask[None], far_scores, -1e30),
    )


def normalise(near_scores, far_scores, near_mask, far_mask, row_max, row_total):
    near_prob = jnp.where(near_mask[None], jnp.exp(near_scores - row_max), 0.0) / row_total
    far_prob = jnp.where(far_mask[None], jnp.exp(far_scores - row_max), 0.0) / row_total
    return (near_prob, far_prob)


def add_rims(middle_part, rim_values, rim_width):
    extra = middle_part.shape[0] - rim_width
    return (
        middle_part
        + jnp.pad(rim_values[:rim_width], ((0, extra), (0, 0)))
        + jnp.pad(rim_values[-rim_width:], ((extra, 0), (0, 0)))
    )


def shards(
    tokens,
    segments,
    cotangent,
    ln1_gain,
    ln1_bias,
    w_qkv,
    pool_taps,
    w_out,
    ln2_gain,
    ln2_bias,
    w_up,
    w_down,
):
    block_rows = tokens.shape[1]
    model_width = tokens.shape[2]
    pool_half = REACH // 4
    score_scale = HEAD ** (-0.5)
    offset_tokens = lax.axis_index("seq") * block_rows
    outputs = []
    input_grads = []
    summed = None
    for micro_step in range(tokens.shape[0]):
        gathered = (
            lax.all_gather(ln1_gain, ("dp", "seq"), axis=0, tiled=True),
            lax.all_gather(ln1_bias, ("dp", "seq"), axis=0, tiled=True),
            lax.all_gather(w_qkv, ("dp", "seq"), axis=0, tiled=True),
            lax.all_gather(pool_taps, ("dp", "seq"), axis=1, tiled=True),
            lax.all_gather(w_out, ("dp", "seq"), axis=0, tiled=True),
            lax.all_gather(ln2_gain, ("dp", "seq"), axis=0, tiled=True),
            lax.all_gather(ln2_bias, ("dp", "seq"), axis=0, tiled=True),
            lax.all_gather(w_up, ("dp", "seq"), axis=0, tiled=True),
            lax.all_gather(w_down, ("dp", "seq"), axis=1, tiled=True),
        )
        gain_one, bias_one, proj_qkv, taps, proj_out, gain_two, bias_two, proj_up, proj_down = (
            gathered
        )
        seg_row = segments[micro_step]
        seg_padded = jnp.pad(seg_row, (REACH, REACH), constant_values=-1)
        seg_window = lax.dynamic_slice_in_dim(
            seg_padded, offset_tokens, block_rows + 2 * REACH, 0
        )
        near_mask, far_mask = window_masks(seg_window, block_rows)
        inputs = tokens[micro_step].astype(jnp.float32)
        gain_float = gain_one.astype(jnp.float32)
        bias_float = bias_one.astype(jnp.float32)
        gain_second = gain_two.astype(jnp.float32)
        bias_second = bias_two.astype(jnp.float32)
        normed = layer_norm(inputs, gain_float, bias_float).astype(jnp.bfloat16)
        projected = jnp.dot(normed, proj_qkv, preferred_element_type=jnp.float32).astype(
            jnp.bfloat16
        )
        queries = projected[:, :model_width].reshape(block_rows, HEADS, HEAD)
        key_value = projected[:, model_width:]
        extended = with_halo(key_value, (("seq", 0),), NEAR)
        ext_float = extended.astype(jnp.float32)
        taps_float = taps.astype(jnp.float32)
        pooled = pool_local(ext_float, taps_float, seg_window).astype(jnp.bfloat16)
        pool_ext = with_halo(pooled, (("seq", 0),), pool_half)
        near_keys = extended[:, :model_width].reshape(-1, HEADS, HEAD)
        near_values = extended[:, model_width:].reshape(-1, HEADS, HEAD)
        far_keys = pool_ext[:, :model_width].reshape(-1, HEADS, HEAD)
        far_values = pool_ext[:, model_width:].reshape(-1, HEADS, HEAD)
        near_scores, far_scores = scores_of(queries, near_keys, far_keys, near_mask, far_mask)
        row_max = jnp.maximum(
            jnp.max(near_scores, axis=2, keepdims=True), jnp.max(far_scores, axis=2, keepdims=True)
        )
        near_exp = jnp.where(near_mask[None], jnp.exp(near_scores - row_max), 0.0)
        far_exp = jnp.where(far_mask[None], jnp.exp(far_scores - row_max), 0.0)
        row_total = jnp.sum(near_exp, axis=2, keepdims=True) + jnp.sum(
            far_exp, axis=2, keepdims=True
        )
        near_low = (near_exp / row_total).astype(jnp.bfloat16)
        far_low = (far_exp / row_total).astype(jnp.bfloat16)
        mixed_sum = jnp.einsum(
            "hqk,khd->qhd", near_low, near_values, preferred_element_type=jnp.float32
        ) + jnp.einsum("hqk,khd->qhd", far_low, far_values, preferred_element_type=jnp.float32)
        attended = mixed_sum.reshape(block_rows, model_width).astype(jnp.bfloat16)
        branch = jnp.dot(attended, proj_out, preferred_element_type=jnp.float32)
        middle = inputs + branch
        normed_two = layer_norm(middle, gain_second, bias_second).astype(jnp.bfloat16)
        upward = jnp.dot(normed_two, proj_up, preferred_element_type=jnp.float32)
        activated = jax.nn.gelu(upward).astype(jnp.bfloat16)
        result = middle + jnp.dot(activated, proj_down, preferred_element_type=jnp.float32)
        outputs.append(result.astype(jnp.bfloat16))
        regathered = (
            lax.all_gather(ln1_gain, ("dp", "seq"), axis=0, tiled=True),
            lax.all_gather(ln1_bias, ("dp", "seq"), axis=0, tiled=True),
            lax.all_gather(w_qkv, ("dp", "seq"), axis=0, tiled=True),
            lax.all_gather(pool_taps, ("dp", "seq"), axis=1, tiled=True),
            lax.all_gather(w_out, ("dp", "seq"), axis=0, tiled=True),
            lax.all_gather(ln2_gain, ("dp", "seq"), axis=0, tiled=True),
            lax.all_gather(ln2_bias, ("dp", "seq"), axis=0, tiled=True),
            lax.all_gather(w_up, ("dp", "seq"), axis=0, tiled=True),
            lax.all_gather(w_down, ("dp", "seq"), axis=1, tiled=True),
        )
        back_qkv = regathered[2]
        back_out = regathered[4]
        back_up = regathered[7]
        back_down = regathered[8]
        grad_out = cotangent[micro_step]
        grad_act = jnp.dot(grad_out, back_down.T, preferred_element_type=jnp.float32)
        grad_down = jnp.dot(activated.T, grad_out, preferred_element_type=jnp.float32)
        gelu_value, gelu_back = jax.vjp(jax.nn.gelu, upward)
        grad_upin = gelu_back(grad_act)[0].astype(jnp.bfloat16)
        grad_upw = jnp.dot(normed_two.T, grad_upin, preferred_element_type=jnp.float32)
        grad_normed_two = jnp.dot(grad_upin, back_up.T, preferred_element_type=jnp.float32)
        norm_value_two, norm_back_two = jax.vjp(layer_norm, middle, gain_second, bias_second)
        grad_mid_part, grad_gain_two, grad_bias_two = norm_back_two(grad_normed_two)
        grad_middle = grad_out.astype(jnp.float32) + grad_mid_part
        grad_branch = grad_middle.astype(jnp.bfloat16)
        grad_outw = jnp.dot(attended.T, grad_branch, preferred_element_type=jnp.float32)
        grad_mixed = (
            jnp.dot(grad_branch, back_out.T, preferred_element_type=jnp.float32)
            .astype(jnp.bfloat16)
            .reshape(block_rows, HEADS, HEAD)
        )
        near_scores, far_scores = scores_of(queries, near_keys, far_keys, near_mask, far_mask)
        near_prob, far_prob = normalise(
            near_scores, far_scores, near_mask, far_mask, row_max, row_total
        )
        near_low = near_prob.astype(jnp.bfloat16)
        far_low = far_prob.astype(jnp.bfloat16)
        grad_near_values = jnp.einsum(
            "hqk,qhd->khd", near_low, grad_mixed, preferred_element_type=jnp.float32
        )
        grad_far_values = jnp.einsum(
            "hqk,qhd->khd", far_low, grad_mixed, preferred_element_type=jnp.float32
        )
        grad_near_prob = jnp.einsum(
            "qhd,khd->hqk", grad_mixed, near_values, preferred_element_type=jnp.float32
        )
        grad_far_prob = jnp.einsum(
            "qhd,khd->hqk", grad_mixed, far_values, preferred_element_type=jnp.float32
        )
        row_delta = jnp.sum(near_prob * grad_near_prob, axis=2, keepdims=True) + jnp.sum(
            far_prob * grad_far_prob, axis=2, keepdims=True
        )
        grad_near_scores = (near_prob * (grad_near_prob - row_delta)).astype(jnp.bfloat16)
        grad_far_scores = (far_prob * (grad_far_prob - row_delta)).astype(jnp.bfloat16)
        grad_queries = (
            jnp.einsum(
                "hqk,khd->qhd", grad_near_scores, near_keys, preferred_element_type=jnp.float32
            )
            + jnp.einsum(
                "hqk,khd->qhd", grad_far_scores, far_keys, preferred_element_type=jnp.float32
            )
        ) * score_scale
        grad_near_keys = (
            jnp.einsum(
                "hqk,qhd->khd", grad_near_scores, queries, preferred_element_type=jnp.float32
            )
            * score_scale
        )
        grad_far_keys = (
            jnp.einsum("hqk,qhd->khd", grad_far_scores, queries, preferred_element_type=jnp.float32)
            * score_scale
        )
        grad_extended = jnp.concatenate(
            [grad_near_keys.reshape(-1, model_width), grad_near_values.reshape(-1, model_width)],
            axis=1,
        )
        grad_pool_ext = jnp.concatenate(
            [grad_far_keys.reshape(-1, model_width), grad_far_values.reshape(-1, model_width)],
            axis=1,
        )
        pool_edges = jnp.concatenate(
            [grad_pool_ext[:pool_half], grad_pool_ext[-pool_half:]], axis=0
        )
        pool_returned = with_halo(pool_edges.astype(jnp.bfloat16), (("seq", 0),), pool_half).astype(
            pool_edges.dtype
        )
        grad_pooled = add_rims(grad_pool_ext[pool_half:-pool_half], pool_returned, pool_half)
        pool_value, pool_back = jax.vjp(
            lambda ext_in, taps_part: pool_local(ext_in, taps_part, seg_window),
            ext_float,
            taps_float,
        )
        grad_ext_pool, grad_taps = pool_back(grad_pooled)
        grad_extended = grad_extended + grad_ext_pool
        token_edges = jnp.concatenate(
            [grad_extended[:NEAR], grad_extended[-NEAR:]], axis=0
        )
        token_returned = with_halo(
            token_edges.astype(jnp.bfloat16), (("seq", 0),), NEAR
        ).astype(token_edges.dtype)
        grad_kv = add_rims(grad_extended[NEAR:-NEAR], token_returned, NEAR)
        grad_projected = jnp.concatenate(
            [grad_queries.reshape(block_rows, model_width), grad_kv], axis=1
        ).astype(jnp.bfloat16)
        grad_qkvw = jnp.dot(normed.T, grad_projected, preferred_element_type=jnp.float32)
        grad_normed = jnp.dot(grad_projected, back_qkv.T, preferred_element_type=jnp.float32)
        norm_value_one, norm_back_one = jax.vjp(layer_norm, inputs, gain_float, bias_float)
        grad_in_part, grad_gain_one, grad_bias_one = norm_back_one(grad_normed)
        input_grads.append(grad_middle + grad_in_part)
        shares = (
            lax.psum_scatter(grad_gain_one, ("dp", "seq"), scatter_dimension=0, tiled=True),
            lax.psum_scatter(grad_bias_one, ("dp", "seq"), scatter_dimension=0, tiled=True),
            lax.psum_scatter(grad_qkvw, ("dp", "seq"), scatter_dimension=0, tiled=True),
            lax.psum_scatter(grad_taps, ("dp", "seq"), scatter_dimension=1, tiled=True),
            lax.psum_scatter(grad_outw, ("dp", "seq"), scatter_dimension=0, tiled=True),
            lax.psum_scatter(grad_gain_two, ("dp", "seq"), scatter_dimension=0, tiled=True),
            lax.psum_scatter(grad_bias_two, ("dp", "seq"), scatter_dimension=0, tiled=True),
            lax.psum_scatter(grad_upw, ("dp", "seq"), scatter_dimension=0, tiled=True),
            lax.psum_scatter(grad_down, ("dp", "seq"), scatter_dimension=1, tiled=True),
        )
        if summed is None:
            summed = shares
        else:
            summed = jax.tree.map(jnp.add, summed, shares)
    return (
        jnp.stack(outputs),
        jnp.stack(input_grads),
        summed[0],
        summed[1],
        summed[2],
        summed[3],
        summed[4],
        summed[5],
        summed[6],
        summed[7],
        summed[8],
    )


def chained(
    tokens, segments, cotangent, ln1_gain, ln1_bias, w_qkv, pool_taps, w_out, ln2_gain, ln2_bias, w_up, w_down,
):
    winc, win4, winr = windows(segments)
    small = small_share(pool_taps, ln1_gain, ln1_bias, ln2_gain, ln2_bias)
    wq, wo, wu, wd, taps, gains, h1, q, kv, pe, att, bias = front(
        tokens, winc, win4, winr, w_qkv, w_out, w_up, w_down.T, small
    )
    flat, split = (1024, 768), (2, 512, 768)
    out, _, g_in, g_wq, g_wo, g_wu, g_wd, g_small = back_part(
        tokens.reshape(flat), att.reshape(flat), cotangent.reshape(flat), wo, wu, wd,
        q, kv, pe, bias, h1, wq, taps, gains, win4,
    )
    return (
        out.reshape(split), g_in.reshape(split), g_small[5, :24], g_small[6, :24], g_wq, g_small[0:5, :48], g_wo,
        g_small[7, :24], g_small[8, :24], g_wu, g_wd.T,
    )


def solution(mesh):
    both = ("dp", "seq")
    row, tok, first, second = P(both), P("dp", "seq", None), P(both, None), P(None, both)
    small_mesh = mesh.shape["dp"] == 2 and mesh.shape["seq"] == 16
    return jax.shard_map(
        chained if small_mesh else shards,
        mesh=mesh,
        in_specs=(tok, P("dp", None), tok, row, row, first, second, first, row, row, first, second),
        out_specs=(tok, tok, row, row, first, second, first, row, row, first, second),
        check_vma=False,
    )
```

```python
import functools

import jax
import jax.numpy as jnp
from jax import lax
from jax.experimental import pallas as pl
from jax.experimental.pallas import tpu as pltpu
from jax.sharding import PartitionSpec as P

HEADS = 12
HEAD = 64
NEAR = 64
REACH = 256
F32, BF = jnp.float32, jnp.bfloat16
NT = (((1,), (1,)), ((), ()))
TN = (((0,), (0,)), ((), ()))
NN = (((1,), (0,)), ((), ()))
MESH = pl.DeviceIdType.MESH
ANY = pl.BlockSpec(memory_space=pl.ANY)
VM = pl.BlockSpec(memory_space=pltpu.VMEM)
VMEM_LIMIT = 62 * 2**20
UNIT = 384
CLS = 3456
WIDE = 3584
PLACE = {"qkv": (0, 0, 2304), "out": (1, 0, 768), "up": (1, 3, 3072), "down": (1, 15, 3072)}


def dg(a, b, dims):
    return lax.dot_general(a, b, dims, preferred_element_type=F32)


def spot(name, unit):
    first, start, _ = PLACE[name]
    at = start + unit
    return first + at // 9, (at % 9) * UNIT


def units(name):
    return PLACE[name][2] // UNIT


def where_am_i():
    c = lax.axis_index("dp")
    s = lax.axis_index("seq")
    z, col = s // 4, s % 4
    x, y = col % 2, col // 2
    colx, coly, cold = y * 2 + (1 - x), (1 - y) * 2 + x, 3 - col
    return dict(
        c=c, s=s, z=z, col=col, colx=colx, coly=coly, cold=cold,
        px=(c, z * 4 + colx), py=(c, z * 4 + coly), pd=(1 - c, s),
    )


def greet(me, halo):
    bar = pltpu.get_barrier_semaphore()
    who = [me["px"], me["py"], me["pd"]]
    who += [(me["c"], lax.rem(me["z"] + j, 4) * 4 + me["col"]) for j in (1, 2, 3)]
    for dev in who:
        pl.semaphore_signal(bar, inc=1, device_id=dev, device_id_type=MESH)
    count = 6
    if halo:
        last = lax.axis_size("seq") - 1

        @pl.when(me["s"] > 0)
        def _():
            pl.semaphore_signal(bar, inc=1, device_id=(me["c"], me["s"] - 1), device_id_type=MESH)

        @pl.when(me["s"] < last)
        def _():
            pl.semaphore_signal(bar, inc=1, device_id=(me["c"], me["s"] + 1), device_id_type=MESH)

        count = 6 + (me["s"] > 0).astype(jnp.int32) + (me["s"] < last).astype(jnp.int32)
    pl.semaphore_wait(bar, count)


def greet_all(me):
    bar = pltpu.get_barrier_semaphore()
    pl.semaphore_signal(bar, inc=1, device_id=me["pd"], device_id_type=MESH)
    for d in range(1, 16):
        pl.semaphore_signal(bar, inc=1, device_id=(me["c"], lax.rem(me["s"] + d, 16)), device_id_type=MESH)
    pl.semaphore_wait(bar, 16)


def lane_low():
    return lax.broadcasted_iota(jnp.int32, (128, 128), 1) < HEAD


def pair_rows(v):
    low = lane_low()
    zero = jnp.zeros_like(v)
    return jnp.concatenate([jnp.where(low, v, zero), jnp.where(low, zero, v)], axis=0)


def pair_out(t):
    return jnp.concatenate([t[:HEAD, :128], t[HEAD:, 128:]], axis=0).T


def softmax_block(q2, kn, kf, bias):
    st = jnp.concatenate([dg(kn, q2, NT), dg(kf, q2, NT)], axis=0)
    st = st + jnp.concatenate([bias, bias], axis=1)
    top = jnp.max(st, axis=0, keepdims=True)
    e = jnp.exp(st - top)
    total = jnp.sum(e, axis=0, keepdims=True)
    return e, 1.0 / total, top + jnp.log(total)


def mask_block(winc, win4, winr, r, b):
    seg_q = winr[r : r + 1, 256 + 128 * b : 384 + 128 * b]
    kk = lax.broadcasted_iota(jnp.int32, (256, 128), 0)
    ii = lax.broadcasted_iota(jnp.int32, (256, 128), 1)
    seg_k = winc[r, 192 + 128 * b : 448 + 128 * b, :]
    near = (jnp.abs(kk - NEAR - ii) <= NEAR) & (seg_k == seg_q)
    pp = lax.broadcasted_iota(jnp.int32, (160, 128), 0)
    qi = lax.broadcasted_iota(jnp.int32, (160, 128), 1)
    seg_p = win4[r, 32 * b : 32 * b + 160, 0:1]
    far = (jnp.abs(4 * pp - REACH - qi) <= REACH) & (seg_p == seg_q)
    return jnp.where(near, 0.0, -1e30), jnp.where(far, 0.0, -1e30)


def fill_masks(winc, win4, winr, bias):
    for r in range(2):
        for b in range(4):
            near, far = mask_block(winc, win4, winr, r, b)
            bias[r * 4 + b, 0:256] = near
            bias[r * 4 + b, 256:416] = far


def head_lanes(h):
    return (
        pl.ds(pl.multiple_of(h * 128, 128), 128),
        pl.ds(pl.multiple_of(768 + h * 128, 128), 128),
    )


def attend(q, kv, pe, bias, att, lse, r, h):
    kl, vl = head_lanes(h)
    for b in range(4):
        n, f, i = slice(b * 128, b * 128 + 256), slice(b * 32, b * 32 + 160), slice(b * 128, b * 128 + 128)
        e, rt, lse[r * 6 + h, b : b + 1] = softmax_block(
            pair_rows(q[r, i, kl]), kv[r, n, kl], pe[r, f, kl], bias[r * 4 + b]
        )
        low = (e * rt).astype(BF)
        values = jnp.concatenate([kv[r, n, vl], pe[r, f, vl]], axis=0)
        att[r, i, kl] = pair_out(dg(values, low, TN)).astype(BF)


def attend_back(q, kv, pe, bias, lse, g, gext, dkv, dpe, r, h):
    kl, vl = head_lanes(h)
    for part in (h, 6 + h):
        dkv[r, part] = jnp.zeros((640, 128), F32)
        dpe[r, part] = jnp.zeros((256, 128), F32)
    for b in range(4):
        n, f, i = slice(b * 128, b * 128 + 256), slice(b * 32, b * 32 + 160), slice(b * 128, b * 128 + 128)
        q2, g2 = pair_rows(q[r, i, kl]), pair_rows(g[r * 512 + b * 128 : r * 512 + b * 128 + 128, kl])
        kn, vn, kf, vf = kv[r, n, kl], kv[r, n, vl], pe[r, f, kl], pe[r, f, vl]
        st = jnp.concatenate([dg(kn, q2, NT), dg(kf, q2, NT)], axis=0) - lse[r * 6 + h, b : b + 1]
        p = jnp.exp(st + jnp.concatenate([bias[r * 4 + b], bias[r * 4 + b]], axis=1))
        dp = jnp.concatenate([dg(vn, g2, NT), dg(vf, g2, NT)], axis=0)
        delta = jnp.sum(p * dp, axis=0, keepdims=True)
        ds = (p * (dp - delta)).astype(BF)
        low = p.astype(BF)
        dv, dk = dg(low, g2, NN), dg(ds, q2, NN)
        dkv[r, h, n] += dk[:256]
        dkv[r, 6 + h, n] += dv[:256]
        dpe[r, h, f] += dk[256:]
        dpe[r, 6 + h, f] += dv[256:]
        dqt = dg(jnp.concatenate([kn, kf], axis=0), ds, TN)
        gext[r * 640 + 64 + b * 128 : r * 640 + 192 + b * 128, kl] = (pair_out(dqt) * HEAD**-0.5).astype(BF)


def norm_parts(v):
    mean = jnp.mean(v, axis=-1, keepdims=True)
    cen = v - mean
    var = jnp.mean(cen * cen, axis=-1, keepdims=True)
    rs = lax.rsqrt(var + 1e-05)
    return cen * rs, rs


def pack_own(grab, put):
    for name in ("qkv", "out", "up", "down"):
        half = units(name) // 2
        for u in range(units(name)):
            k, lo = spot(name, u)
            put(k, lo, grab(name, 0, 16, u))
        for u in range(half):
            k, lo = spot(name, units(name) + u)
            put(k, lo, jnp.concatenate([grab(name, 16, 24, u), grab(name, 16, 24, u + half)], axis=0))


def hidden_place(n):
    half, r = divmod(n, 1536)
    return (r // 256) * 512 + half * 256 + r % 256


def unpack(name, got, dst):
    half = units(name) // 2

    def pair(p, carry):
        rows = pl.ds(pl.multiple_of(48 * p, 16), 48)
        for u in range(units(name)):
            k, lo = spot(name, u)
            kt, lt = spot(name, units(name) + u % half)
            cut = slice(0, 8) if u < half else slice(8, 16)
            hidden = name in ("up", "down")
            for i in range(0, UNIT, 128) if hidden else (0,):
                n = 128 if hidden else UNIT
                to = hidden_place(u * UNIT + i) if hidden else u * UNIT
                parts = []
                for j in (0, 1):
                    parts.append(got[k, 2 * p + j, :, lo + i : lo + i + n])
                    parts.append(got[kt, 2 * p + j, :, lt + i : lt + i + n][cut])
                dst[rows, to : to + n] = jnp.concatenate(parts, axis=0)
        return carry

    lax.fori_loop(0, 16, pair, 0)


def spread_small(got, taps, gains):
    lane = lax.broadcasted_iota(jnp.int32, (16, 128), 1)

    def place(width, tiles):
        acc = [jnp.zeros((16, 128), F32) for _ in range(tiles)]
        for s in range(32):
            at, off = divmod(width * s, 128)
            v = jnp.where(lane < width, got[0, s, :, CLS:WIDE].astype(F32), 0.0)
            v = pltpu.roll(v, off, 1) if off else v
            acc[at] = acc[at] + jnp.where(lane >= off, v, 0.0)
            if off + width > 128:
                acc[at + 1] = acc[at + 1] + jnp.where(lane < off, v, 0.0)
        return acc

    for i, v in enumerate(place(48, 12)):
        taps[:, i * 128 : (i + 1) * 128] = v
    for i, v in enumerate(place(24, 6)):
        gains[:, i * 128 : (i + 1) * 128] = v


def front_kernel(
    tok, winc, win4, winr, wq, wo, wu, wd, small,
    o_wq, o_wo, o_wu, o_wd, o_taps, o_gains, o_h1, o_q, o_kv, o_pe, o_att, o_bias, o_lse,
    G, Wq, Wo, Wu, Wd, taps, gains, xe, h1, q, kv, pe, att, bias, lse, chunk,
    send_x, send_y, send_d, send_z, send_g, recv, hsend, hrecv, local,
):
    me = where_am_i()
    c, s, z, col = me["c"], me["s"], me["z"], me["col"]
    mine = c * 16 + s
    last = lax.axis_size("seq") - 1
    has_left, has_right = s > 0, s < last

    def cols(k):
        return WIDE if isinstance(k, int) and k == 0 else CLS

    def hop(k, slot, to, sem):
        part = G.at[k, slot, :, pl.ds(0, cols(k))]
        return pltpu.make_async_remote_copy(
            src_ref=part, dst_ref=part, send_sem=sem, recv_sem=recv.at[k, slot],
            device_id=to, device_id_type=MESH,
        )

    def to_x(k, at):
        return hop(k, c * 16 + at, me["px"], send_x.at[k, at])

    def to_y(k, at):
        return hop(k, c * 16 + at, me["py"], send_y.at[k, at])

    def to_d(k, at):
        return hop(k, c * 16 + at, me["pd"], send_d.at[k, at])

    def to_z(k, j):
        return hop(k, mine, (c, lax.rem(z + j, 4) * 4 + col), send_z.at[k, j - 1])

    def by_y(k, zz):
        return zz != 3

    def to_g(k, zz):
        over_y = by_y(k, zz)
        at = zz * 4 + jnp.where(over_y, me["colx"], me["coly"])
        to = (c, z * 4 + jnp.where(over_y, me["coly"], me["colx"]))
        return hop(k, c * 16 + at, to, send_g.at[k, zz])

    def got(k, slot):
        hop(k, slot, me["px"], send_x.at[k, 0]).wait_recv()

    def own(k):
        for j in (1, 2, 3):
            to_z(k, j).start()
        to_x(k, s).start()
        to_y(k, s).start()
        to_d(k, s).start()

    def column(k, j):
        at = lax.rem(z + j, 4) * 4 + col
        got(k, c * 16 + at)
        to_x(k, at).start()
        to_y(k, at).start()
        to_d(k, at).start()

    def plane(k, j):
        zz = lax.rem(z + j, 4)
        got(k, c * 16 + zz * 4 + me["colx"])
        to_d(k, zz * 4 + me["colx"]).start()
        got(k, c * 16 + zz * 4 + me["coly"])
        to_d(k, zz * 4 + me["coly"]).start()
        to_g(k, zz).start()

    def diag(k, j):
        at = lax.rem(z + j, 4) * 4 + me["cold"]
        got(k, c * 16 + at)
        to_d(k, at).start()

    def event(e):
        k, i = e // 11 + 1, lax.rem(e, 11)

        @pl.when(i < 4)
        def _():
            plane(k, i)

        @pl.when((i >= 4) & (i < 7) & (k < 3))
        def _():
            column(k + 1, i - 3)

        @pl.when(i >= 7)
        def _():
            diag(k, i - 7)

    def halo_tok(r, right):
        src = tok.at[r, pl.ds(448 if right else 0, 64)]
        dst = xe.at[r, pl.ds(0 if right else 576, 64)]
        i = r * 2 + int(right)
        return pltpu.make_async_remote_copy(
            src_ref=src, dst_ref=dst, send_sem=hsend.at[i], recv_sem=hrecv.at[i],
            device_id=(c, s + 1 if right else s - 1), device_id_type=MESH,
        )

    def halo_pool(r, right):
        src = pe.at[r, pl.ds(128 if right else 64, 64)]
        dst = pe.at[r, pl.ds(0 if right else 192, 64)]
        i = 4 + r * 2 + int(right)
        return pltpu.make_async_remote_copy(
            src_ref=src, dst_ref=dst, send_sem=hsend.at[i], recv_sem=hrecv.at[i],
            device_id=(c, s + 1 if right else s - 1), device_id_type=MESH,
        )

    def both(make, r, act):
        @pl.when(has_right)
        def _():
            act(make(r, True), True)

        @pl.when(has_left)
        def _():
            act(make(r, False), False)

    def arrived(make, r):
        @pl.when(has_left)
        def _():
            make(r, True).wait_recv()

        @pl.when(has_right)
        def _():
            make(r, False).wait_recv()

    load = [pltpu.make_async_copy(tok.at[r], xe.at[r, pl.ds(64, 512)], local.at[r]) for r in range(2)]
    for copy in load:
        copy.start()
    shares = {"qkv": wq, "out": wo, "up": wu, "down": wd}

    def grab(name, a, b, u):
        return shares[name][a:b, u * UNIT : (u + 1) * UNIT]

    def put(k, lo, v):
        G[k, mine, :, lo : lo + UNIT] = v

    pack_own(grab, put)
    G[0, mine, :, CLS:WIDE] = small[...]

    @pl.when(jnp.logical_not(has_left))
    def _():
        for r in range(2):
            xe[r, 0:64] = jnp.zeros((64, 768), BF)
            pe[r, 0:64] = jnp.zeros((64, 1536), BF)

    @pl.when(jnp.logical_not(has_right))
    def _():
        for r in range(2):
            xe[r, 576:640] = jnp.zeros((64, 768), BF)
            pe[r, 192:256] = jnp.zeros((64, 1536), BF)

    lse[...] = jnp.zeros((12, 8, 256), F32)
    greet(me, True)
    own(0)
    for r in range(2):
        both(halo_tok, r, lambda copy, right: copy.start())
    own(1)
    own(2)
    fill_masks(winc, win4, winr, bias)
    for j in (1, 2, 3):
        column(0, j)
    for j in range(4):
        plane(0, j)
    own(3)
    for j in (1, 2, 3):
        column(1, j)
    for j in range(4):
        diag(0, j)

    def other(k):
        def body(i, carry):
            got(k, (1 - c) * 16 + i)
            return carry

        lax.fori_loop(0, 16, body, 0)

    other(0)
    unpack("qkv", G, Wq)
    spread_small(G, taps, gains)
    outs = [
        pltpu.make_async_copy(a, b, local.at[2 + i])
        for i, (a, b) in enumerate(
            [(Wq, o_wq), (taps, o_taps), (gains, o_gains), (h1, o_h1), (q, o_q), (kv, o_kv), (pe, o_pe),
             (att, o_att), (bias, o_bias), (Wo, o_wo), (Wu, o_wu), (Wd, o_wd), (lse, o_lse)]
        )
    ]
    for i in (0, 1, 2, 8):
        outs[i].start()
    for copy in load:
        copy.wait()
    for r in range(2):
        arrived(halo_tok, r)

    for r in range(2):
        def norm_rows(i, carry):
            rows = pl.ds(pl.multiple_of(i * 128, 128), 128)
            n, _ = norm_parts(xe[r, rows].astype(F32))
            h1[r, rows] = (n * gains[5:6] + gains[6:7]).astype(BF)
            return carry

        lax.fori_loop(0, 5, norm_rows, 0)
    outs[3].start()

    for r in range(2):
        def queries(j, carry):
            lanes = pl.ds(pl.multiple_of(j * 256, 256), 256)
            v = dg(h1[r, 64:576], Wq[:, lanes], NN)
            q[r, :, lanes] = v.astype(BF) * jnp.asarray(HEAD**-0.5, BF)
            return carry

        lax.fori_loop(0, 3, queries, 0)
        anchor = win4[r, 64:192, 0:1]
        same = [
            (win4[r, a : a + 128, f : f + 1] == anchor).astype(F32)
            for a, f in ((63, 2), (63, 3), (64, 0), (64, 1), (64, 2))
        ]

        def keys(j, carry):
            event(r * 6 + j)
            lanes = pl.ds(pl.multiple_of(j * 128, 128), 128)
            from_lanes = pl.ds(pl.multiple_of(768 + j * 256, 256), 256)
            to_lanes = pl.ds(pl.multiple_of(j * 256, 256), 256)
            v = dg(h1[r], Wq[:, from_lanes], NN).astype(BF)
            kv[r, :, to_lanes] = v
            chunk[0] = v[:, :128].astype(F32)
            chunk[1] = v[:, 128:].astype(F32)
            for half in range(2):
                hl = pl.ds(pl.multiple_of(j * 256 + half * 128, 128), 128)
                acc = jnp.zeros((128, 128), F32)
                for t in range(5):
                    acc = acc + taps[t : t + 1, hl] * chunk[half, pl.ds(62 + t, 128, stride=4), :] * same[t]
                pe[r, 64:192, hl] = acc.astype(BF)
            return carry

        lax.fori_loop(0, 6, keys, 0)
        both(halo_pool, r, lambda copy, right: copy.start())
    outs[4].start()
    outs[5].start()
    for r in range(2):
        arrived(halo_pool, r)

        def heads_event(h, carry):
            attend(q, kv, pe, bias, att, lse, r, h)
            base = 12 + (r * 6 + h) * 2

            @pl.when(base < 33)
            def _():
                event(base)

            @pl.when(base + 1 < 33)
            def _():
                event(base + 1)

            return carry

        lax.fori_loop(0, 6, heads_event, 0)
    outs[6].start()
    outs[7].start()
    outs[12].start()
    for k in (1, 2, 3):
        other(k)
    for i, (name, dst) in enumerate((("out", Wo), ("up", Wu), ("down", Wd))):
        unpack(name, G, dst)
        outs[9 + i].start()
    for r in range(2):
        both(halo_tok, r, lambda copy, right: copy.wait_send())
        both(halo_pool, r, lambda copy, right: copy.wait_send())
    for k in range(4):
        def done(i, carry):
            to_x(k, i * 4 + col).wait_send()
            to_y(k, i * 4 + col).wait_send()
            to_g(k, i).wait_send()
            for j in range(4):
                to_d(k, i * 4 + j).wait_send()
            return carry

        lax.fori_loop(0, 4, done, 0)
        for j in (1, 2, 3):
            to_z(k, j).wait_send()
    for copy in outs:
        copy.wait()


def front(tok, winc, win4, winr, wq, wo, wu, wd, small):
    sds = jax.ShapeDtypeStruct
    shapes = [
        ((768, 2304), BF), ((768, 768), BF), ((768, 3072), BF), ((768, 3072), BF),
        ((16, 1536), F32), ((16, 768), F32),
        ((2, 640, 768), BF), ((2, 512, 768), BF), ((2, 640, 1536), BF), ((2, 256, 1536), BF),
        ((2, 512, 768), BF), ((8, 416, 128), F32), ((12, 8, 256), F32),
    ]
    scratch = [pltpu.VMEM((4, 32, 16, WIDE), BF)]
    scratch += [pltpu.VMEM(sh, dt) for sh, dt in shapes[:6]]
    scratch += [pltpu.VMEM((2, 640, 768), BF)]
    scratch += [pltpu.VMEM(sh, dt) for sh, dt in shapes[6:]]
    scratch += [pltpu.VMEM((2, 640, 128), F32)]
    dma = pltpu.SemaphoreType.DMA
    scratch += [dma((4, 16)), dma((4, 16)), dma((4, 16)), dma((4, 3)), dma((4, 4)), dma((4, 32)), dma((8,)), dma((8,)), dma((15,))]
    return pl.pallas_call(
        front_kernel,
        out_shape=[sds(sh, dt) for sh, dt in shapes],
        in_specs=[ANY] + [VM] * 8,
        out_specs=[ANY] * len(shapes),
        scratch_shapes=scratch,
        compiler_params=pltpu.CompilerParams(collective_id=0, has_side_effects=True, vmem_limit_bytes=VMEM_LIMIT),
    )(tok, winc, win4, winr, wq, wo, wu, wd, small)


def windows(segments):
    block = 512
    padded = jnp.pad(segments, ((0, 0), (REACH, REACH)), constant_values=-1)
    win = lax.dynamic_slice_in_dim(padded, lax.axis_index("seq") * block, block + 2 * REACH, 1)
    return win[:, :, None], win.reshape(2, 256, 4), win


def small_share(pool_taps, ln1_gain, ln1_bias, ln2_gain, ln2_bias):
    rows = jnp.stack([ln1_gain, ln1_bias, ln2_gain, ln2_bias])
    return jnp.concatenate(
        [jnp.pad(pool_taps, ((0, 0), (0, 80))), jnp.pad(rows, ((0, 7), (0, 104)))], axis=0
    )


def gelu_both(u):
    a, b = 0.7978845608028654, 0.044715
    sq = u * u
    t = jnp.tanh(a * u * (1.0 + b * sq))
    half = 0.5 + 0.5 * t
    grad = half + 0.5 * u * (1.0 - t * t) * (a + (3.0 * a * b) * sq)
    return u * half, grad


def pack_pair(lo, hi):
    return jnp.concatenate([lo, hi], axis=0).astype(BF)


def pick_small(tg, lg, put):
    lane = lax.broadcasted_iota(jnp.int32, (16, 128), 1)

    def part(src, width, s):
        at, off = divmod(width * s, 128)
        v = src[:, at * 128 : at * 128 + 128]
        v = pltpu.roll(v, 128 - off, 1) if off else v
        if off + width > 128:
            w = pltpu.roll(src[:, at * 128 + 128 : at * 128 + 256], 128 - off, 1)
            v = jnp.where(lane < 128 - off, v, w)
        return jnp.where(lane < width, v, 0.0)

    for s in range(32):
        put(s, (part(tg, 48, s) + part(lg, 24, s)).astype(BF))


def back_kernel(
    tok_in, att_in, dy_in, wo_in, wu_in, wd_in,
    q_in, kv_in, pe_in, bias_in, h1_in, wq_in, taps, gains, win4, lse,
    o_out, o_gmid, o_in, o_wq, o_wo, o_wu, o_wd, o_small,
    Sf, So, Ss, Rf, Ro, Rq, Rs, gatt, pstage, precv, hstage, hrecv, tg, lg,
    send, recv, psend, prsem, local,
):
    me = where_am_i()
    c, s, z, col = me["c"], me["s"], me["z"], me["col"]
    has_left, has_right = s > 0, s < lax.axis_size("seq") - 1

    def copy(i, a, b):
        return pltpu.make_async_copy(a, b, local.at[i])

    late = []

    def cls(k):
        if k < 3:
            return Sf.at[k, pl.ds(c * 16, 16)], Rf.at[k]
        if k == 3:
            return So.at[pl.ds(c * 16, 16)], Ro
        if k < 7:
            return late[0].at[k - 4, pl.ds(c * 16, 16)], Rq.at[k - 4]
        return Ss.at[pl.ds(c * 16, 16)], Rs

    def other(k):
        start = (1 - c) * 16
        if k < 3:
            return Sf.at[k, pl.ds(start, 16)]
        if k == 3 or k == 7:
            return (So if k == 3 else Ss).at[pl.ds(start, 16)]
        return late[0].at[k - 4, pl.ds(start, 16)]

    def remote(k, src, slot, i, to):
        return pltpu.make_async_remote_copy(
            src_ref=src, dst_ref=slot, send_sem=send.at[k, i], recv_sem=recv.at[k, i],
            device_id=to, device_id_type=MESH,
        )

    def swap(k):
        return remote(k, other(k), cls(k)[1].at[pl.ds(0, 16)], 0, me["pd"])

    def step_g(k, zz):
        S, R = cls(k)
        to = me["px"] if zz % 2 == 0 else me["py"]
        return remote(k, S.at[zz * 4 + me["cold"]], R.at[16 + zz], 1 + zz, to)

    def step_x(k, zz):
        S, R = cls(k)
        return remote(k, S.at[zz * 4 + me["colx"]], R.at[20 + zz], 5 + zz, me["px"])

    def step_y(k, zz):
        S, R = cls(k)
        return remote(k, S.at[zz * 4 + me["coly"]], R.at[24 + zz], 9 + zz, me["py"])

    def step_z(k, j):
        S, R = cls(k)
        zz = lax.rem(z + j, 4)
        return remote(k, S.at[zz * 4 + col], R.at[27 + j], 12 + j, (c, zz * 4 + col))

    def add(k, at, slots):
        S, R = cls(k)
        v = S[at].astype(F32) + R[at].astype(F32)
        for slot in slots:
            v = v + R[slot].astype(F32)
        return v

    def begin(k):
        swap(k).start()

    def do_g(k, zz):
        if zz == 0:
            swap(k).wait_recv()
        at = zz * 4 + me["cold"]
        cls(k)[0][at] = add(k, at, []).astype(BF)
        step_g(k, zz).start()

    def do_p(k, zz):
        step_g(k, zz).wait_recv()
        even = zz % 2 == 0
        for at, step, has in ((zz * 4 + me["colx"], step_x, not even), (zz * 4 + me["coly"], step_y, even)):
            cls(k)[0][at] = add(k, at, [16 + zz] if has else []).astype(BF)
            step(k, zz).start()

    def arrive(k, zz):
        S, R = cls(k)
        remote(k, S.at[0], R.at[20 + zz], 5 + zz, me["px"]).wait_recv()
        remote(k, S.at[0], R.at[24 + zz], 9 + zz, me["py"]).wait_recv()

    def do_c(k, j):
        zz = lax.rem(z + j, 4)
        arrive(k, zz)
        at = zz * 4 + col
        cls(k)[0][at] = add(k, at, [20 + zz, 24 + zz]).astype(BF)
        step_z(k, j).start()

    def total(k):
        arrive(k, z)
        for j in (1, 2, 3):
            step_z(k, j).wait_recv()
        return add(k, z * 4 + col, [20 + z, 24 + z, 28, 29, 30])

    def drain(k):
        swap(k).wait_send()
        for zz in range(4):
            step_g(k, zz).wait_send()
            step_x(k, zz).wait_send()
            step_y(k, zz).wait_send()
        for j in (1, 2, 3):
            step_z(k, j).wait_send()

    def finish(k):
        v = total(k)
        if k < 3:
            for i in range(2):
                for ref, base in ((o_wu, i * 1536), (o_wd, i * 1536 + 768)):
                    lo, hi = (2 * k + i) * 256, 1536 + (2 * k + i) * 256
                    ref[0:16, lo : lo + 256] = v[:, base : base + 256]
                    ref[0:16, hi : hi + 256] = v[:, base + 256 : base + 512]
                    ref[16:24, lo : lo + 256] = v[0:8, base + 512 : base + 768]
                    ref[16:24, hi : hi + 256] = v[8:16, base + 512 : base + 768]
        else:
            ref, at = (o_wo, 0) if k == 3 else (o_wq, (k - 4) * 768)
            ref[0:16, at : at + 768] = v[:, 0:768]
            ref[16:24, at : at + 384] = v[0:8, 768:1152]
            ref[16:24, at + 384 : at + 768] = v[8:16, 768:1152]
        drain(k)

    def to_owner(d):
        owner = lax.rem(s + d, 16)
        return remote(7, Ss.at[c * 16 + owner], Rs.at[16 + s], d, (c, owner))

    def from_peer(d):
        slot = 16 + lax.rem(s + 16 - d, 16)
        return remote(7, Ss.at[0], Rs.at[slot], d, me["px"])

    def small_out():
        swap(7).wait_recv()
        for i in range(16):
            Ss[c * 16 + i] = (Ss[c * 16 + i].astype(F32) + Rs[i].astype(F32)).astype(BF)
        for d in range(1, 16):
            to_owner(d).start()

    def small_in():
        v = Ss[c * 16 + s].astype(F32)
        for d in range(1, 16):
            from_peer(d).wait_recv()
            v = v + Rs[16 + lax.rem(s + 16 - d, 16)].astype(F32)
        o_small[...] = v
        swap(7).wait_send()
        for d in range(1, 16):
            to_owner(d).wait_send()

    def halo(src, dst, r, right, h):
        side = int(right)
        i = 24 + r * 2 + side if h is None else (r * 2 + side) * 6 + h
        at = (r, side) if h is None else (r, side, h)
        return pltpu.make_async_remote_copy(
            src_ref=src.at[at], dst_ref=dst.at[at], send_sem=psend.at[i], recv_sem=prsem.at[i],
            device_id=(c, s + 1 if right else s - 1), device_id_type=MESH,
        )

    def both(src, dst, r, h, act):
        @pl.when(has_right)
        def _():
            act(halo(src, dst, r, True, h))

        @pl.when(has_left)
        def _():
            act(halo(src, dst, r, False, h))

    def arrived(src, dst, r, h):
        @pl.when(has_left)
        def _():
            halo(src, dst, r, True, h).wait_recv()

        @pl.when(has_right)
        def _():
            halo(src, dst, r, False, h).wait_recv()

    @pl.when(jnp.logical_not(has_left))
    def _():
        precv[:, 1] = jnp.zeros((2, 6, 2, 64, 128), BF)
        hrecv[:, 1] = jnp.zeros((2, 64, 768), BF)

    @pl.when(jnp.logical_not(has_right))
    def _():
        precv[:, 0] = jnp.zeros((2, 6, 2, 64, 128), BF)
        hrecv[:, 0] = jnp.zeros((2, 64, 768), BF)

    tg[...] = jnp.zeros((16, 1536), F32)
    lg[...] = jnp.zeros((16, 768), F32)
    greet_all(me)

    def perform(todo):
        for fn, k in todo:
            if fn is begin or fn is finish:
                fn(k)
            else:
                for j in (1, 2, 3) if fn is do_c else (0, 1, 2, 3):
                    fn(k, j)

    def run(plan, at):
        for i, todo in plan.items():
            @pl.when(at == i)
            def _():
                perform(todo)

    def feed_forward(Tok, Att, Dy, Wo, Wu, Wd, mid, h2, DyT, H2T, y, gh2, act, gu):
        loads = [
            copy(i, a, b)
            for i, (a, b) in enumerate(
                [(tok_in, Tok), (att_in, Att), (wo_in, Wo), (dy_in, Dy), (wu_in, Wu), (wd_in, Wd)]
            )
        ]
        for ld in loads:
            ld.start()
        y[...] = jnp.zeros((1024, 768), F32)
        gh2[...] = jnp.zeros((1024, 768), F32)
        for ld in loads[:3]:
            ld.wait()
        mid[...] = dg(Att[...], Wo[...], NN)

        def first(i, carry):
            rows = pl.ds(pl.multiple_of(i * 128, 128), 128)
            v = Tok[rows].astype(F32) + mid[rows]
            mid[rows] = v
            n, _ = norm_parts(v)
            h2[rows] = (n * gains[7:8] + gains[8:9]).astype(BF)
            return carry

        lax.fori_loop(0, 8, first, 0)
        loads[3].wait()

        def flip(i, carry):
            rows = pl.ds(pl.multiple_of(i * 128, 128), 128)
            for j in range(3):
                cols = slice(j * 256, j * 256 + 256)
                DyT[cols, rows] = Dy[rows, cols].T
                H2T[cols, rows] = h2[rows, cols].T
            return carry

        lax.fori_loop(0, 8, flip, 0)
        loads[4].wait()
        loads[5].wait()
        plan = {
            5: [(begin, 0)], 7: [(do_g, 0)], 11: [(do_p, 0), (begin, 1)], 13: [(do_g, 1)],
            17: [(do_c, 0), (begin, 2)],
        }

        def chunk(j, carry):
            lanes = [pl.ds(pl.multiple_of(j * 512 + h * 256, 256), 256) for h in range(2)]
            whole = pl.ds(pl.multiple_of(j * 512, 512), 512)
            for m in range(2):
                rows = slice(m * 512, m * 512 + 512)
                for h in range(2):
                    u = dg(h2[rows], Wu[:, lanes[h]], NN)
                    ga = dg(Dy[rows], Wd[:, lanes[h]], NN)
                    a, da = gelu_both(u)
                    act[rows, h * 256 : h * 256 + 256] = a.astype(BF)
                    gu[rows, h * 256 : h * 256 + 256] = (ga * da).astype(BF)
            run(plan, j * 3)
            y[...] += dg(act[...], Wd[:, whole], NT)
            gh2[...] += dg(gu[...], Wu[:, whole], NT)
            run(plan, j * 3 + 1)
            for which, (left, right) in enumerate(((H2T, gu), (DyT, act))):
                base = lax.rem(j, 2) * 1536 + which * 768
                at = [pl.ds(pl.multiple_of(base + i * 256, 256), 256) for i in range(3)]
                dws = dg(left[...], right[...], NN)
                for i in range(32):
                    head, tail = dws[i * 24 : i * 24 + 16].astype(BF), dws[i * 24 + 16 : i * 24 + 24]
                    Sf[j // 2, i, :, at[0]] = head[:, 0:256]
                    Sf[j // 2, i, :, at[1]] = head[:, 256:512]
                    Sf[j // 2, i, :, at[2]] = pack_pair(tail[:, 0:256], tail[:, 256:512])
            run(plan, j * 3 + 2)
            return carry

        lax.fori_loop(0, 6, chunk, 0)

        def last(i, carry):
            rows = pl.ds(pl.multiple_of(i * 128, 128), 128)
            v = mid[rows]
            Tok[rows] = (v + y[rows]).astype(BF)
            n, rs = norm_parts(v)
            g = gh2[rows]
            e = g * gains[7:8]
            gm = Dy[rows].astype(F32) + rs * (
                e - jnp.mean(e, axis=-1, keepdims=True) - n * jnp.mean(e * n, axis=-1, keepdims=True)
            )
            y[rows] = gm
            h2[rows] = gm.astype(BF)
            a, b = carry
            return a + jnp.sum((g * n).reshape(16, 8, 768), axis=0), b + jnp.sum(g.reshape(16, 8, 768), axis=0)

        zero = jnp.zeros((8, 768), F32)
        a, b = lax.fori_loop(0, 8, last, (zero, zero))
        perform([(do_p, 1)])
        lg[7:8] = jnp.sum(a, axis=0, keepdims=True)
        lg[8:9] = jnp.sum(b, axis=0, keepdims=True)
        store = [copy(6, Tok, o_out), copy(7, y, o_gmid)]
        for st in store:
            st.start()

        def flip_att(i, carry):
            rows = pl.ds(pl.multiple_of(i * 128, 128), 128)
            for j in range(3):
                DyT[j * 256 : j * 256 + 256, rows] = Att[rows, j * 256 : j * 256 + 256].T
            return carry

        lax.fori_loop(0, 8, flip_att, 0)
        gatt[...] = dg(h2[...], Wo[...], NT).astype(BF)
        dws = dg(DyT[...], h2[...], NN)
        for i in range(32):
            tail = dws[i * 24 + 16 : i * 24 + 24]
            So[i, :, 0:768] = dws[i * 24 : i * 24 + 16].astype(BF)
            So[i, :, 768:1152] = pack_pair(tail[:, 0:384], tail[:, 384:768])
        begin(3)
        perform([(do_g, 2)])
        for st in store:
            st.wait()

    def weight_grad(gext, h1t, Sq, j):
        dws = dg(h1t[...], gext[:, j * 768 : j * 768 + 768], NN)
        for i in range(32):
            tail = dws[i * 24 + 16 : i * 24 + 24]
            Sq[j, i, :, 0:768] = dws[i * 24 : i * 24 + 16].astype(BF)
            Sq[j, i, :, 768:1152] = pack_pair(tail[:, 0:384], tail[:, 384:768])
        begin(4 + j)

    def attention(gext, h1, h1t, Sq, q, kv, pe, bias, dkv, dpe, chunk):
        loads = [
            copy(4 + i, a, b)
            for i, (a, b) in enumerate([(q_in, q), (kv_in, kv), (pe_in, pe), (bias_in, bias), (h1_in, h1)])
        ]
        for ld in loads:
            ld.start()
        for r in range(2):
            gext[r * 640 : r * 640 + 64, 0:768] = jnp.zeros((64, 768), BF)
            gext[r * 640 + 576 : r * 640 + 640, 0:768] = jnp.zeros((64, 768), BF)
        for ld in loads[:4]:
            ld.wait()
        plans = (
            {0: [(do_c, 1)], 2: [(do_p, 2)], 3: [(do_g, 3)], 5: [(do_p, 3)]},
            {2: [(do_c, 2)], 3: [(do_c, 3)]},
        )
        for r in range(2):
            def heads(h, carry):
                attend_back(q, kv, pe, bias, lse, gatt, gext, dkv, dpe, r, h)
                for part in range(2):
                    pstage[r, 0, h, part] = dpe[r, part * 6 + h, 0:64].astype(BF)
                    pstage[r, 1, h, part] = dpe[r, part * 6 + h, 192:256].astype(BF)
                both(pstage, precv, r, h, lambda cp: cp.start())
                run(plans[r], h)
                return carry

            lax.fori_loop(0, 6, heads, 0)

        loads[4].wait()
        for r in range(2):
            def flip(i, carry):
                rows = pl.ds(pl.multiple_of(i * 128, 128), 128)
                for j in range(3):
                    to = pl.ds(pl.multiple_of(r * 640 + i * 128, 128), 128)
                    h1t[j * 256 : j * 256 + 256, to] = h1[r, rows, j * 256 : j * 256 + 256].T
                return carry

            lax.fori_loop(0, 5, flip, 0)
        weight_grad(gext, h1t, Sq, 0)
        for r in range(2):
            anchor = win4[r, 64:192, 0:1]
            same = [
                (win4[r, a : a + 128, f : f + 1] == anchor).astype(F32)
                for a, f in ((63, 2), (63, 3), (64, 0), (64, 1), (64, 2))
            ]

            def pool_back(t, carry):
                lanes = pl.ds(pl.multiple_of(t * 128, 128), 128)
                h, part = lax.rem(t, 6), t // 6

                @pl.when(t < 6)
                def _():
                    arrived(pstage, precv, r, h)

                low = dpe[r, t, 64:128] + precv[r, 1, h, part].astype(F32)
                high = dpe[r, t, 128:192] + precv[r, 0, h, part].astype(F32)
                gp = jnp.concatenate([low, high], axis=0)
                chunk[...] = kv[r, :, lanes].astype(F32)
                for i in range(5):
                    at = pl.ds(62 + i, 128, stride=4)
                    gm = gp * same[i]
                    tg[i : i + 1, lanes] += jnp.sum(gm * chunk[at, :], axis=0, keepdims=True)
                    dkv[r, t, at, :] += gm * taps[i : i + 1, lanes]
                out_lanes = pl.ds(pl.multiple_of(768 + t * 128, 128), 128)
                gext[r * 640 : r * 640 + 640, out_lanes] = dkv[r, t].astype(BF)
                return carry

            lax.fori_loop(0, 12, pool_back, 0)
        perform([(do_g, 4)])

    def projection(gext, h1t, Sq, wq, tok, gmid, gh):
        loads = [
            copy(9 + i, a, b) for i, (a, b) in enumerate([(wq_in, wq), (tok_in, tok), (o_gmid, gmid)])
        ]
        for ld in loads:
            ld.start()
        weight_grad(gext, h1t, Sq, 1)
        weight_grad(gext, h1t, Sq, 2)
        perform([(do_p, 4), (do_g, 5)])
        for ld in loads:
            ld.wait()
        for r in range(2):
            gh[r] = dg(gext[r * 640 : r * 640 + 640], wq[...], NT)
            hstage[r, 0] = gh[r, 0:64].astype(BF)
            hstage[r, 1] = gh[r, 576:640].astype(BF)
            both(hstage, hrecv, r, None, lambda cp: cp.start())
            perform(([(do_g, 6), (do_p, 5)], [(do_p, 6), (do_c, 4)])[r])

        def rows_norm(r, i, carry):
            rows = pl.ds(pl.multiple_of(r * 512 + i * 128, 128), 128)
            n, rs = norm_parts(tok[rows].astype(F32))
            g = gh[r, pl.ds(pl.multiple_of(i * 128 + 64, 64), 128)]
            e = g * gains[5:6]
            gmid[rows] += rs * (
                e - jnp.mean(e, axis=-1, keepdims=True) - n * jnp.mean(e * n, axis=-1, keepdims=True)
            )
            a, b = carry
            return a + jnp.sum((g * n).reshape(16, 8, 768), axis=0), b + jnp.sum(g.reshape(16, 8, 768), axis=0)

        def add_halo(r):
            arrived(hstage, hrecv, r, None)
            gh[r, 64:128] += hrecv[r, 1].astype(F32)
            gh[r, 512:576] += hrecv[r, 0].astype(F32)

        zero = jnp.zeros((8, 768), F32)
        add_halo(0)
        acc = lax.fori_loop(0, 4, lambda i, cr: rows_norm(0, i, cr), (zero, zero))
        acc = lax.fori_loop(1, 3, lambda i, cr: rows_norm(1, i, cr), acc)
        add_halo(1)
        acc = lax.fori_loop(0, 2, lambda i, cr: rows_norm(1, 3 * i, cr), acc)
        out = copy(13, gmid, o_in)
        out.start()
        lg[5:6] = jnp.sum(acc[0], axis=0, keepdims=True)
        lg[6:7] = jnp.sum(acc[1], axis=0, keepdims=True)

        def put(i, v):
            Ss[i] = v

        pick_small(tg, lg, put)
        begin(7)
        perform([(do_c, 5), (finish, 0)])
        small_out()
        perform([(finish, 1), (finish, 2), (finish, 3), (do_c, 6), (finish, 4), (finish, 5)])
        small_in()
        perform([(finish, 6)])
        out.wait()

    vm = pltpu.VMEM
    tall, wide = (lambda dt: vm((1024, 768), dt)), (lambda dt: vm((768, 1024), dt))
    pl.run_scoped(
        feed_forward,
        tall(BF), tall(BF), tall(BF), vm((768, 768), BF), vm((768, 3072), BF), vm((768, 3072), BF),
        tall(F32), tall(BF), wide(BF), wide(BF), tall(F32), tall(F32), vm((1024, 512), BF), vm((1024, 512), BF),
    )

    def rest(gext, h1, h1t, Sq):
        late.append(Sq)
        pl.run_scoped(
            functools.partial(attention, gext, h1, h1t, Sq),
            vm((2, 512, 768), BF), vm((2, 640, 1536), BF), vm((2, 256, 1536), BF), vm((8, 416, 128), F32),
            vm((2, 12, 640, 128), F32), vm((2, 12, 256, 128), F32), vm((640, 128), F32),
        )
        pl.run_scoped(
            functools.partial(projection, gext, h1t, Sq),
            vm((768, 2304), BF), tall(BF), tall(F32), vm((2, 640, 768), F32),
        )

    pl.run_scoped(
        rest, vm((1280, 2304), BF), vm((2, 640, 768), BF), vm((768, 1280), BF), vm((3, 32, 16, 1152), BF)
    )
    for r in range(2):
        for h in range(6):
            both(pstage, precv, r, h, lambda cp: cp.wait_send())
        both(hstage, hrecv, r, None, lambda cp: cp.wait_send())


def back_part(*args):
    sds = jax.ShapeDtypeStruct
    vm, dma = pltpu.VMEM, pltpu.SemaphoreType.DMA
    return pl.pallas_call(
        back_kernel,
        out_shape=[
            sds((1024, 768), BF), sds((1024, 768), F32), sds((1024, 768), F32),
            sds((24, 2304), F32), sds((24, 768), F32), sds((24, 3072), F32), sds((24, 3072), F32), sds((16, 128), F32),
        ],
        in_specs=[ANY] * 12 + [VM] * 4,
        out_specs=[ANY] * 3 + [VM] * 5,
        scratch_shapes=[
            vm((3, 32, 16, 3072), BF), vm((32, 16, 1152), BF), vm((32, 16, 128), BF),
            vm((3, 31, 16, 3072), BF), vm((31, 16, 1152), BF), vm((3, 31, 16, 1152), BF), vm((32, 16, 128), BF),
            vm((1024, 768), BF),
            vm((2, 2, 6, 2, 64, 128), BF), vm((2, 2, 6, 2, 64, 128), BF), vm((2, 2, 64, 768), BF), vm((2, 2, 64, 768), BF),
            vm((16, 1536), F32), vm((16, 768), F32),
            dma((8, 16)), dma((8, 16)), dma((28,)), dma((28,)), dma((14,)),
        ],
        compiler_params=pltpu.CompilerParams(collective_id=1, has_side_effects=True, vmem_limit_bytes=VMEM_LIMIT),
    )(*args)


def with_halo(x, sides, width):
    for axis, dim in sides:
        size, length = (lax.axis_size(axis), x.shape[dim])
        up = [(i, (i + 1) % size) for i in range(size - 1)]
        down = [(j, i) for i, j in up]
        last = lax.slice_in_dim(x, length - width, length, axis=dim)
        first = lax.slice_in_dim(x, 0, width, axis=dim)
        before = lax.ppermute(last, axis, up)
        after = lax.ppermute(first, axis, down)
        x = jnp.concatenate([before, x, after], axis=dim)
    return x


def layer_norm(inputs, norm_gain, norm_bias):
    middle = jnp.mean(inputs, axis=-1, keepdims=True)
    centred = inputs - middle
    spread = jnp.mean(centred * centred, axis=-1, keepdims=True)
    return centred * lax.rsqrt(spread + 1e-05) * norm_gain + norm_bias


def pool_local(extended, taps_in, seg_window):
    block_rows = extended.shape[0] - 2 * NEAR
    anchors = seg_window[REACH : REACH + block_rows : 4]
    pooled = jnp.zeros((block_rows // 4, extended.shape[1]), jnp.float32)
    for offset in range(5):
        start_row = NEAR - 2 + offset
        picked = extended[start_row : start_row + block_rows : 4]
        seg_start = REACH - 2 + offset
        same_doc = (seg_window[seg_start : seg_start + block_rows : 4] == anchors).astype(
            jnp.float32
        )
        pooled = pooled + taps_in[offset] * picked * same_doc[:, None]
    return pooled


def window_masks(seg_window, block_rows):
    seg_query = seg_window[REACH : REACH + block_rows]
    seg_key = seg_window[REACH - NEAR : REACH + block_rows + NEAR]
    seg_pool = seg_window[0 : block_rows + 2 * REACH : 4]
    q_index = jnp.arange(block_rows, dtype=jnp.int32)
    k_index = jnp.arange(seg_key.shape[0], dtype=jnp.int32)
    p_index = jnp.arange(seg_pool.shape[0], dtype=jnp.int32)
    near_mask = (jnp.abs(q_index[:, None] - k_index[None, :] + NEAR) <= NEAR) & (
        seg_query[:, None] == seg_key[None, :]
    )
    far_mask = (jnp.abs(4 * p_index[None, :] - REACH - q_index[:, None]) <= REACH) & (
        seg_query[:, None] == seg_pool[None, :]
    )
    return (near_mask, far_mask)


def scores_of(queries, near_keys, far_keys, near_mask, far_mask):
    score_scale = HEAD ** (-0.5)
    near_scores = (
        jnp.einsum("qhd,khd->hqk", queries, near_keys, preferred_element_type=jnp.float32)
        * score_scale
    )
    far_scores = (
        jnp.einsum("qhd,khd->hqk", queries, far_keys, preferred_element_type=jnp.float32)
        * score_scale
    )
    return (
        jnp.where(near_mask[None], near_scores, -1e30),
        jnp.where(far_mask[None], far_scores, -1e30),
    )


def normalise(near_scores, far_scores, near_mask, far_mask, row_max, row_total):
    near_prob = jnp.where(near_mask[None], jnp.exp(near_scores - row_max), 0.0) / row_total
    far_prob = jnp.where(far_mask[None], jnp.exp(far_scores - row_max), 0.0) / row_total
    return (near_prob, far_prob)


def add_rims(middle_part, rim_values, rim_width):
    extra = middle_part.shape[0] - rim_width
    return (
        middle_part
        + jnp.pad(rim_values[:rim_width], ((0, extra), (0, 0)))
        + jnp.pad(rim_values[-rim_width:], ((extra, 0), (0, 0)))
    )


def shards(
    tokens,
    segments,
    cotangent,
    ln1_gain,
    ln1_bias,
    w_qkv,
    pool_taps,
    w_out,
    ln2_gain,
    ln2_bias,
    w_up,
    w_down,
):
    block_rows = tokens.shape[1]
    model_width = tokens.shape[2]
    pool_half = REACH // 4
    score_scale = HEAD ** (-0.5)
    offset_tokens = lax.axis_index("seq") * block_rows
    outputs = []
    input_grads = []
    summed = None
    for micro_step in range(tokens.shape[0]):
        gathered = (
            lax.all_gather(ln1_gain, ("dp", "seq"), axis=0, tiled=True),
            lax.all_gather(ln1_bias, ("dp", "seq"), axis=0, tiled=True),
            lax.all_gather(w_qkv, ("dp", "seq"), axis=0, tiled=True),
            lax.all_gather(pool_taps, ("dp", "seq"), axis=1, tiled=True),
            lax.all_gather(w_out, ("dp", "seq"), axis=0, tiled=True),
            lax.all_gather(ln2_gain, ("dp", "seq"), axis=0, tiled=True),
            lax.all_gather(ln2_bias, ("dp", "seq"), axis=0, tiled=True),
            lax.all_gather(w_up, ("dp", "seq"), axis=0, tiled=True),
            lax.all_gather(w_down, ("dp", "seq"), axis=1, tiled=True),
        )
        gain_one, bias_one, proj_qkv, taps, proj_out, gain_two, bias_two, proj_up, proj_down = (
            gathered
        )
        seg_row = segments[micro_step]
        seg_padded = jnp.pad(seg_row, (REACH, REACH), constant_values=-1)
        seg_window = lax.dynamic_slice_in_dim(
            seg_padded, offset_tokens, block_rows + 2 * REACH, 0
        )
        near_mask, far_mask = window_masks(seg_window, block_rows)
        inputs = tokens[micro_step].astype(jnp.float32)
        gain_float = gain_one.astype(jnp.float32)
        bias_float = bias_one.astype(jnp.float32)
        gain_second = gain_two.astype(jnp.float32)
        bias_second = bias_two.astype(jnp.float32)
        normed = layer_norm(inputs, gain_float, bias_float).astype(jnp.bfloat16)
        projected = jnp.dot(normed, proj_qkv, preferred_element_type=jnp.float32).astype(
            jnp.bfloat16
        )
        queries = projected[:, :model_width].reshape(block_rows, HEADS, HEAD)
        key_value = projected[:, model_width:]
        extended = with_halo(key_value, (("seq", 0),), NEAR)
        ext_float = extended.astype(jnp.float32)
        taps_float = taps.astype(jnp.float32)
        pooled = pool_local(ext_float, taps_float, seg_window).astype(jnp.bfloat16)
        pool_ext = with_halo(pooled, (("seq", 0),), pool_half)
        near_keys = extended[:, :model_width].reshape(-1, HEADS, HEAD)
        near_values = extended[:, model_width:].reshape(-1, HEADS, HEAD)
        far_keys = pool_ext[:, :model_width].reshape(-1, HEADS, HEAD)
        far_values = pool_ext[:, model_width:].reshape(-1, HEADS, HEAD)
        near_scores, far_scores = scores_of(queries, near_keys, far_keys, near_mask, far_mask)
        row_max = jnp.maximum(
            jnp.max(near_scores, axis=2, keepdims=True), jnp.max(far_scores, axis=2, keepdims=True)
        )
        near_exp = jnp.where(near_mask[None], jnp.exp(near_scores - row_max), 0.0)
        far_exp = jnp.where(far_mask[None], jnp.exp(far_scores - row_max), 0.0)
        row_total = jnp.sum(near_exp, axis=2, keepdims=True) + jnp.sum(
            far_exp, axis=2, keepdims=True
        )
        near_low = (near_exp / row_total).astype(jnp.bfloat16)
        far_low = (far_exp / row_total).astype(jnp.bfloat16)
        mixed_sum = jnp.einsum(
            "hqk,khd->qhd", near_low, near_values, preferred_element_type=jnp.float32
        ) + jnp.einsum("hqk,khd->qhd", far_low, far_values, preferred_element_type=jnp.float32)
        attended = mixed_sum.reshape(block_rows, model_width).astype(jnp.bfloat16)
        branch = jnp.dot(attended, proj_out, preferred_element_type=jnp.float32)
        middle = inputs + branch
        normed_two = layer_norm(middle, gain_second, bias_second).astype(jnp.bfloat16)
        upward = jnp.dot(normed_two, proj_up, preferred_element_type=jnp.float32)
        activated = jax.nn.gelu(upward).astype(jnp.bfloat16)
        result = middle + jnp.dot(activated, proj_down, preferred_element_type=jnp.float32)
        outputs.append(result.astype(jnp.bfloat16))
        regathered = (
            lax.all_gather(ln1_gain, ("dp", "seq"), axis=0, tiled=True),
            lax.all_gather(ln1_bias, ("dp", "seq"), axis=0, tiled=True),
            lax.all_gather(w_qkv, ("dp", "seq"), axis=0, tiled=True),
            lax.all_gather(pool_taps, ("dp", "seq"), axis=1, tiled=True),
            lax.all_gather(w_out, ("dp", "seq"), axis=0, tiled=True),
            lax.all_gather(ln2_gain, ("dp", "seq"), axis=0, tiled=True),
            lax.all_gather(ln2_bias, ("dp", "seq"), axis=0, tiled=True),
            lax.all_gather(w_up, ("dp", "seq"), axis=0, tiled=True),
            lax.all_gather(w_down, ("dp", "seq"), axis=1, tiled=True),
        )
        back_qkv = regathered[2]
        back_out = regathered[4]
        back_up = regathered[7]
        back_down = regathered[8]
        grad_out = cotangent[micro_step]
        grad_act = jnp.dot(grad_out, back_down.T, preferred_element_type=jnp.float32)
        grad_down = jnp.dot(activated.T, grad_out, preferred_element_type=jnp.float32)
        gelu_value, gelu_back = jax.vjp(jax.nn.gelu, upward)
        grad_upin = gelu_back(grad_act)[0].astype(jnp.bfloat16)
        grad_upw = jnp.dot(normed_two.T, grad_upin, preferred_element_type=jnp.float32)
        grad_normed_two = jnp.dot(grad_upin, back_up.T, preferred_element_type=jnp.float32)
        norm_value_two, norm_back_two = jax.vjp(layer_norm, middle, gain_second, bias_second)
        grad_mid_part, grad_gain_two, grad_bias_two = norm_back_two(grad_normed_two)
        grad_middle = grad_out.astype(jnp.float32) + grad_mid_part
        grad_branch = grad_middle.astype(jnp.bfloat16)
        grad_outw = jnp.dot(attended.T, grad_branch, preferred_element_type=jnp.float32)
        grad_mixed = (
            jnp.dot(grad_branch, back_out.T, preferred_element_type=jnp.float32)
            .astype(jnp.bfloat16)
            .reshape(block_rows, HEADS, HEAD)
        )
        near_scores, far_scores = scores_of(queries, near_keys, far_keys, near_mask, far_mask)
        near_prob, far_prob = normalise(
            near_scores, far_scores, near_mask, far_mask, row_max, row_total
        )
        near_low = near_prob.astype(jnp.bfloat16)
        far_low = far_prob.astype(jnp.bfloat16)
        grad_near_values = jnp.einsum(
            "hqk,qhd->khd", near_low, grad_mixed, preferred_element_type=jnp.float32
        )
        grad_far_values = jnp.einsum(
            "hqk,qhd->khd", far_low, grad_mixed, preferred_element_type=jnp.float32
        )
        grad_near_prob = jnp.einsum(
            "qhd,khd->hqk", grad_mixed, near_values, preferred_element_type=jnp.float32
        )
        grad_far_prob = jnp.einsum(
            "qhd,khd->hqk", grad_mixed, far_values, preferred_element_type=jnp.float32
        )
        row_delta = jnp.sum(near_prob * grad_near_prob, axis=2, keepdims=True) + jnp.sum(
            far_prob * grad_far_prob, axis=2, keepdims=True
        )
        grad_near_scores = (near_prob * (grad_near_prob - row_delta)).astype(jnp.bfloat16)
        grad_far_scores = (far_prob * (grad_far_prob - row_delta)).astype(jnp.bfloat16)
        grad_queries = (
            jnp.einsum(
                "hqk,khd->qhd", grad_near_scores, near_keys, preferred_element_type=jnp.float32
            )
            + jnp.einsum(
                "hqk,khd->qhd", grad_far_scores, far_keys, preferred_element_type=jnp.float32
            )
        ) * score_scale
        grad_near_keys = (
            jnp.einsum(
                "hqk,qhd->khd", grad_near_scores, queries, preferred_element_type=jnp.float32
            )
            * score_scale
        )
        grad_far_keys = (
            jnp.einsum("hqk,qhd->khd", grad_far_scores, queries, preferred_element_type=jnp.float32)
            * score_scale
        )
        grad_extended = jnp.concatenate(
            [grad_near_keys.reshape(-1, model_width), grad_near_values.reshape(-1, model_width)],
            axis=1,
        )
        grad_pool_ext = jnp.concatenate(
            [grad_far_keys.reshape(-1, model_width), grad_far_values.reshape(-1, model_width)],
            axis=1,
        )
        pool_edges = jnp.concatenate(
            [grad_pool_ext[:pool_half], grad_pool_ext[-pool_half:]], axis=0
        )
        pool_returned = with_halo(pool_edges.astype(jnp.bfloat16), (("seq", 0),), pool_half).astype(
            pool_edges.dtype
        )
        grad_pooled = add_rims(grad_pool_ext[pool_half:-pool_half], pool_returned, pool_half)
        pool_value, pool_back = jax.vjp(
            lambda ext_in, taps_part: pool_local(ext_in, taps_part, seg_window),
            ext_float,
            taps_float,
        )
        grad_ext_pool, grad_taps = pool_back(grad_pooled)
        grad_extended = grad_extended + grad_ext_pool
        token_edges = jnp.concatenate(
            [grad_extended[:NEAR], grad_extended[-NEAR:]], axis=0
        )
        token_returned = with_halo(
            token_edges.astype(jnp.bfloat16), (("seq", 0),), NEAR
        ).astype(token_edges.dtype)
        grad_kv = add_rims(grad_extended[NEAR:-NEAR], token_returned, NEAR)
        grad_projected = jnp.concatenate(
            [grad_queries.reshape(block_rows, model_width), grad_kv], axis=1
        ).astype(jnp.bfloat16)
        grad_qkvw = jnp.dot(normed.T, grad_projected, preferred_element_type=jnp.float32)
        grad_normed = jnp.dot(grad_projected, back_qkv.T, preferred_element_type=jnp.float32)
        norm_value_one, norm_back_one = jax.vjp(layer_norm, inputs, gain_float, bias_float)
        grad_in_part, grad_gain_one, grad_bias_one = norm_back_one(grad_normed)
        input_grads.append(grad_middle + grad_in_part)
        shares = (
            lax.psum_scatter(grad_gain_one, ("dp", "seq"), scatter_dimension=0, tiled=True),
            lax.psum_scatter(grad_bias_one, ("dp", "seq"), scatter_dimension=0, tiled=True),
            lax.psum_scatter(grad_qkvw, ("dp", "seq"), scatter_dimension=0, tiled=True),
            lax.psum_scatter(grad_taps, ("dp", "seq"), scatter_dimension=1, tiled=True),
            lax.psum_scatter(grad_outw, ("dp", "seq"), scatter_dimension=0, tiled=True),
            lax.psum_scatter(grad_gain_two, ("dp", "seq"), scatter_dimension=0, tiled=True),
            lax.psum_scatter(grad_bias_two, ("dp", "seq"), scatter_dimension=0, tiled=True),
            lax.psum_scatter(grad_upw, ("dp", "seq"), scatter_dimension=0, tiled=True),
            lax.psum_scatter(grad_down, ("dp", "seq"), scatter_dimension=1, tiled=True),
        )
        if summed is None:
            summed = shares
        else:
            summed = jax.tree.map(jnp.add, summed, shares)
    return (
        jnp.stack(outputs),
        jnp.stack(input_grads),
        summed[0],
        summed[1],
        summed[2],
        summed[3],
        summed[4],
        summed[5],
        summed[6],
        summed[7],
        summed[8],
    )


def chained(
    tokens, segments, cotangent, ln1_gain, ln1_bias, w_qkv, pool_taps, w_out, ln2_gain, ln2_bias, w_up, w_down,
):
    winc, win4, winr = windows(segments)
    small = small_share(pool_taps, ln1_gain, ln1_bias, ln2_gain, ln2_bias)
    wq, wo, wu, wd, taps, gains, h1, q, kv, pe, att, bias, lse = front(
        tokens, winc, win4, winr, w_qkv, w_out, w_up, w_down.T, small
    )
    flat, split = (1024, 768), (2, 512, 768)
    out, _, g_in, g_wq, g_wo, g_wu, g_wd, g_small = back_part(
        tokens.reshape(flat), att.reshape(flat), cotangent.reshape(flat), wo, wu, wd,
        q, kv, pe, bias, h1, wq, taps, gains, win4, lse,
    )
    return (
        out.reshape(split), g_in.reshape(split), g_small[5, :24], g_small[6, :24], g_wq, g_small[0:5, :48], g_wo,
        g_small[7, :24], g_small[8, :24], g_wu, g_wd.T,
    )


def solution(mesh):
    both = ("dp", "seq")
    row, tok, first, second = P(both), P("dp", "seq", None), P(both, None), P(None, both)
    small_mesh = mesh.shape["dp"] == 2 and mesh.shape["seq"] == 16
    return jax.shard_map(
        chained if small_mesh else shards,
        mesh=mesh,
        in_specs=(tok, P("dp", None), tok, row, row, first, second, first, row, row, first, second),
        out_specs=(tok, tok, row, row, first, second, first, row, row, first, second),
        check_vma=False,
    )
```

```python
import functools

import jax
import jax.numpy as jnp
from jax import lax
from jax.experimental import pallas as pl
from jax.experimental.pallas import tpu as pltpu
from jax.sharding import PartitionSpec as P

HEADS = 12
HEAD = 64
NEAR = 64
REACH = 256
F32, BF = jnp.float32, jnp.bfloat16
NT = (((1,), (1,)), ((), ()))
TN = (((0,), (0,)), ((), ()))
NN = (((1,), (0,)), ((), ()))
MESH = pl.DeviceIdType.MESH
ANY = pl.BlockSpec(memory_space=pl.ANY)
VM = pl.BlockSpec(memory_space=pltpu.VMEM)
VMEM_LIMIT = 63 * 2**20
UNIT = 384
CLS = 3456
WIDE = 3584
PLACE = {"qkv": (0, 0, 2304), "out": (1, 0, 768), "up": (1, 3, 3072), "down": (1, 15, 3072)}


def dg(a, b, dims):
    return lax.dot_general(a, b, dims, preferred_element_type=F32)


def spot(name, unit):
    first, start, _ = PLACE[name]
    at = start + unit
    return first + at // 9, (at % 9) * UNIT


def units(name):
    return PLACE[name][2] // UNIT


def where_am_i():
    c = lax.axis_index("dp")
    s = lax.axis_index("seq")
    z, col = s // 4, s % 4
    x, y = col % 2, col // 2
    colx, coly, cold = y * 2 + (1 - x), (1 - y) * 2 + x, 3 - col
    return dict(
        c=c, s=s, z=z, col=col, colx=colx, coly=coly, cold=cold,
        px=(c, z * 4 + colx), py=(c, z * 4 + coly), pd=(1 - c, s),
    )


def greet(me):
    bar = pltpu.get_barrier_semaphore()
    who = [me["px"], me["py"], me["pd"]]
    who += [(me["c"], lax.rem(me["z"] + j, 4) * 4 + me["col"]) for j in (1, 2, 3)]
    for dev in who:
        pl.semaphore_signal(bar, inc=1, device_id=dev, device_id_type=MESH)
    last = lax.axis_size("seq") - 1

    @pl.when(me["s"] > 0)
    def _():
        pl.semaphore_signal(bar, inc=1, device_id=(me["c"], me["s"] - 1), device_id_type=MESH)

    @pl.when(me["s"] < last)
    def _():
        pl.semaphore_signal(bar, inc=1, device_id=(me["c"], me["s"] + 1), device_id_type=MESH)

    return 6 + (me["s"] > 0).astype(jnp.int32) + (me["s"] < last).astype(jnp.int32)


def all_here(count):
    pl.semaphore_wait(pltpu.get_barrier_semaphore(), count)


def greet_all(me):
    bar = pltpu.get_barrier_semaphore()
    pl.semaphore_signal(bar, inc=1, device_id=me["pd"], device_id_type=MESH)
    for d in range(1, 16):
        pl.semaphore_signal(bar, inc=1, device_id=(me["c"], lax.rem(me["s"] + d, 16)), device_id_type=MESH)


def lane_low():
    return lax.broadcasted_iota(jnp.int32, (128, 128), 1) < HEAD


def pair_rows(v):
    low = lane_low()
    zero = jnp.zeros_like(v)
    return jnp.concatenate([jnp.where(low, v, zero), jnp.where(low, zero, v)], axis=0)


def pair_out(t):
    return jnp.concatenate([t[:HEAD, :128], t[HEAD:, 128:]], axis=0).T


def softmax_block(q2, kn, kf, bias):
    st = jnp.concatenate([dg(kn, q2, NT), dg(kf, q2, NT)], axis=0)
    st = st + jnp.concatenate([bias, bias], axis=1)
    top = jnp.max(st, axis=0, keepdims=True)
    e = jnp.exp(st - top)
    total = jnp.sum(e, axis=0, keepdims=True)
    return e, 1.0 / total, top + jnp.log(total)


def fill_window(seg, winr, wcol, has_left, has_right, s):
    length, block = seg.shape[1], 512
    left = pl.multiple_of(jnp.maximum(s * block - REACH, 0), REACH)
    right = pl.multiple_of(jnp.minimum(s * block + block, length - REACH), REACH)
    before = seg[:, pl.ds(left, REACH)].astype(F32)
    after = seg[:, pl.ds(right, REACH)].astype(F32)
    winr[:, 0:REACH] = jnp.where(has_left, before, -1.0)
    winr[:, REACH : REACH + block] = seg[:, pl.ds(pl.multiple_of(s * block, block), block)].astype(F32)
    winr[:, REACH + block :] = jnp.where(has_right, after, -1.0)
    for r in range(2):
        for t in range(8):
            row = winr[r : r + 1, t * 128 : t * 128 + 128]
            wcol[r, t * 128 : t * 128 + 128] = jnp.broadcast_to(row, (128, 128)).T


def fill_masks(winr, wcol, bias, same):
    kk = lax.broadcasted_iota(jnp.int32, (256, 128), 0)
    ii = lax.broadcasted_iota(jnp.int32, (256, 128), 1)
    pp = lax.broadcasted_iota(jnp.int32, (160, 128), 0)
    qi = lax.broadcasted_iota(jnp.int32, (160, 128), 1)
    close = jnp.abs(kk - NEAR - ii) <= NEAR
    reach = jnp.abs(4 * pp - REACH - qi) <= REACH
    for r in range(2):
        for b in range(4):
            seg_q = winr[r : r + 1, 256 + 128 * b : 384 + 128 * b]
            near = close & (wcol[r, 192 + 128 * b : 448 + 128 * b] == seg_q)
            far = reach & (wcol[r, pl.ds(128 * b, 160, stride=4), :] == seg_q)
            bias[r * 4 + b, 0:256] = jnp.where(near, 0.0, -1e30)
            bias[r * 4 + b, 256:416] = jnp.where(far, 0.0, -1e30)
        anchor = wcol[r, pl.ds(REACH, 128, stride=4), :]
        for t in range(5):
            hit = wcol[r, pl.ds(REACH - 2 + t, 128, stride=4), :] == anchor
            same[r, t] = jnp.where(hit, 1.0, 0.0).astype(BF)


def head_lanes(h):
    return (
        pl.ds(pl.multiple_of(h * 128, 128), 128),
        pl.ds(pl.multiple_of(768 + h * 128, 128), 128),
    )


def attend(q, kv, pe, bias, att, lse, r, h):
    kl, vl = head_lanes(h)
    for b in range(4):
        n, f, i = slice(b * 128, b * 128 + 256), slice(b * 32, b * 32 + 160), slice(b * 128, b * 128 + 128)
        e, rt, lse[r * 6 + h, b : b + 1] = softmax_block(
            pair_rows(q[r, i, kl]), kv[r, n, kl], pe[r, f, kl], bias[r * 4 + b]
        )
        low = (e * rt).astype(BF)
        values = jnp.concatenate([kv[r, n, vl], pe[r, f, vl]], axis=0)
        att[r, i, kl] = pair_out(dg(values, low, TN)).astype(BF)


def attend_back(q, kv, pe, bias, lse, g, gext, dkv, dpe, r, h):
    kl, vl = head_lanes(h)
    for part in (h, 6 + h):
        dkv[r, part] = jnp.zeros((640, 128), F32)
        dpe[r, part] = jnp.zeros((256, 128), F32)
    for b in range(4):
        n, f, i = slice(b * 128, b * 128 + 256), slice(b * 32, b * 32 + 160), slice(b * 128, b * 128 + 128)
        q2, g2 = pair_rows(q[r, i, kl]), pair_rows(g[r * 512 + b * 128 : r * 512 + b * 128 + 128, kl])
        kn, vn, kf, vf = kv[r, n, kl], kv[r, n, vl], pe[r, f, kl], pe[r, f, vl]
        st = jnp.concatenate([dg(kn, q2, NT), dg(kf, q2, NT)], axis=0) - lse[r * 6 + h, b : b + 1]
        p = jnp.exp(st + jnp.concatenate([bias[r * 4 + b], bias[r * 4 + b]], axis=1))
        dp = jnp.concatenate([dg(vn, g2, NT), dg(vf, g2, NT)], axis=0)
        delta = jnp.sum(p * dp, axis=0, keepdims=True)
        ds = (p * (dp - delta)).astype(BF)
        low = p.astype(BF)
        dv, dk = dg(low, g2, NN), dg(ds, q2, NN)
        dkv[r, h, n] += dk[:256]
        dkv[r, 6 + h, n] += dv[:256]
        dpe[r, h, f] += dk[256:]
        dpe[r, 6 + h, f] += dv[256:]
        dqt = dg(jnp.concatenate([kn, kf], axis=0), ds, TN)
        gext[r * 640 + 64 + b * 128 : r * 640 + 192 + b * 128, kl] = (pair_out(dqt) * HEAD**-0.5).astype(BF)


def norm_parts(v):
    mean = jnp.mean(v, axis=-1, keepdims=True)
    cen = v - mean
    var = jnp.mean(cen * cen, axis=-1, keepdims=True)
    rs = lax.rsqrt(var + 1e-05)
    return cen * rs, rs


LAST = 29


def pack_own(grab, put):
    for name in ("qkv", "out", "up", "down"):
        half = units(name) // 2
        for u in range(units(name)):
            k, lo = spot(name, u)
            put(k, lo, grab(name, 0, 16, u))
        for u in range(half):
            k, lo = spot(name, units(name) + u)
            put(k, lo, jnp.concatenate([grab(name, 16, 24, u), grab(name, 16, 24, u + half)], axis=0))


def hidden_place(n):
    half, r = divmod(n, 1536)
    return (r // 256) * 512 + half * 256 + r % 256


def unpack(name, got, dst):
    half = units(name) // 2

    def pair(p, carry):
        rows = pl.ds(pl.multiple_of(48 * p, 16), 48)
        for u in range(units(name)):
            k, lo = spot(name, u)
            kt, lt = spot(name, units(name) + u % half)
            cut = slice(0, 8) if u < half else slice(8, 16)
            hidden = name in ("up", "down")
            for i in range(0, UNIT, 128) if hidden else (0,):
                n = 128 if hidden else UNIT
                to = hidden_place(u * UNIT + i) if hidden else u * UNIT
                parts = []
                for j in (0, 1):
                    parts.append(got[k, 2 * p + j, :, lo + i : lo + i + n])
                    parts.append(got[kt, 2 * p + j, :, lt + i : lt + i + n][cut])
                dst[rows, to : to + n] = jnp.concatenate(parts, axis=0)
        return carry

    lax.fori_loop(0, 16, pair, 0)


def spread_small(got, taps, gains):
    lane = lax.broadcasted_iota(jnp.int32, (16, 128), 1)

    def place(width, tiles):
        acc = [jnp.zeros((16, 128), F32) for _ in range(tiles)]
        for s in range(32):
            at, off = divmod(width * s, 128)
            v = jnp.where(lane < width, got[0, s, :, CLS:WIDE].astype(F32), 0.0)
            v = pltpu.roll(v, off, 1) if off else v
            acc[at] = acc[at] + jnp.where(lane >= off, v, 0.0)
            if off + width > 128:
                acc[at + 1] = acc[at + 1] + jnp.where(lane < off, v, 0.0)
        return acc

    for i, v in enumerate(place(48, 12)):
        taps[:, i * 128 : (i + 1) * 128] = v
    for i, v in enumerate(place(24, 6)):
        gains[:, i * 128 : (i + 1) * 128] = v


def front_kernel(
    tok, seg, wq, wo, wu, wd, small,
    o_wq, o_wo, o_wu, o_wd, o_taps, o_gains, o_h1, o_q, o_kv, o_pe, o_att, o_bias, o_lse, o_same,
    G, Wq, Wo, Wu, Wd, taps, gains, xe, h1, q, kv, pe, att, bias, lse, same, chunk, winr, wcol,
    send_x, send_y, send_d, send_z, send_g, recv, hsend, hrecv, local,
):
    me = where_am_i()
    c, s, z, col = me["c"], me["s"], me["z"], me["col"]
    mine = c * 16 + s
    last = lax.axis_size("seq") - 1
    has_left, has_right = s > 0, s < last

    def cols(k):
        return WIDE if isinstance(k, int) and k == 0 else CLS

    def hop(k, slot, to, sem):
        part = G.at[k, slot, :, pl.ds(0, cols(k))]
        return pltpu.make_async_remote_copy(
            src_ref=part, dst_ref=part, send_sem=sem, recv_sem=recv.at[k, slot],
            device_id=to, device_id_type=MESH,
        )

    def to_x(k, at):
        return hop(k, c * 16 + at, me["px"], send_x.at[k, at])

    def to_y(k, at):
        return hop(k, c * 16 + at, me["py"], send_y.at[k, at])

    def to_d(k, at):
        return hop(k, c * 16 + at, me["pd"], send_d.at[k, at])

    def to_z(k, j):
        return hop(k, mine, (c, lax.rem(z + j, 4) * 4 + col), send_z.at[k, j - 1])

    def by_y(k, zz):
        return zz != 3

    def to_g(k, zz):
        over_y = by_y(k, zz)
        at = zz * 4 + jnp.where(over_y, me["colx"], me["coly"])
        to = (c, z * 4 + jnp.where(over_y, me["coly"], me["colx"]))
        return hop(k, c * 16 + at, to, send_g.at[k, zz])

    def got(k, slot):
        hop(k, slot, me["px"], send_x.at[k, 0]).wait_recv()

    def own(k):
        for j in (1, 2, 3):
            to_z(k, j).start()
        to_x(k, s).start()
        to_y(k, s).start()
        to_d(k, s).start()

    def column(k, j):
        at = lax.rem(z + j, 4) * 4 + col
        got(k, c * 16 + at)
        to_x(k, at).start()
        to_y(k, at).start()
        to_d(k, at).start()

    def plane(k, j):
        zz = lax.rem(z + j, 4)
        got(k, c * 16 + zz * 4 + me["colx"])
        to_d(k, zz * 4 + me["colx"]).start()
        got(k, c * 16 + zz * 4 + me["coly"])
        to_d(k, zz * 4 + me["coly"]).start()
        to_g(k, zz).start()

    def diag(k, j):
        at = lax.rem(z + j, 4) * 4 + me["cold"]
        got(k, c * 16 + at)
        to_d(k, at).start()

    def event(e):
        k, i = e // 11 + 1, lax.rem(e, 11)

        @pl.when(i < 4)
        def _():
            plane(k, i)

        @pl.when((i >= 4) & (i < 7) & (k < 3))
        def _():
            column(k + 1, i - 3)

        @pl.when(i >= 7)
        def _():
            diag(k, i - 7)

    def halo_tok(r, right):
        src = tok.at[r, pl.ds(448 if right else 0, 64)]
        dst = xe.at[r, pl.ds(0 if right else 576, 64)]
        i = r * 2 + int(right)
        return pltpu.make_async_remote_copy(
            src_ref=src, dst_ref=dst, send_sem=hsend.at[i], recv_sem=hrecv.at[i],
            device_id=(c, s + 1 if right else s - 1), device_id_type=MESH,
        )

    def halo_pool(r, right):
        src = pe.at[r, pl.ds(128 if right else 64, 64)]
        dst = pe.at[r, pl.ds(0 if right else 192, 64)]
        i = 4 + r * 2 + int(right)
        return pltpu.make_async_remote_copy(
            src_ref=src, dst_ref=dst, send_sem=hsend.at[i], recv_sem=hrecv.at[i],
            device_id=(c, s + 1 if right else s - 1), device_id_type=MESH,
        )

    def both(make, r, act):
        @pl.when(has_right)
        def _():
            act(make(r, True), True)

        @pl.when(has_left)
        def _():
            act(make(r, False), False)

    def arrived(make, r):
        @pl.when(has_left)
        def _():
            make(r, True).wait_recv()

        @pl.when(has_right)
        def _():
            make(r, False).wait_recv()

    expected = greet(me)
    load = [pltpu.make_async_copy(tok.at[r], xe.at[r, pl.ds(64, 512)], local.at[r]) for r in range(2)]
    for copy in load:
        copy.start()
    shares = {"qkv": wq, "out": wo, "up": wu, "down": wd}

    def grab(name, a, b, u):
        return shares[name][a:b, u * UNIT : (u + 1) * UNIT]

    def put(k, lo, v):
        G[k, mine, :, lo : lo + UNIT] = v

    pack_own(grab, put)
    G[0, mine, :, CLS:WIDE] = small[...]

    @pl.when(jnp.logical_not(has_left))
    def _():
        for r in range(2):
            xe[r, 0:64] = jnp.zeros((64, 768), BF)
            pe[r, 0:64] = jnp.zeros((64, 1536), BF)

    @pl.when(jnp.logical_not(has_right))
    def _():
        for r in range(2):
            xe[r, 576:640] = jnp.zeros((64, 768), BF)
            pe[r, 192:256] = jnp.zeros((64, 1536), BF)

    lse[...] = jnp.zeros((12, 8, 256), F32)
    all_here(expected)
    own(0)
    for r in range(2):
        both(halo_tok, r, lambda copy, right: copy.start())
    own(1)
    own(2)
    fill_window(seg, winr, wcol, has_left, has_right, s)
    fill_masks(winr, wcol, bias, same)
    for j in (1, 2, 3):
        column(0, j)
    for j in range(4):
        plane(0, j)
    own(3)
    for j in (1, 2, 3):
        column(1, j)
    for j in range(4):
        diag(0, j)

    def other(k):
        def body(i, carry):
            got(k, (1 - c) * 16 + i)
            return carry

        lax.fori_loop(0, 16, body, 0)

    other(0)
    unpack("qkv", G, Wq)
    spread_small(G, taps, gains)
    outs = [
        pltpu.make_async_copy(a, b, local.at[2 + i])
        for i, (a, b) in enumerate(
            [(Wq, o_wq), (taps, o_taps), (gains, o_gains), (h1, o_h1), (q, o_q), (kv, o_kv), (pe, o_pe),
             (att, o_att), (bias, o_bias), (Wo, o_wo), (Wu, o_wu), (Wd, o_wd), (lse, o_lse), (same, o_same)]
        )
    ]
    for i in (0, 1, 2, 8, 13):
        outs[i].start()
    for copy in load:
        copy.wait()
    for r in range(2):
        arrived(halo_tok, r)

    for r in range(2):
        def norm_rows(i, carry):
            rows = pl.ds(pl.multiple_of(i * 128, 128), 128)
            n, _ = norm_parts(xe[r, rows].astype(F32))
            h1[r, rows] = (n * gains[5:6] + gains[6:7]).astype(BF)
            return carry

        lax.fori_loop(0, 5, norm_rows, 0)
    outs[3].start()

    for r in range(2):
        def queries(j, carry):
            lanes = pl.ds(pl.multiple_of(j * 256, 256), 256)
            v = dg(h1[r, 64:576], Wq[:, lanes], NN)
            q[r, :, lanes] = v.astype(BF) * jnp.asarray(HEAD**-0.5, BF)
            return carry

        lax.fori_loop(0, 3, queries, 0)
        def keys(j, carry):
            event(r * 6 + j)
            lanes = pl.ds(pl.multiple_of(j * 128, 128), 128)
            from_lanes = pl.ds(pl.multiple_of(768 + j * 256, 256), 256)
            to_lanes = pl.ds(pl.multiple_of(j * 256, 256), 256)
            v = dg(h1[r], Wq[:, from_lanes], NN).astype(BF)
            kv[r, :, to_lanes] = v
            chunk[0] = v[:, :128].astype(F32)
            chunk[1] = v[:, 128:].astype(F32)
            for half in range(2):
                hl = pl.ds(pl.multiple_of(j * 256 + half * 128, 128), 128)
                acc = jnp.zeros((128, 128), F32)
                for t in range(5):
                    acc = acc + taps[t : t + 1, hl] * chunk[half, pl.ds(62 + t, 128, stride=4), :] * same[r, t].astype(F32)
                pe[r, 64:192, hl] = acc.astype(BF)
            return carry

        lax.fori_loop(0, 6, keys, 0)
        both(halo_pool, r, lambda copy, right: copy.start())
    outs[4].start()
    outs[5].start()
    for r in range(2):
        arrived(halo_pool, r)

        def heads_event(h, carry):
            attend(q, kv, pe, bias, att, lse, r, h)
            base = 12 + (r * 6 + h) * 2

            @pl.when(base < LAST)
            def _():
                event(base)

            @pl.when(base + 1 < LAST)
            def _():
                event(base + 1)

            return carry

        lax.fori_loop(0, 6, heads_event, 0)
    outs[6].start()
    outs[7].start()
    outs[12].start()
    for k in (1, 2):
        other(k)
    finish = (("out", Wo), ("up", Wu), ("down", Wd))
    for i in range(2):
        unpack(finish[i][0], G, finish[i][1])
        outs[9 + i].start()
    lax.fori_loop(LAST, 33, lambda e, carry: (event(e), carry)[1], 0)
    other(3)
    unpack("down", G, Wd)
    outs[11].start()
    for r in range(2):
        both(halo_tok, r, lambda copy, right: copy.wait_send())
        both(halo_pool, r, lambda copy, right: copy.wait_send())
    for k in range(4):
        def done(i, carry):
            to_x(k, i * 4 + col).wait_send()
            to_y(k, i * 4 + col).wait_send()
            to_g(k, i).wait_send()
            for j in range(4):
                to_d(k, i * 4 + j).wait_send()
            return carry

        lax.fori_loop(0, 4, done, 0)
        for j in (1, 2, 3):
            to_z(k, j).wait_send()
    for copy in outs:
        copy.wait()


def front(tok, seg, wq, wo, wu, wd, small):
    sds = jax.ShapeDtypeStruct
    shapes = [
        ((768, 2304), BF), ((768, 768), BF), ((768, 3072), BF), ((768, 3072), BF),
        ((16, 1536), F32), ((16, 768), F32),
        ((2, 640, 768), BF), ((2, 512, 768), BF), ((2, 640, 1536), BF), ((2, 256, 1536), BF),
        ((2, 512, 768), BF), ((8, 416, 128), F32), ((12, 8, 256), F32),
        ((2, 5, 128, 128), BF),
    ]
    scratch = [pltpu.VMEM((4, 32, 16, WIDE), BF)]
    scratch += [pltpu.VMEM(sh, dt) for sh, dt in shapes[:6]]
    scratch += [pltpu.VMEM((2, 640, 768), BF)]
    scratch += [pltpu.VMEM(sh, dt) for sh, dt in shapes[6:]]
    scratch += [pltpu.VMEM((2, 640, 128), F32), pltpu.VMEM((2, 1024), F32), pltpu.VMEM((2, 1024, 128), F32)]
    dma = pltpu.SemaphoreType.DMA
    scratch += [dma((4, 16)), dma((4, 16)), dma((4, 16)), dma((4, 3)), dma((4, 4)), dma((4, 32)), dma((8,)), dma((8,)), dma((16,))]
    return pl.pallas_call(
        front_kernel,
        out_shape=[sds(sh, dt) for sh, dt in shapes],
        in_specs=[ANY] + [VM] * 6,
        out_specs=[ANY] * len(shapes),
        scratch_shapes=scratch,
        compiler_params=pltpu.CompilerParams(collective_id=0, has_side_effects=True, vmem_limit_bytes=VMEM_LIMIT),
    )(tok, seg, wq, wo, wu, wd, small)


def small_share(pool_taps, ln1_gain, ln1_bias, ln2_gain, ln2_bias):
    rows = jnp.stack([ln1_gain, ln1_bias, ln2_gain, ln2_bias])
    return jnp.concatenate(
        [jnp.pad(pool_taps, ((0, 0), (0, 80))), jnp.pad(rows, ((0, 7), (0, 104)))], axis=0
    )


def gelu_both(u):
    a, b = 0.7978845608028654, 0.044715
    sq = u * u
    t = jnp.tanh(a * u * (1.0 + b * sq))
    half = 0.5 + 0.5 * t
    grad = half + 0.5 * u * (1.0 - t * t) * (a + (3.0 * a * b) * sq)
    return u * half, grad


def pack_pair(lo, hi):
    return jnp.concatenate([lo, hi], axis=0).astype(BF)


def pick_small(tg, lg, put):
    lane = lax.broadcasted_iota(jnp.int32, (16, 128), 1)

    def part(src, width, s):
        at, off = divmod(width * s, 128)
        v = src[:, at * 128 : at * 128 + 128]
        v = pltpu.roll(v, 128 - off, 1) if off else v
        if off + width > 128:
            w = pltpu.roll(src[:, at * 128 + 128 : at * 128 + 256], 128 - off, 1)
            v = jnp.where(lane < 128 - off, v, w)
        return jnp.where(lane < width, v, 0.0)

    for s in range(32):
        put(s, (part(tg, 48, s) + part(lg, 24, s)).astype(BF))


def back_kernel(
    tok_in, att_in, dy_in, wo_in, wu_in, wd_in,
    q_in, kv_in, pe_in, bias_in, h1_in, wq_in, taps, gains, same, lse,
    o_out, o_gmid, o_in, o_wq, o_wo, o_wu, o_wd, o_small,
    Sf, So, Ss, Rf, Ro, Rq, Rs, gatt, pstage, precv, hstage, hrecv, tg, lg,
    send, recv, psend, prsem, local,
):
    me = where_am_i()
    greet_all(me)
    c, s, z, col = me["c"], me["s"], me["z"], me["col"]
    has_left, has_right = s > 0, s < lax.axis_size("seq") - 1

    def copy(i, a, b):
        return pltpu.make_async_copy(a, b, local.at[i])

    late = []

    def cls(k):
        if k < 3:
            return Sf.at[k, pl.ds(c * 16, 16)], Rf.at[k]
        if k == 3:
            return So.at[pl.ds(c * 16, 16)], Ro
        if k < 7:
            return late[0].at[k - 4, pl.ds(c * 16, 16)], Rq.at[k - 4]
        return Ss.at[pl.ds(c * 16, 16)], Rs

    def other(k):
        start = (1 - c) * 16
        if k < 3:
            return Sf.at[k, pl.ds(start, 16)]
        if k == 3 or k == 7:
            return (So if k == 3 else Ss).at[pl.ds(start, 16)]
        return late[0].at[k - 4, pl.ds(start, 16)]

    def remote(k, src, slot, i, to):
        return pltpu.make_async_remote_copy(
            src_ref=src, dst_ref=slot, send_sem=send.at[k, i], recv_sem=recv.at[k, i],
            device_id=to, device_id_type=MESH,
        )

    def swap(k):
        return remote(k, other(k), cls(k)[1].at[pl.ds(0, 16)], 0, me["pd"])

    def step_g(k, zz):
        S, R = cls(k)
        to = me["px"] if zz % 2 == 0 else me["py"]
        return remote(k, S.at[zz * 4 + me["cold"]], R.at[16 + zz], 1 + zz, to)

    def step_x(k, zz):
        S, R = cls(k)
        return remote(k, S.at[zz * 4 + me["colx"]], R.at[20 + zz], 5 + zz, me["px"])

    def step_y(k, zz):
        S, R = cls(k)
        return remote(k, S.at[zz * 4 + me["coly"]], R.at[24 + zz], 9 + zz, me["py"])

    def step_z(k, j):
        S, R = cls(k)
        zz = lax.rem(z + j, 4)
        return remote(k, S.at[zz * 4 + col], R.at[27 + j], 12 + j, (c, zz * 4 + col))

    def add(k, at, slots):
        S, R = cls(k)
        v = S[at].astype(F32) + R[at].astype(F32)
        for slot in slots:
            v = v + R[slot].astype(F32)
        return v

    def begin(k):
        swap(k).start()

    def do_g(k, zz):
        if zz == 0:
            swap(k).wait_recv()
        at = zz * 4 + me["cold"]
        cls(k)[0][at] = add(k, at, []).astype(BF)
        step_g(k, zz).start()

    def do_p(k, zz):
        step_g(k, zz).wait_recv()
        even = zz % 2 == 0
        for at, step, has in ((zz * 4 + me["colx"], step_x, not even), (zz * 4 + me["coly"], step_y, even)):
            cls(k)[0][at] = add(k, at, [16 + zz] if has else []).astype(BF)
            step(k, zz).start()

    def arrive(k, zz):
        S, R = cls(k)
        remote(k, S.at[0], R.at[20 + zz], 5 + zz, me["px"]).wait_recv()
        remote(k, S.at[0], R.at[24 + zz], 9 + zz, me["py"]).wait_recv()

    def do_c(k, j):
        zz = lax.rem(z + j, 4)
        arrive(k, zz)
        at = zz * 4 + col
        cls(k)[0][at] = add(k, at, [20 + zz, 24 + zz]).astype(BF)
        step_z(k, j).start()

    def total(k):
        arrive(k, z)
        for j in (1, 2, 3):
            step_z(k, j).wait_recv()
        return add(k, z * 4 + col, [20 + z, 24 + z, 28, 29, 30])

    def drain(k):
        swap(k).wait_send()
        for zz in range(4):
            step_g(k, zz).wait_send()
            step_x(k, zz).wait_send()
            step_y(k, zz).wait_send()
        for j in (1, 2, 3):
            step_z(k, j).wait_send()

    def finish(k):
        v = total(k)
        if k < 3:
            for i in range(2):
                for ref, base in ((o_wu, i * 1536), (o_wd, i * 1536 + 768)):
                    lo, hi = (2 * k + i) * 256, 1536 + (2 * k + i) * 256
                    ref[0:16, lo : lo + 256] = v[:, base : base + 256]
                    ref[0:16, hi : hi + 256] = v[:, base + 256 : base + 512]
                    ref[16:24, lo : lo + 256] = v[0:8, base + 512 : base + 768]
                    ref[16:24, hi : hi + 256] = v[8:16, base + 512 : base + 768]
        else:
            ref, at = (o_wo, 0) if k == 3 else (o_wq, (k - 4) * 768)
            ref[0:16, at : at + 768] = v[:, 0:768]
            ref[16:24, at : at + 384] = v[0:8, 768:1152]
            ref[16:24, at + 384 : at + 768] = v[8:16, 768:1152]
        drain(k)

    def to_owner(d):
        owner = lax.rem(s + d, 16)
        return remote(7, Ss.at[c * 16 + owner], Rs.at[16 + s], d, (c, owner))

    def from_peer(d):
        slot = 16 + lax.rem(s + 16 - d, 16)
        return remote(7, Ss.at[0], Rs.at[slot], d, me["px"])

    def small_out():
        swap(7).wait_recv()
        for i in range(16):
            Ss[c * 16 + i] = (Ss[c * 16 + i].astype(F32) + Rs[i].astype(F32)).astype(BF)
        for d in range(1, 16):
            to_owner(d).start()

    def small_in():
        v = Ss[c * 16 + s].astype(F32)
        for d in range(1, 16):
            from_peer(d).wait_recv()
            v = v + Rs[16 + lax.rem(s + 16 - d, 16)].astype(F32)
        o_small[...] = v
        swap(7).wait_send()
        for d in range(1, 16):
            to_owner(d).wait_send()

    def halo(src, dst, r, right, h):
        side = int(right)
        i = 24 + r * 2 + side if h is None else (r * 2 + side) * 6 + h
        at = (r, side) if h is None else (r, side, h)
        return pltpu.make_async_remote_copy(
            src_ref=src.at[at], dst_ref=dst.at[at], send_sem=psend.at[i], recv_sem=prsem.at[i],
            device_id=(c, s + 1 if right else s - 1), device_id_type=MESH,
        )

    def both(src, dst, r, h, act):
        @pl.when(has_right)
        def _():
            act(halo(src, dst, r, True, h))

        @pl.when(has_left)
        def _():
            act(halo(src, dst, r, False, h))

    def arrived(src, dst, r, h):
        @pl.when(has_left)
        def _():
            halo(src, dst, r, True, h).wait_recv()

        @pl.when(has_right)
        def _():
            halo(src, dst, r, False, h).wait_recv()

    @pl.when(jnp.logical_not(has_left))
    def _():
        precv[:, 1] = jnp.zeros((2, 6, 2, 64, 128), BF)
        hrecv[:, 1] = jnp.zeros((2, 64, 768), BF)

    @pl.when(jnp.logical_not(has_right))
    def _():
        precv[:, 0] = jnp.zeros((2, 6, 2, 64, 128), BF)
        hrecv[:, 0] = jnp.zeros((2, 64, 768), BF)

    tg[...] = jnp.zeros((16, 1536), F32)
    lg[...] = jnp.zeros((16, 768), F32)

    def perform(todo):
        for fn, k in todo:
            if fn is begin or fn is finish:
                fn(k)
            else:
                for j in (1, 2, 3) if fn is do_c else (0, 1, 2, 3):
                    fn(k, j)

    def run(plan, at):
        for i, todo in plan.items():
            @pl.when(at == i)
            def _():
                perform(todo)

    def feed_forward(Tok, Att, Dy, Wo, Wu, Wd, mid, h2, DyT, H2T, y, gh2, act, gu):
        loads = [
            copy(i, a, b)
            for i, (a, b) in enumerate(
                [(tok_in, Tok), (att_in, Att), (wo_in, Wo), (dy_in, Dy), (wu_in, Wu), (wd_in, Wd)]
            )
        ]
        for ld in loads:
            ld.start()
        y[...] = jnp.zeros((1024, 768), F32)
        gh2[...] = jnp.zeros((1024, 768), F32)
        for ld in loads[:3]:
            ld.wait()
        mid[...] = dg(Att[...], Wo[...], NN)

        def first(i, carry):
            rows = pl.ds(pl.multiple_of(i * 128, 128), 128)
            v = Tok[rows].astype(F32) + mid[rows]
            mid[rows] = v
            n, _ = norm_parts(v)
            h2[rows] = (n * gains[7:8] + gains[8:9]).astype(BF)
            return carry

        lax.fori_loop(0, 8, first, 0)
        loads[3].wait()

        def flip(i, carry):
            rows = pl.ds(pl.multiple_of(i * 128, 128), 128)
            for j in range(3):
                cols = slice(j * 256, j * 256 + 256)
                DyT[cols, rows] = Dy[rows, cols].T
                H2T[cols, rows] = h2[rows, cols].T
            return carry

        lax.fori_loop(0, 8, flip, 0)
        loads[4].wait()
        loads[5].wait()
        plan = {
            5: [(begin, 0)], 7: [(do_g, 0)], 11: [(do_p, 0), (begin, 1)], 13: [(do_g, 1)],
            17: [(do_c, 0), (begin, 2)],
        }

        all_here(16)

        def chunk(j, carry):
            lanes = [pl.ds(pl.multiple_of(j * 512 + h * 256, 256), 256) for h in range(2)]
            whole = pl.ds(pl.multiple_of(j * 512, 512), 512)
            for m in range(2):
                rows = slice(m * 512, m * 512 + 512)
                for h in range(2):
                    u = dg(h2[rows], Wu[:, lanes[h]], NN)
                    ga = dg(Dy[rows], Wd[:, lanes[h]], NN)
                    a, da = gelu_both(u)
                    act[rows, h * 256 : h * 256 + 256] = a.astype(BF)
                    gu[rows, h * 256 : h * 256 + 256] = (ga * da).astype(BF)
            run(plan, j * 3)
            y[...] += dg(act[...], Wd[:, whole], NT)
            gh2[...] += dg(gu[...], Wu[:, whole], NT)
            run(plan, j * 3 + 1)
            for which, (left, right) in enumerate(((H2T, gu), (DyT, act))):
                base = lax.rem(j, 2) * 1536 + which * 768
                at = [pl.ds(pl.multiple_of(base + i * 256, 256), 256) for i in range(3)]
                dws = dg(left[...], right[...], NN)
                for i in range(32):
                    head, tail = dws[i * 24 : i * 24 + 16].astype(BF), dws[i * 24 + 16 : i * 24 + 24]
                    Sf[j // 2, i, :, at[0]] = head[:, 0:256]
                    Sf[j // 2, i, :, at[1]] = head[:, 256:512]
                    Sf[j // 2, i, :, at[2]] = pack_pair(tail[:, 0:256], tail[:, 256:512])
            run(plan, j * 3 + 2)
            return carry

        lax.fori_loop(0, 6, chunk, 0)

        def last(i, carry):
            rows = pl.ds(pl.multiple_of(i * 128, 128), 128)
            v = mid[rows]
            Tok[rows] = (v + y[rows]).astype(BF)
            n, rs = norm_parts(v)
            g = gh2[rows]
            e = g * gains[7:8]
            gm = Dy[rows].astype(F32) + rs * (
                e - jnp.mean(e, axis=-1, keepdims=True) - n * jnp.mean(e * n, axis=-1, keepdims=True)
            )
            y[rows] = gm
            h2[rows] = gm.astype(BF)
            a, b = carry
            return a + jnp.sum((g * n).reshape(16, 8, 768), axis=0), b + jnp.sum(g.reshape(16, 8, 768), axis=0)

        zero = jnp.zeros((8, 768), F32)
        a, b = lax.fori_loop(0, 8, last, (zero, zero))
        perform([(do_p, 1)])
        lg[7:8] = jnp.sum(a, axis=0, keepdims=True)
        lg[8:9] = jnp.sum(b, axis=0, keepdims=True)
        store = [copy(6, Tok, o_out), copy(7, y, o_gmid)]
        for st in store:
            st.start()

        def flip_att(i, carry):
            rows = pl.ds(pl.multiple_of(i * 128, 128), 128)
            for j in range(3):
                DyT[j * 256 : j * 256 + 256, rows] = Att[rows, j * 256 : j * 256 + 256].T
            return carry

        lax.fori_loop(0, 8, flip_att, 0)
        gatt[...] = dg(h2[...], Wo[...], NT).astype(BF)
        dws = dg(DyT[...], h2[...], NN)
        for i in range(32):
            tail = dws[i * 24 + 16 : i * 24 + 24]
            So[i, :, 0:768] = dws[i * 24 : i * 24 + 16].astype(BF)
            So[i, :, 768:1152] = pack_pair(tail[:, 0:384], tail[:, 384:768])
        begin(3)
        perform([(do_g, 2)])
        for st in store:
            st.wait()

    def weight_grad(gext, h1t, Sq, j):
        dws = dg(h1t[...], gext[:, j * 768 : j * 768 + 768], NN)
        for i in range(32):
            tail = dws[i * 24 + 16 : i * 24 + 24]
            Sq[j, i, :, 0:768] = dws[i * 24 : i * 24 + 16].astype(BF)
            Sq[j, i, :, 768:1152] = pack_pair(tail[:, 0:384], tail[:, 384:768])
        begin(4 + j)

    def attention(gext, h1, h1t, Sq, kv, dkv, dpe, chunk):
        late_load = copy(8, h1_in, h1)
        late_load.start()

        def scores(q, pe, bias):
            loads = [
                copy(4 + i, a, b)
                for i, (a, b) in enumerate([(q_in, q), (kv_in, kv), (pe_in, pe), (bias_in, bias)])
            ]
            for ld in loads:
                ld.start()
            for r in range(2):
                gext[r * 640 : r * 640 + 64, 0:768] = jnp.zeros((64, 768), BF)
                gext[r * 640 + 576 : r * 640 + 640, 0:768] = jnp.zeros((64, 768), BF)
            for ld in loads:
                ld.wait()
            plans = (
                {0: [(do_c, 1)], 2: [(do_p, 2)], 3: [(do_g, 3)], 5: [(do_p, 3)]},
                {2: [(do_c, 2)], 3: [(do_c, 3)]},
            )
            for r in range(2):
                def heads(h, carry):
                    attend_back(q, kv, pe, bias, lse, gatt, gext, dkv, dpe, r, h)
                    for part in range(2):
                        pstage[r, 0, h, part] = dpe[r, part * 6 + h, 0:64].astype(BF)
                        pstage[r, 1, h, part] = dpe[r, part * 6 + h, 192:256].astype(BF)
                    both(pstage, precv, r, h, lambda cp: cp.start())
                    run(plans[r], h)
                    return carry

                lax.fori_loop(0, 6, heads, 0)

        pl.run_scoped(
            scores, vm((2, 512, 768), BF), vm((2, 256, 1536), BF), vm((8, 416, 128), F32)
        )
        late_load.wait()
        for r in range(2):
            def flip(i, carry):
                rows = pl.ds(pl.multiple_of(i * 128, 128), 128)
                for j in range(3):
                    to = pl.ds(pl.multiple_of(r * 640 + i * 128, 128), 128)
                    h1t[j * 256 : j * 256 + 256, to] = h1[r, rows, j * 256 : j * 256 + 256].T
                return carry

            lax.fori_loop(0, 5, flip, 0)
        weight_grad(gext, h1t, Sq, 0)
        for part in range(2):
            for r in range(2):
                def pool_back(h, carry):
                    t = part * 6 + h
                    lanes = pl.ds(pl.multiple_of(t * 128, 128), 128)
                    if part == 0:
                        arrived(pstage, precv, r, h)

                    low = dpe[r, t, 64:128] + precv[r, 1, h, part].astype(F32)
                    high = dpe[r, t, 128:192] + precv[r, 0, h, part].astype(F32)
                    gp = jnp.concatenate([low, high], axis=0)
                    chunk[...] = kv[r, :, lanes].astype(F32)
                    for i in range(5):
                        at = pl.ds(62 + i, 128, stride=4)
                        gm = gp * same[r, i].astype(F32)
                        tg[i : i + 1, lanes] += jnp.sum(gm * chunk[at, :], axis=0, keepdims=True)
                        dkv[r, t, at, :] += gm * taps[i : i + 1, lanes]
                    out_lanes = pl.ds(pl.multiple_of(768 + t * 128, 128), 128)
                    gext[r * 640 : r * 640 + 640, out_lanes] = dkv[r, t].astype(BF)
                    return carry

                lax.fori_loop(0, 6, pool_back, 0)
            weight_grad(gext, h1t, Sq, 1 + part)
            perform([(do_g, 4 + part)])

    def projection(gext, h1t, Sq, wq, tok, gmid, gh):
        loads = [
            copy(9 + i, a, b) for i, (a, b) in enumerate([(wq_in, wq), (tok_in, tok), (o_gmid, gmid)])
        ]
        for ld in loads:
            ld.start()
        perform([(do_p, 4)])
        for ld in loads:
            ld.wait()
        for r in range(2):
            gh[r] = dg(gext[r * 640 : r * 640 + 640], wq[...], NT)
            hstage[r, 0] = gh[r, 0:64].astype(BF)
            hstage[r, 1] = gh[r, 576:640].astype(BF)
            both(hstage, hrecv, r, None, lambda cp: cp.start())
            perform(([(do_g, 6), (do_p, 5)], [(do_p, 6), (do_c, 4)])[r])

        def rows_norm(r, i, carry):
            rows = pl.ds(pl.multiple_of(r * 512 + i * 128, 128), 128)
            n, rs = norm_parts(tok[rows].astype(F32))
            g = gh[r, pl.ds(pl.multiple_of(i * 128 + 64, 64), 128)]
            e = g * gains[5:6]
            gmid[rows] += rs * (
                e - jnp.mean(e, axis=-1, keepdims=True) - n * jnp.mean(e * n, axis=-1, keepdims=True)
            )
            a, b = carry
            return a + jnp.sum((g * n).reshape(16, 8, 768), axis=0), b + jnp.sum(g.reshape(16, 8, 768), axis=0)

        def add_halo(r):
            arrived(hstage, hrecv, r, None)
            gh[r, 64:128] += hrecv[r, 1].astype(F32)
            gh[r, 512:576] += hrecv[r, 0].astype(F32)

        zero = jnp.zeros((8, 768), F32)
        add_halo(0)
        acc = lax.fori_loop(0, 4, lambda i, cr: rows_norm(0, i, cr), (zero, zero))
        acc = lax.fori_loop(1, 3, lambda i, cr: rows_norm(1, i, cr), acc)
        add_halo(1)
        acc = lax.fori_loop(0, 2, lambda i, cr: rows_norm(1, 3 * i, cr), acc)
        out = copy(13, gmid, o_in)
        out.start()
        lg[5:6] = jnp.sum(acc[0], axis=0, keepdims=True)
        lg[6:7] = jnp.sum(acc[1], axis=0, keepdims=True)

        def put(i, v):
            Ss[i] = v

        pick_small(tg, lg, put)
        begin(7)
        perform([(do_c, 5), (finish, 0)])
        small_out()
        perform([(finish, 1), (finish, 2), (finish, 3), (do_c, 6), (finish, 4), (finish, 5)])
        small_in()
        perform([(finish, 6)])
        out.wait()

    vm = pltpu.VMEM
    tall, wide = (lambda dt: vm((1024, 768), dt)), (lambda dt: vm((768, 1024), dt))
    pl.run_scoped(
        feed_forward,
        tall(BF), tall(BF), tall(BF), vm((768, 768), BF), vm((768, 3072), BF), vm((768, 3072), BF),
        tall(F32), tall(BF), wide(BF), wide(BF), tall(F32), tall(F32), vm((1024, 512), BF), vm((1024, 512), BF),
    )

    def rest(gext, h1, h1t, Sq):
        late.append(Sq)
        pl.run_scoped(
            functools.partial(attention, gext, h1, h1t, Sq),
            vm((2, 640, 1536), BF), vm((2, 12, 640, 128), F32), vm((2, 12, 256, 128), F32), vm((640, 128), F32),
        )
        pl.run_scoped(
            functools.partial(projection, gext, h1t, Sq),
            vm((768, 2304), BF), tall(BF), tall(F32), vm((2, 640, 768), F32),
        )

    pl.run_scoped(
        rest, vm((1280, 2304), BF), vm((2, 640, 768), BF), vm((768, 1280), BF), vm((3, 32, 16, 1152), BF)
    )
    for r in range(2):
        for h in range(6):
            both(pstage, precv, r, h, lambda cp: cp.wait_send())
        both(hstage, hrecv, r, None, lambda cp: cp.wait_send())


def back_part(*args):
    sds = jax.ShapeDtypeStruct
    vm, dma = pltpu.VMEM, pltpu.SemaphoreType.DMA
    return pl.pallas_call(
        back_kernel,
        out_shape=[
            sds((1024, 768), BF), sds((1024, 768), F32), sds((1024, 768), F32),
            sds((24, 2304), F32), sds((24, 768), F32), sds((24, 3072), F32), sds((24, 3072), F32), sds((16, 128), F32),
        ],
        in_specs=[ANY] * 12 + [VM] * 4,
        out_specs=[ANY] * 3 + [VM] * 5,
        scratch_shapes=[
            vm((3, 32, 16, 3072), BF), vm((32, 16, 1152), BF), vm((32, 16, 128), BF),
            vm((3, 31, 16, 3072), BF), vm((31, 16, 1152), BF), vm((3, 31, 16, 1152), BF), vm((32, 16, 128), BF),
            vm((1024, 768), BF),
            vm((2, 2, 6, 2, 64, 128), BF), vm((2, 2, 6, 2, 64, 128), BF), vm((2, 2, 64, 768), BF), vm((2, 2, 64, 768), BF),
            vm((16, 1536), F32), vm((16, 768), F32),
            dma((8, 16)), dma((8, 16)), dma((28,)), dma((28,)), dma((14,)),
        ],
        compiler_params=pltpu.CompilerParams(collective_id=1, has_side_effects=True, vmem_limit_bytes=VMEM_LIMIT),
    )(*args)


def with_halo(x, sides, width):
    for axis, dim in sides:
        size, length = (lax.axis_size(axis), x.shape[dim])
        up = [(i, (i + 1) % size) for i in range(size - 1)]
        down = [(j, i) for i, j in up]
        last = lax.slice_in_dim(x, length - width, length, axis=dim)
        first = lax.slice_in_dim(x, 0, width, axis=dim)
        before = lax.ppermute(last, axis, up)
        after = lax.ppermute(first, axis, down)
        x = jnp.concatenate([before, x, after], axis=dim)
    return x


def layer_norm(inputs, norm_gain, norm_bias):
    middle = jnp.mean(inputs, axis=-1, keepdims=True)
    centred = inputs - middle
    spread = jnp.mean(centred * centred, axis=-1, keepdims=True)
    return centred * lax.rsqrt(spread + 1e-05) * norm_gain + norm_bias


def pool_local(extended, taps_in, seg_window):
    block_rows = extended.shape[0] - 2 * NEAR
    anchors = seg_window[REACH : REACH + block_rows : 4]
    pooled = jnp.zeros((block_rows // 4, extended.shape[1]), jnp.float32)
    for offset in range(5):
        start_row = NEAR - 2 + offset
        picked = extended[start_row : start_row + block_rows : 4]
        seg_start = REACH - 2 + offset
        same_doc = (seg_window[seg_start : seg_start + block_rows : 4] == anchors).astype(
            jnp.float32
        )
        pooled = pooled + taps_in[offset] * picked * same_doc[:, None]
    return pooled


def window_masks(seg_window, block_rows):
    seg_query = seg_window[REACH : REACH + block_rows]
    seg_key = seg_window[REACH - NEAR : REACH + block_rows + NEAR]
    seg_pool = seg_window[0 : block_rows + 2 * REACH : 4]
    q_index = jnp.arange(block_rows, dtype=jnp.int32)
    k_index = jnp.arange(seg_key.shape[0], dtype=jnp.int32)
    p_index = jnp.arange(seg_pool.shape[0], dtype=jnp.int32)
    near_mask = (jnp.abs(q_index[:, None] - k_index[None, :] + NEAR) <= NEAR) & (
        seg_query[:, None] == seg_key[None, :]
    )
    far_mask = (jnp.abs(4 * p_index[None, :] - REACH - q_index[:, None]) <= REACH) & (
        seg_query[:, None] == seg_pool[None, :]
    )
    return (near_mask, far_mask)


def scores_of(queries, near_keys, far_keys, near_mask, far_mask):
    score_scale = HEAD ** (-0.5)
    near_scores = (
        jnp.einsum("qhd,khd->hqk", queries, near_keys, preferred_element_type=jnp.float32)
        * score_scale
    )
    far_scores = (
        jnp.einsum("qhd,khd->hqk", queries, far_keys, preferred_element_type=jnp.float32)
        * score_scale
    )
    return (
        jnp.where(near_mask[None], near_scores, -1e30),
        jnp.where(far_mask[None], far_scores, -1e30),
    )


def normalise(near_scores, far_scores, near_mask, far_mask, row_max, row_total):
    near_prob = jnp.where(near_mask[None], jnp.exp(near_scores - row_max), 0.0) / row_total
    far_prob = jnp.where(far_mask[None], jnp.exp(far_scores - row_max), 0.0) / row_total
    return (near_prob, far_prob)


def add_rims(middle_part, rim_values, rim_width):
    extra = middle_part.shape[0] - rim_width
    return (
        middle_part
        + jnp.pad(rim_values[:rim_width], ((0, extra), (0, 0)))
        + jnp.pad(rim_values[-rim_width:], ((extra, 0), (0, 0)))
    )


def shards(
    tokens,
    segments,
    cotangent,
    ln1_gain,
    ln1_bias,
    w_qkv,
    pool_taps,
    w_out,
    ln2_gain,
    ln2_bias,
    w_up,
    w_down,
):
    block_rows = tokens.shape[1]
    model_width = tokens.shape[2]
    pool_half = REACH // 4
    score_scale = HEAD ** (-0.5)
    offset_tokens = lax.axis_index("seq") * block_rows
    outputs = []
    input_grads = []
    summed = None
    for micro_step in range(tokens.shape[0]):
        gathered = (
            lax.all_gather(ln1_gain, ("dp", "seq"), axis=0, tiled=True),
            lax.all_gather(ln1_bias, ("dp", "seq"), axis=0, tiled=True),
            lax.all_gather(w_qkv, ("dp", "seq"), axis=0, tiled=True),
            lax.all_gather(pool_taps, ("dp", "seq"), axis=1, tiled=True),
            lax.all_gather(w_out, ("dp", "seq"), axis=0, tiled=True),
            lax.all_gather(ln2_gain, ("dp", "seq"), axis=0, tiled=True),
            lax.all_gather(ln2_bias, ("dp", "seq"), axis=0, tiled=True),
            lax.all_gather(w_up, ("dp", "seq"), axis=0, tiled=True),
            lax.all_gather(w_down, ("dp", "seq"), axis=1, tiled=True),
        )
        gain_one, bias_one, proj_qkv, taps, proj_out, gain_two, bias_two, proj_up, proj_down = (
            gathered
        )
        seg_row = segments[micro_step]
        seg_padded = jnp.pad(seg_row, (REACH, REACH), constant_values=-1)
        seg_window = lax.dynamic_slice_in_dim(
            seg_padded, offset_tokens, block_rows + 2 * REACH, 0
        )
        near_mask, far_mask = window_masks(seg_window, block_rows)
        inputs = tokens[micro_step].astype(jnp.float32)
        gain_float = gain_one.astype(jnp.float32)
        bias_float = bias_one.astype(jnp.float32)
        gain_second = gain_two.astype(jnp.float32)
        bias_second = bias_two.astype(jnp.float32)
        normed = layer_norm(inputs, gain_float, bias_float).astype(jnp.bfloat16)
        projected = jnp.dot(normed, proj_qkv, preferred_element_type=jnp.float32).astype(
            jnp.bfloat16
        )
        queries = projected[:, :model_width].reshape(block_rows, HEADS, HEAD)
        key_value = projected[:, model_width:]
        extended = with_halo(key_value, (("seq", 0),), NEAR)
        ext_float = extended.astype(jnp.float32)
        taps_float = taps.astype(jnp.float32)
        pooled = pool_local(ext_float, taps_float, seg_window).astype(jnp.bfloat16)
        pool_ext = with_halo(pooled, (("seq", 0),), pool_half)
        near_keys = extended[:, :model_width].reshape(-1, HEADS, HEAD)
        near_values = extended[:, model_width:].reshape(-1, HEADS, HEAD)
        far_keys = pool_ext[:, :model_width].reshape(-1, HEADS, HEAD)
        far_values = pool_ext[:, model_width:].reshape(-1, HEADS, HEAD)
        near_scores, far_scores = scores_of(queries, near_keys, far_keys, near_mask, far_mask)
        row_max = jnp.maximum(
            jnp.max(near_scores, axis=2, keepdims=True), jnp.max(far_scores, axis=2, keepdims=True)
        )
        near_exp = jnp.where(near_mask[None], jnp.exp(near_scores - row_max), 0.0)
        far_exp = jnp.where(far_mask[None], jnp.exp(far_scores - row_max), 0.0)
        row_total = jnp.sum(near_exp, axis=2, keepdims=True) + jnp.sum(
            far_exp, axis=2, keepdims=True
        )
        near_low = (near_exp / row_total).astype(jnp.bfloat16)
        far_low = (far_exp / row_total).astype(jnp.bfloat16)
        mixed_sum = jnp.einsum(
            "hqk,khd->qhd", near_low, near_values, preferred_element_type=jnp.float32
        ) + jnp.einsum("hqk,khd->qhd", far_low, far_values, preferred_element_type=jnp.float32)
        attended = mixed_sum.reshape(block_rows, model_width).astype(jnp.bfloat16)
        branch = jnp.dot(attended, proj_out, preferred_element_type=jnp.float32)
        middle = inputs + branch
        normed_two = layer_norm(middle, gain_second, bias_second).astype(jnp.bfloat16)
        upward = jnp.dot(normed_two, proj_up, preferred_element_type=jnp.float32)
        activated = jax.nn.gelu(upward).astype(jnp.bfloat16)
        result = middle + jnp.dot(activated, proj_down, preferred_element_type=jnp.float32)
        outputs.append(result.astype(jnp.bfloat16))
        regathered = (
            lax.all_gather(ln1_gain, ("dp", "seq"), axis=0, tiled=True),
            lax.all_gather(ln1_bias, ("dp", "seq"), axis=0, tiled=True),
            lax.all_gather(w_qkv, ("dp", "seq"), axis=0, tiled=True),
            lax.all_gather(pool_taps, ("dp", "seq"), axis=1, tiled=True),
            lax.all_gather(w_out, ("dp", "seq"), axis=0, tiled=True),
            lax.all_gather(ln2_gain, ("dp", "seq"), axis=0, tiled=True),
            lax.all_gather(ln2_bias, ("dp", "seq"), axis=0, tiled=True),
            lax.all_gather(w_up, ("dp", "seq"), axis=0, tiled=True),
            lax.all_gather(w_down, ("dp", "seq"), axis=1, tiled=True),
        )
        back_qkv = regathered[2]
        back_out = regathered[4]
        back_up = regathered[7]
        back_down = regathered[8]
        grad_out = cotangent[micro_step]
        grad_act = jnp.dot(grad_out, back_down.T, preferred_element_type=jnp.float32)
        grad_down = jnp.dot(activated.T, grad_out, preferred_element_type=jnp.float32)
        gelu_value, gelu_back = jax.vjp(jax.nn.gelu, upward)
        grad_upin = gelu_back(grad_act)[0].astype(jnp.bfloat16)
        grad_upw = jnp.dot(normed_two.T, grad_upin, preferred_element_type=jnp.float32)
        grad_normed_two = jnp.dot(grad_upin, back_up.T, preferred_element_type=jnp.float32)
        norm_value_two, norm_back_two = jax.vjp(layer_norm, middle, gain_second, bias_second)
        grad_mid_part, grad_gain_two, grad_bias_two = norm_back_two(grad_normed_two)
        grad_middle = grad_out.astype(jnp.float32) + grad_mid_part
        grad_branch = grad_middle.astype(jnp.bfloat16)
        grad_outw = jnp.dot(attended.T, grad_branch, preferred_element_type=jnp.float32)
        grad_mixed = (
            jnp.dot(grad_branch, back_out.T, preferred_element_type=jnp.float32)
            .astype(jnp.bfloat16)
            .reshape(block_rows, HEADS, HEAD)
        )
        near_scores, far_scores = scores_of(queries, near_keys, far_keys, near_mask, far_mask)
        near_prob, far_prob = normalise(
            near_scores, far_scores, near_mask, far_mask, row_max, row_total
        )
        near_low = near_prob.astype(jnp.bfloat16)
        far_low = far_prob.astype(jnp.bfloat16)
        grad_near_values = jnp.einsum(
            "hqk,qhd->khd", near_low, grad_mixed, preferred_element_type=jnp.float32
        )
        grad_far_values = jnp.einsum(
            "hqk,qhd->khd", far_low, grad_mixed, preferred_element_type=jnp.float32
        )
        grad_near_prob = jnp.einsum(
            "qhd,khd->hqk", grad_mixed, near_values, preferred_element_type=jnp.float32
        )
        grad_far_prob = jnp.einsum(
            "qhd,khd->hqk", grad_mixed, far_values, preferred_element_type=jnp.float32
        )
        row_delta = jnp.sum(near_prob * grad_near_prob, axis=2, keepdims=True) + jnp.sum(
            far_prob * grad_far_prob, axis=2, keepdims=True
        )
        grad_near_scores = (near_prob * (grad_near_prob - row_delta)).astype(jnp.bfloat16)
        grad_far_scores = (far_prob * (grad_far_prob - row_delta)).astype(jnp.bfloat16)
        grad_queries = (
            jnp.einsum(
                "hqk,khd->qhd", grad_near_scores, near_keys, preferred_element_type=jnp.float32
            )
            + jnp.einsum(
                "hqk,khd->qhd", grad_far_scores, far_keys, preferred_element_type=jnp.float32
            )
        ) * score_scale
        grad_near_keys = (
            jnp.einsum(
                "hqk,qhd->khd", grad_near_scores, queries, preferred_element_type=jnp.float32
            )
            * score_scale
        )
        grad_far_keys = (
            jnp.einsum("hqk,qhd->khd", grad_far_scores, queries, preferred_element_type=jnp.float32)
            * score_scale
        )
        grad_extended = jnp.concatenate(
            [grad_near_keys.reshape(-1, model_width), grad_near_values.reshape(-1, model_width)],
            axis=1,
        )
        grad_pool_ext = jnp.concatenate(
            [grad_far_keys.reshape(-1, model_width), grad_far_values.reshape(-1, model_width)],
            axis=1,
        )
        pool_edges = jnp.concatenate(
            [grad_pool_ext[:pool_half], grad_pool_ext[-pool_half:]], axis=0
        )
        pool_returned = with_halo(pool_edges.astype(jnp.bfloat16), (("seq", 0),), pool_half).astype(
            pool_edges.dtype
        )
        grad_pooled = add_rims(grad_pool_ext[pool_half:-pool_half], pool_returned, pool_half)
        pool_value, pool_back = jax.vjp(
            lambda ext_in, taps_part: pool_local(ext_in, taps_part, seg_window),
            ext_float,
            taps_float,
        )
        grad_ext_pool, grad_taps = pool_back(grad_pooled)
        grad_extended = grad_extended + grad_ext_pool
        token_edges = jnp.concatenate(
            [grad_extended[:NEAR], grad_extended[-NEAR:]], axis=0
        )
        token_returned = with_halo(
            token_edges.astype(jnp.bfloat16), (("seq", 0),), NEAR
        ).astype(token_edges.dtype)
        grad_kv = add_rims(grad_extended[NEAR:-NEAR], token_returned, NEAR)
        grad_projected = jnp.concatenate(
            [grad_queries.reshape(block_rows, model_width), grad_kv], axis=1
        ).astype(jnp.bfloat16)
        grad_qkvw = jnp.dot(normed.T, grad_projected, preferred_element_type=jnp.float32)
        grad_normed = jnp.dot(grad_projected, back_qkv.T, preferred_element_type=jnp.float32)
        norm_value_one, norm_back_one = jax.vjp(layer_norm, inputs, gain_float, bias_float)
        grad_in_part, grad_gain_one, grad_bias_one = norm_back_one(grad_normed)
        input_grads.append(grad_middle + grad_in_part)
        shares = (
            lax.psum_scatter(grad_gain_one, ("dp", "seq"), scatter_dimension=0, tiled=True),
            lax.psum_scatter(grad_bias_one, ("dp", "seq"), scatter_dimension=0, tiled=True),
            lax.psum_scatter(grad_qkvw, ("dp", "seq"), scatter_dimension=0, tiled=True),
            lax.psum_scatter(grad_taps, ("dp", "seq"), scatter_dimension=1, tiled=True),
            lax.psum_scatter(grad_outw, ("dp", "seq"), scatter_dimension=0, tiled=True),
            lax.psum_scatter(grad_gain_two, ("dp", "seq"), scatter_dimension=0, tiled=True),
            lax.psum_scatter(grad_bias_two, ("dp", "seq"), scatter_dimension=0, tiled=True),
            lax.psum_scatter(grad_upw, ("dp", "seq"), scatter_dimension=0, tiled=True),
            lax.psum_scatter(grad_down, ("dp", "seq"), scatter_dimension=1, tiled=True),
        )
        if summed is None:
            summed = shares
        else:
            summed = jax.tree.map(jnp.add, summed, shares)
    return (
        jnp.stack(outputs),
        jnp.stack(input_grads),
        summed[0],
        summed[1],
        summed[2],
        summed[3],
        summed[4],
        summed[5],
        summed[6],
        summed[7],
        summed[8],
    )


def chained(
    tokens, segments, cotangent, ln1_gain, ln1_bias, w_qkv, pool_taps, w_out, ln2_gain, ln2_bias, w_up, w_down,
):
    small = small_share(pool_taps, ln1_gain, ln1_bias, ln2_gain, ln2_bias)
    wq, wo, wu, wd, taps, gains, h1, q, kv, pe, att, bias, lse, same = front(
        tokens, segments, w_qkv, w_out, w_up, w_down.T, small
    )
    flat, split = (1024, 768), (2, 512, 768)
    out, _, g_in, g_wq, g_wo, g_wu, g_wd, g_small = back_part(
        tokens.reshape(flat), att.reshape(flat), cotangent.reshape(flat), wo, wu, wd,
        q, kv, pe, bias, h1, wq, taps, gains, same, lse,
    )
    return (
        out.reshape(split), g_in.reshape(split), g_small[5, :24], g_small[6, :24], g_wq, g_small[0:5, :48], g_wo,
        g_small[7, :24], g_small[8, :24], g_wu, g_wd.T,
    )


def solution(mesh):
    both = ("dp", "seq")
    row, tok, first, second = P(both), P("dp", "seq", None), P(both, None), P(None, both)
    small_mesh = mesh.shape["dp"] == 2 and mesh.shape["seq"] == 16
    return jax.shard_map(
        chained if small_mesh else shards,
        mesh=mesh,
        in_specs=(tok, P("dp", None), tok, row, row, first, second, first, row, row, first, second),
        out_specs=(tok, tok, row, row, first, second, first, row, row, first, second),
        check_vma=False,
    )
```

```python
import functools

import jax
import jax.numpy as jnp
from jax import lax
from jax.experimental import pallas as pl
from jax.experimental.pallas import tpu as pltpu
from jax.sharding import PartitionSpec as P

HEADS = 12
HEAD = 64
NEAR = 64
REACH = 256
F32, BF = jnp.float32, jnp.bfloat16
NT = (((1,), (1,)), ((), ()))
TN = (((0,), (0,)), ((), ()))
NN = (((1,), (0,)), ((), ()))
MESH = pl.DeviceIdType.MESH
ANY = pl.BlockSpec(memory_space=pl.ANY)
VM = pl.BlockSpec(memory_space=pltpu.VMEM)
VMEM_LIMIT = 63 * 2**20
UNIT = 384
CLS = 3456
WIDE = 3584
PLACE = {"qkv": (0, 0, 2304), "out": (1, 0, 768), "up": (1, 3, 3072), "down": (1, 15, 3072)}


def dg(a, b, dims):
    return lax.dot_general(a, b, dims, preferred_element_type=F32)


def spot(name, unit):
    first, start, _ = PLACE[name]
    at = start + unit
    return first + at // 9, (at % 9) * UNIT


def units(name):
    return PLACE[name][2] // UNIT


def where_am_i():
    c = lax.axis_index("dp")
    s = lax.axis_index("seq")
    z, col = s // 4, s % 4
    x, y = col % 2, col // 2
    colx, coly, cold = y * 2 + (1 - x), (1 - y) * 2 + x, 3 - col
    return dict(
        c=c, s=s, z=z, col=col, colx=colx, coly=coly, cold=cold,
        px=(c, z * 4 + colx), py=(c, z * 4 + coly), pd=(1 - c, s),
    )


def greet(me):
    bar = pltpu.get_barrier_semaphore()
    who = [me["px"], me["py"], me["pd"]]
    who += [(me["c"], lax.rem(me["z"] + j, 4) * 4 + me["col"]) for j in (1, 2, 3)]
    for dev in who:
        pl.semaphore_signal(bar, inc=1, device_id=dev, device_id_type=MESH)
    last = lax.axis_size("seq") - 1

    @pl.when(me["s"] > 0)
    def _():
        pl.semaphore_signal(bar, inc=1, device_id=(me["c"], me["s"] - 1), device_id_type=MESH)

    @pl.when(me["s"] < last)
    def _():
        pl.semaphore_signal(bar, inc=1, device_id=(me["c"], me["s"] + 1), device_id_type=MESH)

    return 6 + (me["s"] > 0).astype(jnp.int32) + (me["s"] < last).astype(jnp.int32)


def all_here(count):
    pl.semaphore_wait(pltpu.get_barrier_semaphore(), count)


def greet_all(me):
    bar = pltpu.get_barrier_semaphore()
    pl.semaphore_signal(bar, inc=1, device_id=me["pd"], device_id_type=MESH)
    for d in range(1, 16):
        pl.semaphore_signal(bar, inc=1, device_id=(me["c"], lax.rem(me["s"] + d, 16)), device_id_type=MESH)


def lane_low():
    return lax.broadcasted_iota(jnp.int32, (128, 128), 1) < HEAD


def pair_rows(v):
    low = lane_low()
    zero = jnp.zeros_like(v)
    return jnp.concatenate([jnp.where(low, v, zero), jnp.where(low, zero, v)], axis=0)


def pair_out(t):
    return jnp.concatenate([t[:HEAD, :128], t[HEAD:, 128:]], axis=0).T


def softmax_block(q2, kn, kf, bias):
    st = jnp.concatenate([dg(kn, q2, NT), dg(kf, q2, NT)], axis=0)
    st = st + jnp.concatenate([bias, bias], axis=1)
    top = jnp.max(st, axis=0, keepdims=True)
    e = jnp.exp(st - top)
    total = jnp.sum(e, axis=0, keepdims=True)
    return e, 1.0 / total, top + jnp.log(total)


def fill_window(seg, winr, wcol, has_left, has_right, s):
    length, block = seg.shape[1], 512
    left = pl.multiple_of(jnp.maximum(s * block - REACH, 0), REACH)
    right = pl.multiple_of(jnp.minimum(s * block + block, length - REACH), REACH)
    before = seg[:, pl.ds(left, REACH)].astype(F32)
    after = seg[:, pl.ds(right, REACH)].astype(F32)
    winr[:, 0:REACH] = jnp.where(has_left, before, -1.0)
    winr[:, REACH : REACH + block] = seg[:, pl.ds(pl.multiple_of(s * block, block), block)].astype(F32)
    winr[:, REACH + block :] = jnp.where(has_right, after, -1.0)
    for r in range(2):
        for t in range(8):
            row = winr[r : r + 1, t * 128 : t * 128 + 128]
            wcol[r, t * 128 : t * 128 + 128] = jnp.broadcast_to(row, (128, 128)).T


def fill_masks(winr, wcol, bias, same):
    kk = lax.broadcasted_iota(jnp.int32, (256, 128), 0)
    ii = lax.broadcasted_iota(jnp.int32, (256, 128), 1)
    pp = lax.broadcasted_iota(jnp.int32, (160, 128), 0)
    qi = lax.broadcasted_iota(jnp.int32, (160, 128), 1)
    close = jnp.abs(kk - NEAR - ii) <= NEAR
    reach = jnp.abs(4 * pp - REACH - qi) <= REACH
    for r in range(2):
        for b in range(4):
            seg_q = winr[r : r + 1, 256 + 128 * b : 384 + 128 * b]
            near = close & (wcol[r, 192 + 128 * b : 448 + 128 * b] == seg_q)
            far = reach & (wcol[r, pl.ds(128 * b, 160, stride=4), :] == seg_q)
            bias[r * 4 + b, 0:256] = jnp.where(near, 0.0, -1e30)
            bias[r * 4 + b, 256:416] = jnp.where(far, 0.0, -1e30)
        anchor = wcol[r, pl.ds(REACH, 128, stride=4), :]
        for t in range(5):
            hit = wcol[r, pl.ds(REACH - 2 + t, 128, stride=4), :] == anchor
            same[r, t] = jnp.where(hit, 1.0, 0.0).astype(BF)


def head_lanes(h):
    return (
        pl.ds(pl.multiple_of(h * 128, 128), 128),
        pl.ds(pl.multiple_of(768 + h * 128, 128), 128),
    )


def attend(q, kv, pe, bias, att, lse, r, h):
    kl, vl = head_lanes(h)
    for b in range(4):
        n, f, i = slice(b * 128, b * 128 + 256), slice(b * 32, b * 32 + 160), slice(b * 128, b * 128 + 128)
        e, rt, lse[r * 6 + h, b : b + 1] = softmax_block(
            pair_rows(q[r, i, kl]), kv[r, n, kl], pe[r, f, kl], bias[r * 4 + b]
        )
        low = (e * rt).astype(BF)
        values = jnp.concatenate([kv[r, n, vl], pe[r, f, vl]], axis=0)
        att[r, i, kl] = pair_out(dg(values, low, TN)).astype(BF)


def attend_back(q, kv, pe, bias, lse, delta, g, gext, dkv, dpe, r, h):
    kl, vl = head_lanes(h)
    for part in (h, 6 + h):
        dkv[r, part] = jnp.zeros((640, 128), F32)
        dpe[r, part] = jnp.zeros((256, 128), F32)
    for b in range(4):
        n, f, i = slice(b * 128, b * 128 + 256), slice(b * 32, b * 32 + 160), slice(b * 128, b * 128 + 128)
        q2, g2 = pair_rows(q[r, i, kl]), pair_rows(g[r * 512 + b * 128 : r * 512 + b * 128 + 128, kl])
        kn, vn, kf, vf = kv[r, n, kl], kv[r, n, vl], pe[r, f, kl], pe[r, f, vl]
        st = jnp.concatenate([dg(kn, q2, NT), dg(kf, q2, NT)], axis=0) - lse[r * 6 + h, b : b + 1]
        p = jnp.exp(st + jnp.concatenate([bias[r * 4 + b], bias[r * 4 + b]], axis=1))
        dp = jnp.concatenate([dg(vn, g2, NT), dg(vf, g2, NT)], axis=0)
        at = slice(r * 512 + b * 128, r * 512 + b * 128 + 128)
        ds = (p * (dp - jnp.concatenate([delta[h, 0:1, at], delta[h, 1:2, at]], axis=1))).astype(BF)
        low = p.astype(BF)
        dv, dk = dg(low, g2, NN), dg(ds, q2, NN)
        dkv[r, h, n] += dk[:256]
        dkv[r, 6 + h, n] += dv[:256]
        dpe[r, h, f] += dk[256:]
        dpe[r, 6 + h, f] += dv[256:]
        dqt = dg(jnp.concatenate([kn, kf], axis=0), ds, TN)
        gext[r * 640 + 64 + b * 128 : r * 640 + 192 + b * 128, kl] = (pair_out(dqt) * HEAD**-0.5).astype(BF)


def norm_parts(v):
    mean = jnp.mean(v, axis=-1, keepdims=True)
    cen = v - mean
    var = jnp.mean(cen * cen, axis=-1, keepdims=True)
    rs = lax.rsqrt(var + 1e-05)
    return cen * rs, rs


LAST = 29


def pack_own(grab, put):
    for name in ("qkv", "out", "up", "down"):
        half = units(name) // 2
        for u in range(units(name)):
            k, lo = spot(name, u)
            put(k, lo, grab(name, 0, 16, u))
        for u in range(half):
            k, lo = spot(name, units(name) + u)
            put(k, lo, jnp.concatenate([grab(name, 16, 24, u), grab(name, 16, 24, u + half)], axis=0))


def hidden_place(n):
    half, r = divmod(n, 1536)
    return (r // 256) * 512 + half * 256 + r % 256


def unpack(name, got, dst):
    half = units(name) // 2

    def pair(p, carry):
        rows = pl.ds(pl.multiple_of(48 * p, 16), 48)
        for u in range(units(name)):
            k, lo = spot(name, u)
            kt, lt = spot(name, units(name) + u % half)
            cut = slice(0, 8) if u < half else slice(8, 16)
            hidden = name in ("up", "down")
            for i in range(0, UNIT, 128) if hidden else (0,):
                n = 128 if hidden else UNIT
                to = hidden_place(u * UNIT + i) if hidden else u * UNIT
                parts = []
                for j in (0, 1):
                    parts.append(got[k, 2 * p + j, :, lo + i : lo + i + n])
                    parts.append(got[kt, 2 * p + j, :, lt + i : lt + i + n][cut])
                dst[rows, to : to + n] = jnp.concatenate(parts, axis=0)
        return carry

    lax.fori_loop(0, 16, pair, 0)


def spread_small(got, taps, gains):
    lane = lax.broadcasted_iota(jnp.int32, (16, 128), 1)

    def place(width, tiles):
        acc = [jnp.zeros((16, 128), F32) for _ in range(tiles)]
        for s in range(32):
            at, off = divmod(width * s, 128)
            v = jnp.where(lane < width, got[0, s, :, CLS:WIDE].astype(F32), 0.0)
            v = pltpu.roll(v, off, 1) if off else v
            acc[at] = acc[at] + jnp.where(lane >= off, v, 0.0)
            if off + width > 128:
                acc[at + 1] = acc[at + 1] + jnp.where(lane < off, v, 0.0)
        return acc

    for i, v in enumerate(place(48, 12)):
        taps[:, i * 128 : (i + 1) * 128] = v
    for i, v in enumerate(place(24, 6)):
        gains[:, i * 128 : (i + 1) * 128] = v


def front_kernel(
    tok, seg, wq, wo, wu, wd, small,
    o_wq, o_wo, o_wu, o_wd, o_taps, o_gains, o_h1, o_q, o_kv, o_pe, o_att, o_bias, o_lse, o_same,
    G, Wq, Wo, Wu, Wd, taps, gains, xe, h1, q, kv, pe, att, bias, lse, same, chunk, winr, wcol,
    send_x, send_y, send_d, send_z, send_g, recv, hsend, hrecv, local,
):
    me = where_am_i()
    c, s, z, col = me["c"], me["s"], me["z"], me["col"]
    mine = c * 16 + s
    last = lax.axis_size("seq") - 1
    has_left, has_right = s > 0, s < last

    def cols(k):
        return WIDE if isinstance(k, int) and k == 0 else CLS

    def hop(k, slot, to, sem):
        part = G.at[k, slot, :, pl.ds(0, cols(k))]
        return pltpu.make_async_remote_copy(
            src_ref=part, dst_ref=part, send_sem=sem, recv_sem=recv.at[k, slot],
            device_id=to, device_id_type=MESH,
        )

    def to_x(k, at):
        return hop(k, c * 16 + at, me["px"], send_x.at[k, at])

    def to_y(k, at):
        return hop(k, c * 16 + at, me["py"], send_y.at[k, at])

    def to_d(k, at):
        return hop(k, c * 16 + at, me["pd"], send_d.at[k, at])

    def to_z(k, j):
        return hop(k, mine, (c, lax.rem(z + j, 4) * 4 + col), send_z.at[k, j - 1])

    def by_y(k, zz):
        return zz != 3

    def to_g(k, zz):
        over_y = by_y(k, zz)
        at = zz * 4 + jnp.where(over_y, me["colx"], me["coly"])
        to = (c, z * 4 + jnp.where(over_y, me["coly"], me["colx"]))
        return hop(k, c * 16 + at, to, send_g.at[k, zz])

    def got(k, slot):
        hop(k, slot, me["px"], send_x.at[k, 0]).wait_recv()

    def own(k):
        for j in (1, 2, 3):
            to_z(k, j).start()
        to_x(k, s).start()
        to_y(k, s).start()
        to_d(k, s).start()

    def column(k, j):
        at = lax.rem(z + j, 4) * 4 + col
        got(k, c * 16 + at)
        to_x(k, at).start()
        to_y(k, at).start()
        to_d(k, at).start()

    def plane(k, j):
        zz = lax.rem(z + j, 4)
        got(k, c * 16 + zz * 4 + me["colx"])
        to_d(k, zz * 4 + me["colx"]).start()
        got(k, c * 16 + zz * 4 + me["coly"])
        to_d(k, zz * 4 + me["coly"]).start()
        to_g(k, zz).start()

    def diag(k, j):
        at = lax.rem(z + j, 4) * 4 + me["cold"]
        got(k, c * 16 + at)
        to_d(k, at).start()

    def event(e):
        k, i = e // 11 + 1, lax.rem(e, 11)

        @pl.when(i < 4)
        def _():
            plane(k, i)

        @pl.when((i >= 4) & (i < 7) & (k < 3))
        def _():
            column(k + 1, i - 3)

        @pl.when(i >= 7)
        def _():
            diag(k, i - 7)

    def halo_tok(r, right):
        src = tok.at[r, pl.ds(448 if right else 0, 64)]
        dst = xe.at[r, pl.ds(0 if right else 576, 64)]
        i = r * 2 + int(right)
        return pltpu.make_async_remote_copy(
            src_ref=src, dst_ref=dst, send_sem=hsend.at[i], recv_sem=hrecv.at[i],
            device_id=(c, s + 1 if right else s - 1), device_id_type=MESH,
        )

    def halo_pool(r, right):
        src = pe.at[r, pl.ds(128 if right else 64, 64)]
        dst = pe.at[r, pl.ds(0 if right else 192, 64)]
        i = 4 + r * 2 + int(right)
        return pltpu.make_async_remote_copy(
            src_ref=src, dst_ref=dst, send_sem=hsend.at[i], recv_sem=hrecv.at[i],
            device_id=(c, s + 1 if right else s - 1), device_id_type=MESH,
        )

    def both(make, r, act):
        @pl.when(has_right)
        def _():
            act(make(r, True), True)

        @pl.when(has_left)
        def _():
            act(make(r, False), False)

    def arrived(make, r):
        @pl.when(has_left)
        def _():
            make(r, True).wait_recv()

        @pl.when(has_right)
        def _():
            make(r, False).wait_recv()

    expected = greet(me)
    load = [pltpu.make_async_copy(tok.at[r], xe.at[r, pl.ds(64, 512)], local.at[r]) for r in range(2)]
    for copy in load:
        copy.start()
    shares = {"qkv": wq, "out": wo, "up": wu, "down": wd}

    def grab(name, a, b, u):
        return shares[name][a:b, u * UNIT : (u + 1) * UNIT]

    def put(k, lo, v):
        G[k, mine, :, lo : lo + UNIT] = v

    pack_own(grab, put)
    G[0, mine, :, CLS:WIDE] = small[...]

    @pl.when(jnp.logical_not(has_left))
    def _():
        for r in range(2):
            xe[r, 0:64] = jnp.zeros((64, 768), BF)
            pe[r, 0:64] = jnp.zeros((64, 1536), BF)

    @pl.when(jnp.logical_not(has_right))
    def _():
        for r in range(2):
            xe[r, 576:640] = jnp.zeros((64, 768), BF)
            pe[r, 192:256] = jnp.zeros((64, 1536), BF)

    lse[...] = jnp.zeros((12, 8, 256), F32)
    all_here(expected)
    own(0)
    for r in range(2):
        both(halo_tok, r, lambda copy, right: copy.start())
    own(1)
    own(2)
    fill_window(seg, winr, wcol, has_left, has_right, s)
    fill_masks(winr, wcol, bias, same)
    for j in (1, 2, 3):
        column(0, j)
    for j in range(4):
        plane(0, j)
    own(3)
    for j in (1, 2, 3):
        column(1, j)
    for j in range(4):
        diag(0, j)

    def other(k):
        def body(i, carry):
            got(k, (1 - c) * 16 + i)
            return carry

        lax.fori_loop(0, 16, body, 0)

    other(0)
    unpack("qkv", G, Wq)
    spread_small(G, taps, gains)
    outs = [
        pltpu.make_async_copy(a, b, local.at[2 + i])
        for i, (a, b) in enumerate(
            [(Wq, o_wq), (taps, o_taps), (gains, o_gains), (h1, o_h1), (q, o_q), (kv, o_kv), (pe, o_pe),
             (att, o_att), (bias, o_bias), (Wo, o_wo), (Wu, o_wu), (Wd, o_wd), (lse, o_lse), (same, o_same)]
        )
    ]
    for i in (0, 1, 2, 8, 13):
        outs[i].start()
    for copy in load:
        copy.wait()
    for r in range(2):
        arrived(halo_tok, r)

    for r in range(2):
        def norm_rows(i, carry):
            rows = pl.ds(pl.multiple_of(i * 128, 128), 128)
            n, _ = norm_parts(xe[r, rows].astype(F32))
            h1[r, rows] = (n * gains[5:6] + gains[6:7]).astype(BF)
            return carry

        lax.fori_loop(0, 5, norm_rows, 0)
    outs[3].start()

    for r in range(2):
        def queries(j, carry):
            lanes = pl.ds(pl.multiple_of(j * 256, 256), 256)
            v = dg(h1[r, 64:576], Wq[:, lanes], NN)
            q[r, :, lanes] = v.astype(BF) * jnp.asarray(HEAD**-0.5, BF)
            return carry

        lax.fori_loop(0, 3, queries, 0)
        def keys(j, carry):
            event(r * 6 + j)
            lanes = pl.ds(pl.multiple_of(j * 128, 128), 128)
            from_lanes = pl.ds(pl.multiple_of(768 + j * 256, 256), 256)
            to_lanes = pl.ds(pl.multiple_of(j * 256, 256), 256)
            v = dg(h1[r], Wq[:, from_lanes], NN).astype(BF)
            kv[r, :, to_lanes] = v
            chunk[0] = v[:, :128].astype(F32)
            chunk[1] = v[:, 128:].astype(F32)
            for half in range(2):
                hl = pl.ds(pl.multiple_of(j * 256 + half * 128, 128), 128)
                acc = jnp.zeros((128, 128), F32)
                for t in range(5):
                    acc = acc + taps[t : t + 1, hl] * chunk[half, pl.ds(62 + t, 128, stride=4), :] * same[r, t].astype(F32)
                pe[r, 64:192, hl] = acc.astype(BF)
            return carry

        lax.fori_loop(0, 6, keys, 0)
        both(halo_pool, r, lambda copy, right: copy.start())
    outs[4].start()
    outs[5].start()
    for r in range(2):
        arrived(halo_pool, r)

        def heads_event(h, carry):
            attend(q, kv, pe, bias, att, lse, r, h)
            base = 12 + (r * 6 + h) * 2

            @pl.when(base < LAST)
            def _():
                event(base)

            @pl.when(base + 1 < LAST)
            def _():
                event(base + 1)

            return carry

        lax.fori_loop(0, 6, heads_event, 0)
    outs[6].start()
    outs[7].start()
    outs[12].start()
    for k in (1, 2):
        other(k)
    finish = (("out", Wo), ("up", Wu), ("down", Wd))
    for i in range(2):
        unpack(finish[i][0], G, finish[i][1])
        outs[9 + i].start()
    lax.fori_loop(LAST, 33, lambda e, carry: (event(e), carry)[1], 0)
    other(3)
    unpack("down", G, Wd)
    outs[11].start()
    for r in range(2):
        both(halo_tok, r, lambda copy, right: copy.wait_send())
        both(halo_pool, r, lambda copy, right: copy.wait_send())
    for k in range(4):
        def done(i, carry):
            to_x(k, i * 4 + col).wait_send()
            to_y(k, i * 4 + col).wait_send()
            to_g(k, i).wait_send()
            for j in range(4):
                to_d(k, i * 4 + j).wait_send()
            return carry

        lax.fori_loop(0, 4, done, 0)
        for j in (1, 2, 3):
            to_z(k, j).wait_send()
    for copy in outs:
        copy.wait()


def front(tok, seg, wq, wo, wu, wd, small):
    sds = jax.ShapeDtypeStruct
    shapes = [
        ((768, 2304), BF), ((768, 768), BF), ((768, 3072), BF), ((768, 3072), BF),
        ((16, 1536), F32), ((16, 768), F32),
        ((2, 640, 768), BF), ((2, 512, 768), BF), ((2, 640, 1536), BF), ((2, 256, 1536), BF),
        ((2, 512, 768), BF), ((8, 416, 128), F32), ((12, 8, 256), F32),
        ((2, 5, 128, 128), BF),
    ]
    scratch = [pltpu.VMEM((4, 32, 16, WIDE), BF)]
    scratch += [pltpu.VMEM(sh, dt) for sh, dt in shapes[:6]]
    scratch += [pltpu.VMEM((2, 640, 768), BF)]
    scratch += [pltpu.VMEM(sh, dt) for sh, dt in shapes[6:]]
    scratch += [pltpu.VMEM((2, 640, 128), F32), pltpu.VMEM((2, 1024), F32), pltpu.VMEM((2, 1024, 128), F32)]
    dma = pltpu.SemaphoreType.DMA
    scratch += [dma((4, 16)), dma((4, 16)), dma((4, 16)), dma((4, 3)), dma((4, 4)), dma((4, 32)), dma((8,)), dma((8,)), dma((16,))]
    return pl.pallas_call(
        front_kernel,
        out_shape=[sds(sh, dt) for sh, dt in shapes],
        in_specs=[ANY] + [VM] * 6,
        out_specs=[ANY] * len(shapes),
        scratch_shapes=scratch,
        compiler_params=pltpu.CompilerParams(collective_id=0, has_side_effects=True, vmem_limit_bytes=VMEM_LIMIT),
    )(tok, seg, wq, wo, wu, wd, small)


def small_share(pool_taps, ln1_gain, ln1_bias, ln2_gain, ln2_bias):
    rows = jnp.stack([ln1_gain, ln1_bias, ln2_gain, ln2_bias])
    return jnp.concatenate(
        [jnp.pad(pool_taps, ((0, 0), (0, 80))), jnp.pad(rows, ((0, 7), (0, 104)))], axis=0
    )


def gelu_both(u):
    a, b = 0.7978845608028654, 0.044715
    sq = u * u
    t = jnp.tanh(a * u * (1.0 + b * sq))
    half = 0.5 + 0.5 * t
    grad = half + 0.5 * u * (1.0 - t * t) * (a + (3.0 * a * b) * sq)
    return u * half, grad


def pack_pair(lo, hi):
    return jnp.concatenate([lo, hi], axis=0).astype(BF)


def pick_small(tg, lg, put):
    lane = lax.broadcasted_iota(jnp.int32, (16, 128), 1)

    def part(src, width, s):
        at, off = divmod(width * s, 128)
        v = src[:, at * 128 : at * 128 + 128]
        v = pltpu.roll(v, 128 - off, 1) if off else v
        if off + width > 128:
            w = pltpu.roll(src[:, at * 128 + 128 : at * 128 + 256], 128 - off, 1)
            v = jnp.where(lane < 128 - off, v, w)
        return jnp.where(lane < width, v, 0.0)

    for s in range(32):
        put(s, (part(tg, 48, s) + part(lg, 24, s)).astype(BF))


def back_kernel(
    tok_in, att_in, dy_in, wo_in, wu_in, wd_in,
    q_in, kv_in, pe_in, bias_in, h1_in, wq_in, taps, gains, same, lse,
    o_out, o_gmid, o_in, o_wq, o_wo, o_wu, o_wd, o_small,
    Sf, So, Ss, Rf, Ro, Rq, Rs, gatt, delta, pstage, precv, hstage, hrecv, tg, lg,
    send, recv, psend, prsem, local,
):
    me = where_am_i()
    greet_all(me)
    c, s, z, col = me["c"], me["s"], me["z"], me["col"]
    has_left, has_right = s > 0, s < lax.axis_size("seq") - 1

    def copy(i, a, b):
        return pltpu.make_async_copy(a, b, local.at[i])

    late = []

    def cls(k):
        if k < 3:
            return Sf.at[k, pl.ds(c * 16, 16)], Rf.at[k]
        if k == 3:
            return So.at[pl.ds(c * 16, 16)], Ro
        if k < 7:
            return late[0].at[k - 4, pl.ds(c * 16, 16)], Rq.at[k - 4]
        return Ss.at[pl.ds(c * 16, 16)], Rs

    def other(k):
        start = (1 - c) * 16
        if k < 3:
            return Sf.at[k, pl.ds(start, 16)]
        if k == 3 or k == 7:
            return (So if k == 3 else Ss).at[pl.ds(start, 16)]
        return late[0].at[k - 4, pl.ds(start, 16)]

    def remote(k, src, slot, i, to):
        return pltpu.make_async_remote_copy(
            src_ref=src, dst_ref=slot, send_sem=send.at[k, i], recv_sem=recv.at[k, i],
            device_id=to, device_id_type=MESH,
        )

    def swap(k):
        return remote(k, other(k), cls(k)[1].at[pl.ds(0, 16)], 0, me["pd"])

    def step_g(k, zz):
        S, R = cls(k)
        to = me["px"] if zz == 0 else me["py"]
        return remote(k, S.at[zz * 4 + me["cold"]], R.at[16 + zz], 1 + zz, to)

    def step_x(k, zz):
        S, R = cls(k)
        return remote(k, S.at[zz * 4 + me["colx"]], R.at[20 + zz], 5 + zz, me["px"])

    def step_y(k, zz):
        S, R = cls(k)
        return remote(k, S.at[zz * 4 + me["coly"]], R.at[24 + zz], 9 + zz, me["py"])

    def step_z(k, j):
        S, R = cls(k)
        zz = lax.rem(z + j, 4)
        return remote(k, S.at[zz * 4 + col], R.at[27 + j], 12 + j, (c, zz * 4 + col))

    def add(k, at, slots):
        S, R = cls(k)
        v = S[at].astype(F32) + R[at].astype(F32)
        for slot in slots:
            v = v + R[slot].astype(F32)
        return v

    def begin(k):
        swap(k).start()

    def do_g(k, zz):
        if zz == 0:
            swap(k).wait_recv()
        at = zz * 4 + me["cold"]
        cls(k)[0][at] = add(k, at, []).astype(BF)
        step_g(k, zz).start()

    def do_p(k, zz):
        step_g(k, zz).wait_recv()
        even = zz == 0
        for at, step, has in ((zz * 4 + me["colx"], step_x, not even), (zz * 4 + me["coly"], step_y, even)):
            cls(k)[0][at] = add(k, at, [16 + zz] if has else []).astype(BF)
            step(k, zz).start()

    def arrive(k, zz):
        S, R = cls(k)
        remote(k, S.at[0], R.at[20 + zz], 5 + zz, me["px"]).wait_recv()
        remote(k, S.at[0], R.at[24 + zz], 9 + zz, me["py"]).wait_recv()

    def do_c(k, j):
        zz = lax.rem(z + j, 4)
        arrive(k, zz)
        at = zz * 4 + col
        cls(k)[0][at] = add(k, at, [20 + zz, 24 + zz]).astype(BF)
        step_z(k, j).start()

    def total(k):
        arrive(k, z)
        for j in (1, 2, 3):
            step_z(k, j).wait_recv()
        return add(k, z * 4 + col, [20 + z, 24 + z, 28, 29, 30])

    def drain(k):
        swap(k).wait_send()
        for zz in range(4):
            step_g(k, zz).wait_send()
            step_x(k, zz).wait_send()
            step_y(k, zz).wait_send()
        for j in (1, 2, 3):
            step_z(k, j).wait_send()

    def finish(k):
        v = total(k)
        if k < 3:
            for i in range(2):
                for ref, base in ((o_wu, i * 1536), (o_wd, i * 1536 + 768)):
                    lo, hi = (2 * k + i) * 256, 1536 + (2 * k + i) * 256
                    ref[0:16, lo : lo + 256] = v[:, base : base + 256]
                    ref[0:16, hi : hi + 256] = v[:, base + 256 : base + 512]
                    ref[16:24, lo : lo + 256] = v[0:8, base + 512 : base + 768]
                    ref[16:24, hi : hi + 256] = v[8:16, base + 512 : base + 768]
        else:
            ref, at = (o_wo, 0) if k == 3 else (o_wq, (k - 4) * 768)
            ref[0:16, at : at + 768] = v[:, 0:768]
            ref[16:24, at : at + 384] = v[0:8, 768:1152]
            ref[16:24, at + 384 : at + 768] = v[8:16, 768:1152]
        drain(k)

    def to_owner(d):
        owner = lax.rem(s + d, 16)
        return remote(7, Ss.at[c * 16 + owner], Rs.at[16 + s], d, (c, owner))

    def from_peer(d):
        slot = 16 + lax.rem(s + 16 - d, 16)
        return remote(7, Ss.at[0], Rs.at[slot], d, me["px"])

    def small_out():
        swap(7).wait_recv()
        for i in range(16):
            Ss[c * 16 + i] = (Ss[c * 16 + i].astype(F32) + Rs[i].astype(F32)).astype(BF)
        for d in range(1, 16):
            to_owner(d).start()

    def small_in():
        v = Ss[c * 16 + s].astype(F32)
        for d in range(1, 16):
            from_peer(d).wait_recv()
            v = v + Rs[16 + lax.rem(s + 16 - d, 16)].astype(F32)
        o_small[...] = v
        swap(7).wait_send()
        for d in range(1, 16):
            to_owner(d).wait_send()

    def halo(src, dst, r, right, h):
        side = int(right)
        i = 24 + r * 2 + side if h is None else (r * 2 + side) * 6 + h
        at = (r, side) if h is None else (r, side, h)
        return pltpu.make_async_remote_copy(
            src_ref=src.at[at], dst_ref=dst.at[at], send_sem=psend.at[i], recv_sem=prsem.at[i],
            device_id=(c, s + 1 if right else s - 1), device_id_type=MESH,
        )

    def both(src, dst, r, h, act):
        @pl.when(has_right)
        def _():
            act(halo(src, dst, r, True, h))

        @pl.when(has_left)
        def _():
            act(halo(src, dst, r, False, h))

    def arrived(src, dst, r, h):
        @pl.when(has_left)
        def _():
            halo(src, dst, r, True, h).wait_recv()

        @pl.when(has_right)
        def _():
            halo(src, dst, r, False, h).wait_recv()

    @pl.when(jnp.logical_not(has_left))
    def _():
        precv[:, 1] = jnp.zeros((2, 6, 2, 64, 128), BF)
        hrecv[:, 1] = jnp.zeros((2, 64, 768), BF)

    @pl.when(jnp.logical_not(has_right))
    def _():
        precv[:, 0] = jnp.zeros((2, 6, 2, 64, 128), BF)
        hrecv[:, 0] = jnp.zeros((2, 64, 768), BF)

    tg[...] = jnp.zeros((16, 1536), F32)
    lg[...] = jnp.zeros((16, 768), F32)

    def perform(todo):
        for fn, k in todo:
            if fn is begin or fn is finish:
                fn(k)
            else:
                for j in (1, 2, 3) if fn is do_c else (0, 1, 2, 3):
                    fn(k, j)

    def run(plan, at):
        for i, todo in plan.items():
            @pl.when(at == i)
            def _():
                perform(todo)

    def feed_forward(Tok, Att, Dy, Wo, Wu, Wd, mid, h2, DyT, H2T, y, gh2, act, gu):
        loads = [
            copy(i, a, b)
            for i, (a, b) in enumerate(
                [(tok_in, Tok), (att_in, Att), (wo_in, Wo), (dy_in, Dy), (wu_in, Wu), (wd_in, Wd)]
            )
        ]
        for ld in loads:
            ld.start()
        y[...] = jnp.zeros((1024, 768), F32)
        gh2[...] = jnp.zeros((1024, 768), F32)
        for ld in loads[:3]:
            ld.wait()
        mid[...] = dg(Att[...], Wo[...], NN)

        def first(i, carry):
            rows = pl.ds(pl.multiple_of(i * 128, 128), 128)
            v = Tok[rows].astype(F32) + mid[rows]
            mid[rows] = v
            n, _ = norm_parts(v)
            h2[rows] = (n * gains[7:8] + gains[8:9]).astype(BF)
            return carry

        lax.fori_loop(0, 8, first, 0)
        loads[3].wait()

        def flip(i, carry):
            rows = pl.ds(pl.multiple_of(i * 128, 128), 128)
            for j in range(3):
                cols = slice(j * 256, j * 256 + 256)
                DyT[cols, rows] = Dy[rows, cols].T
                H2T[cols, rows] = h2[rows, cols].T
            return carry

        lax.fori_loop(0, 8, flip, 0)
        loads[4].wait()
        loads[5].wait()
        plan = {
            5: [(begin, 0)], 7: [(do_g, 0)], 11: [(do_p, 0), (begin, 1)], 13: [(do_g, 1)],
            17: [(do_c, 0), (begin, 2)],
        }

        all_here(16)

        def chunk(j, carry):
            lanes = [pl.ds(pl.multiple_of(j * 512 + h * 256, 256), 256) for h in range(2)]
            whole = pl.ds(pl.multiple_of(j * 512, 512), 512)
            for m in range(2):
                rows = slice(m * 512, m * 512 + 512)
                for h in range(2):
                    u = dg(h2[rows], Wu[:, lanes[h]], NN)
                    ga = dg(Dy[rows], Wd[:, lanes[h]], NN)
                    a, da = gelu_both(u)
                    act[rows, h * 256 : h * 256 + 256] = a.astype(BF)
                    gu[rows, h * 256 : h * 256 + 256] = (ga * da).astype(BF)
            run(plan, j * 3)
            y[...] += dg(act[...], Wd[:, whole], NT)
            gh2[...] += dg(gu[...], Wu[:, whole], NT)
            run(plan, j * 3 + 1)
            for which, (left, right) in enumerate(((H2T, gu), (DyT, act))):
                base = lax.rem(j, 2) * 1536 + which * 768
                at = [pl.ds(pl.multiple_of(base + i * 256, 256), 256) for i in range(3)]
                dws = dg(left[...], right[...], NN)
                for i in range(32):
                    head, tail = dws[i * 24 : i * 24 + 16].astype(BF), dws[i * 24 + 16 : i * 24 + 24]
                    Sf[j // 2, i, :, at[0]] = head[:, 0:256]
                    Sf[j // 2, i, :, at[1]] = head[:, 256:512]
                    Sf[j // 2, i, :, at[2]] = pack_pair(tail[:, 0:256], tail[:, 256:512])
            run(plan, j * 3 + 2)
            return carry

        lax.fori_loop(0, 6, chunk, 0)

        def last(i, carry):
            rows = pl.ds(pl.multiple_of(i * 128, 128), 128)
            v = mid[rows]
            Tok[rows] = (v + y[rows]).astype(BF)
            n, rs = norm_parts(v)
            g = gh2[rows]
            e = g * gains[7:8]
            gm = Dy[rows].astype(F32) + rs * (
                e - jnp.mean(e, axis=-1, keepdims=True) - n * jnp.mean(e * n, axis=-1, keepdims=True)
            )
            y[rows] = gm
            h2[rows] = gm.astype(BF)
            a, b = carry
            return a + jnp.sum((g * n).reshape(16, 8, 768), axis=0), b + jnp.sum(g.reshape(16, 8, 768), axis=0)

        zero = jnp.zeros((8, 768), F32)
        a, b = lax.fori_loop(0, 8, last, (zero, zero))
        perform([(do_p, 1)])
        lg[7:8] = jnp.sum(a, axis=0, keepdims=True)
        lg[8:9] = jnp.sum(b, axis=0, keepdims=True)
        store = [copy(6, Tok, o_out), copy(7, y, o_gmid)]
        for st in store:
            st.start()

        def flip_att(i, carry):
            rows = pl.ds(pl.multiple_of(i * 128, 128), 128)
            for j in range(3):
                DyT[j * 256 : j * 256 + 256, rows] = Att[rows, j * 256 : j * 256 + 256].T
            return carry

        lax.fori_loop(0, 8, flip_att, 0)
        gatt[...] = dg(h2[...], Wo[...], NT).astype(BF)
        dws = dg(DyT[...], h2[...], NN)
        for i in range(32):
            tail = dws[i * 24 + 16 : i * 24 + 24]
            So[i, :, 0:768] = dws[i * 24 : i * 24 + 16].astype(BF)
            So[i, :, 768:1152] = pack_pair(tail[:, 0:384], tail[:, 384:768])
        begin(3)
        perform([(do_g, 2)])

        def products(i, carry):
            rows = pl.ds(pl.multiple_of(i * 128, 128), 128)
            v = gatt[rows].astype(F32) * Att[rows].astype(F32)
            high = v.astype(BF)
            Dy[rows] = high
            Att[rows] = (v - high.astype(F32)).astype(BF)
            return carry

        lax.fori_loop(0, 8, products, 0)
        head = lax.broadcasted_iota(jnp.int32, (16, 768), 1) // HEAD
        pick = jnp.where(head == lax.broadcasted_iota(jnp.int32, (16, 768), 0), 1.0, 0.0).astype(BF)
        sums = dg(pick, Dy[...], NT) + dg(pick, Att[...], NT)
        for h in range(6):
            delta[h, 0:2] = sums[2 * h : 2 * h + 2]
        for st in store:
            st.wait()

    def weight_grad(gext, h1t, Sq, j):
        dws = dg(h1t[...], gext[:, j * 768 : j * 768 + 768], NN)
        for i in range(32):
            tail = dws[i * 24 + 16 : i * 24 + 24]
            Sq[j, i, :, 0:768] = dws[i * 24 : i * 24 + 16].astype(BF)
            Sq[j, i, :, 768:1152] = pack_pair(tail[:, 0:384], tail[:, 384:768])
        begin(4 + j)

    def attention(gext, h1, h1t, Sq, kv, dkv, dpe, chunk):
        late_load = copy(8, h1_in, h1)
        late_load.start()

        def scores(q, pe, bias):
            loads = [
                copy(4 + i, a, b)
                for i, (a, b) in enumerate([(q_in, q), (kv_in, kv), (pe_in, pe), (bias_in, bias)])
            ]
            for ld in loads:
                ld.start()
            for r in range(2):
                gext[r * 640 : r * 640 + 64, 0:768] = jnp.zeros((64, 768), BF)
                gext[r * 640 + 576 : r * 640 + 640, 0:768] = jnp.zeros((64, 768), BF)
            for ld in loads:
                ld.wait()
            plans = (
                {0: [(do_c, 1)], 2: [(do_p, 2)], 3: [(do_g, 3)], 5: [(do_p, 3)]},
                {2: [(do_c, 2)], 3: [(do_c, 3)]},
            )
            for r in range(2):
                def heads(h, carry):
                    attend_back(q, kv, pe, bias, lse, delta, gatt, gext, dkv, dpe, r, h)
                    for part in range(2):
                        pstage[r, 0, h, part] = dpe[r, part * 6 + h, 0:64].astype(BF)
                        pstage[r, 1, h, part] = dpe[r, part * 6 + h, 192:256].astype(BF)
                    both(pstage, precv, r, h, lambda cp: cp.start())
                    run(plans[r], h)
                    return carry

                lax.fori_loop(0, 6, heads, 0)

        pl.run_scoped(
            scores, vm((2, 512, 768), BF), vm((2, 256, 1536), BF), vm((8, 416, 128), F32)
        )
        late_load.wait()
        for r in range(2):
            def flip(i, carry):
                rows = pl.ds(pl.multiple_of(i * 128, 128), 128)
                for j in range(3):
                    to = pl.ds(pl.multiple_of(r * 640 + i * 128, 128), 128)
                    h1t[j * 256 : j * 256 + 256, to] = h1[r, rows, j * 256 : j * 256 + 256].T
                return carry

            lax.fori_loop(0, 5, flip, 0)
        weight_grad(gext, h1t, Sq, 0)
        for part in range(2):
            for r in range(2):
                def pool_back(h, carry):
                    t = part * 6 + h
                    lanes = pl.ds(pl.multiple_of(t * 128, 128), 128)
                    if part == 0:
                        arrived(pstage, precv, r, h)

                    low = dpe[r, t, 64:128] + precv[r, 1, h, part].astype(F32)
                    high = dpe[r, t, 128:192] + precv[r, 0, h, part].astype(F32)
                    gp = jnp.concatenate([low, high], axis=0)
                    chunk[...] = kv[r, :, lanes].astype(F32)
                    for i in range(5):
                        at = pl.ds(62 + i, 128, stride=4)
                        gm = gp * same[r, i].astype(F32)
                        tg[i : i + 1, lanes] += jnp.sum(gm * chunk[at, :], axis=0, keepdims=True)
                        dkv[r, t, at, :] += gm * taps[i : i + 1, lanes]
                    out_lanes = pl.ds(pl.multiple_of(768 + t * 128, 128), 128)
                    gext[r * 640 : r * 640 + 640, out_lanes] = dkv[r, t].astype(BF)
                    return carry

                lax.fori_loop(0, 6, pool_back, 0)
            weight_grad(gext, h1t, Sq, 1 + part)
            perform([(do_g, 4 + part)])

    def projection(gext, h1t, Sq, wq, tok, gmid, gh):
        loads = [
            copy(9 + i, a, b) for i, (a, b) in enumerate([(wq_in, wq), (tok_in, tok), (o_gmid, gmid)])
        ]
        for ld in loads:
            ld.start()
        perform([(do_p, 4)])
        for ld in loads:
            ld.wait()
        for r in range(2):
            gh[r] = dg(gext[r * 640 : r * 640 + 640], wq[...], NT)
            hstage[r, 0] = gh[r, 0:64].astype(BF)
            hstage[r, 1] = gh[r, 576:640].astype(BF)
            both(hstage, hrecv, r, None, lambda cp: cp.start())
            perform(([(do_g, 6), (do_p, 5)], [(do_p, 6), (do_c, 4)])[r])

        def rows_norm(r, i, carry):
            rows = pl.ds(pl.multiple_of(r * 512 + i * 128, 128), 128)
            n, rs = norm_parts(tok[rows].astype(F32))
            g = gh[r, pl.ds(pl.multiple_of(i * 128 + 64, 64), 128)]
            e = g * gains[5:6]
            gmid[rows] += rs * (
                e - jnp.mean(e, axis=-1, keepdims=True) - n * jnp.mean(e * n, axis=-1, keepdims=True)
            )
            a, b = carry
            return a + jnp.sum((g * n).reshape(16, 8, 768), axis=0), b + jnp.sum(g.reshape(16, 8, 768), axis=0)

        def add_halo(r):
            arrived(hstage, hrecv, r, None)
            gh[r, 64:128] += hrecv[r, 1].astype(F32)
            gh[r, 512:576] += hrecv[r, 0].astype(F32)

        zero = jnp.zeros((8, 768), F32)
        add_halo(0)
        acc = lax.fori_loop(0, 4, lambda i, cr: rows_norm(0, i, cr), (zero, zero))
        acc = lax.fori_loop(1, 3, lambda i, cr: rows_norm(1, i, cr), acc)
        add_halo(1)
        acc = lax.fori_loop(0, 2, lambda i, cr: rows_norm(1, 3 * i, cr), acc)
        out = copy(13, gmid, o_in)
        out.start()
        lg[5:6] = jnp.sum(acc[0], axis=0, keepdims=True)
        lg[6:7] = jnp.sum(acc[1], axis=0, keepdims=True)

        def put(i, v):
            Ss[i] = v

        pick_small(tg, lg, put)
        begin(7)
        perform([(do_c, 5), (finish, 0)])
        small_out()
        perform([(finish, 1), (finish, 2), (finish, 3), (do_c, 6), (finish, 4), (finish, 5)])
        small_in()
        perform([(finish, 6)])
        out.wait()

    vm = pltpu.VMEM
    tall, wide = (lambda dt: vm((1024, 768), dt)), (lambda dt: vm((768, 1024), dt))
    pl.run_scoped(
        feed_forward,
        tall(BF), tall(BF), tall(BF), vm((768, 768), BF), vm((768, 3072), BF), vm((768, 3072), BF),
        tall(F32), tall(BF), wide(BF), wide(BF), tall(F32), tall(F32), vm((1024, 512), BF), vm((1024, 512), BF),
    )

    def rest(gext, h1, h1t, Sq):
        late.append(Sq)
        pl.run_scoped(
            functools.partial(attention, gext, h1, h1t, Sq),
            vm((2, 640, 1536), BF), vm((2, 12, 640, 128), F32), vm((2, 12, 256, 128), F32), vm((640, 128), F32),
        )
        pl.run_scoped(
            functools.partial(projection, gext, h1t, Sq),
            vm((768, 2304), BF), tall(BF), tall(F32), vm((2, 640, 768), F32),
        )

    pl.run_scoped(
        rest, vm((1280, 2304), BF), vm((2, 640, 768), BF), vm((768, 1280), BF), vm((3, 32, 16, 1152), BF)
    )
    for r in range(2):
        for h in range(6):
            both(pstage, precv, r, h, lambda cp: cp.wait_send())
        both(hstage, hrecv, r, None, lambda cp: cp.wait_send())


def back_part(*args):
    sds = jax.ShapeDtypeStruct
    vm, dma = pltpu.VMEM, pltpu.SemaphoreType.DMA
    return pl.pallas_call(
        back_kernel,
        out_shape=[
            sds((1024, 768), BF), sds((1024, 768), F32), sds((1024, 768), F32),
            sds((24, 2304), F32), sds((24, 768), F32), sds((24, 3072), F32), sds((24, 3072), F32), sds((16, 128), F32),
        ],
        in_specs=[ANY] * 12 + [VM] * 4,
        out_specs=[ANY] * 3 + [VM] * 5,
        scratch_shapes=[
            vm((3, 32, 16, 3072), BF), vm((32, 16, 1152), BF), vm((32, 16, 128), BF),
            vm((3, 31, 16, 3072), BF), vm((31, 16, 1152), BF), vm((3, 31, 16, 1152), BF), vm((32, 16, 128), BF),
            vm((1024, 768), BF), vm((6, 8, 1024), F32),
            vm((2, 2, 6, 2, 64, 128), BF), vm((2, 2, 6, 2, 64, 128), BF), vm((2, 2, 64, 768), BF), vm((2, 2, 64, 768), BF),
            vm((16, 1536), F32), vm((16, 768), F32),
            dma((8, 16)), dma((8, 16)), dma((28,)), dma((28,)), dma((14,)),
        ],
        compiler_params=pltpu.CompilerParams(collective_id=1, has_side_effects=True, vmem_limit_bytes=VMEM_LIMIT),
    )(*args)


def with_halo(x, sides, width):
    for axis, dim in sides:
        size, length = (lax.axis_size(axis), x.shape[dim])
        up = [(i, (i + 1) % size) for i in range(size - 1)]
        down = [(j, i) for i, j in up]
        last = lax.slice_in_dim(x, length - width, length, axis=dim)
        first = lax.slice_in_dim(x, 0, width, axis=dim)
        before = lax.ppermute(last, axis, up)
        after = lax.ppermute(first, axis, down)
        x = jnp.concatenate([before, x, after], axis=dim)
    return x


def layer_norm(inputs, norm_gain, norm_bias):
    middle = jnp.mean(inputs, axis=-1, keepdims=True)
    centred = inputs - middle
    spread = jnp.mean(centred * centred, axis=-1, keepdims=True)
    return centred * lax.rsqrt(spread + 1e-05) * norm_gain + norm_bias


def pool_local(extended, taps_in, seg_window):
    block_rows = extended.shape[0] - 2 * NEAR
    anchors = seg_window[REACH : REACH + block_rows : 4]
    pooled = jnp.zeros((block_rows // 4, extended.shape[1]), jnp.float32)
    for offset in range(5):
        start_row = NEAR - 2 + offset
        picked = extended[start_row : start_row + block_rows : 4]
        seg_start = REACH - 2 + offset
        same_doc = (seg_window[seg_start : seg_start + block_rows : 4] == anchors).astype(
            jnp.float32
        )
        pooled = pooled + taps_in[offset] * picked * same_doc[:, None]
    return pooled


def window_masks(seg_window, block_rows):
    seg_query = seg_window[REACH : REACH + block_rows]
    seg_key = seg_window[REACH - NEAR : REACH + block_rows + NEAR]
    seg_pool = seg_window[0 : block_rows + 2 * REACH : 4]
    q_index = jnp.arange(block_rows, dtype=jnp.int32)
    k_index = jnp.arange(seg_key.shape[0], dtype=jnp.int32)
    p_index = jnp.arange(seg_pool.shape[0], dtype=jnp.int32)
    near_mask = (jnp.abs(q_index[:, None] - k_index[None, :] + NEAR) <= NEAR) & (
        seg_query[:, None] == seg_key[None, :]
    )
    far_mask = (jnp.abs(4 * p_index[None, :] - REACH - q_index[:, None]) <= REACH) & (
        seg_query[:, None] == seg_pool[None, :]
    )
    return (near_mask, far_mask)


def scores_of(queries, near_keys, far_keys, near_mask, far_mask):
    score_scale = HEAD ** (-0.5)
    near_scores = (
        jnp.einsum("qhd,khd->hqk", queries, near_keys, preferred_element_type=jnp.float32)
        * score_scale
    )
    far_scores = (
        jnp.einsum("qhd,khd->hqk", queries, far_keys, preferred_element_type=jnp.float32)
        * score_scale
    )
    return (
        jnp.where(near_mask[None], near_scores, -1e30),
        jnp.where(far_mask[None], far_scores, -1e30),
    )


def normalise(near_scores, far_scores, near_mask, far_mask, row_max, row_total):
    near_prob = jnp.where(near_mask[None], jnp.exp(near_scores - row_max), 0.0) / row_total
    far_prob = jnp.where(far_mask[None], jnp.exp(far_scores - row_max), 0.0) / row_total
    return (near_prob, far_prob)


def add_rims(middle_part, rim_values, rim_width):
    extra = middle_part.shape[0] - rim_width
    return (
        middle_part
        + jnp.pad(rim_values[:rim_width], ((0, extra), (0, 0)))
        + jnp.pad(rim_values[-rim_width:], ((extra, 0), (0, 0)))
    )


def shards(
    tokens,
    segments,
    cotangent,
    ln1_gain,
    ln1_bias,
    w_qkv,
    pool_taps,
    w_out,
    ln2_gain,
    ln2_bias,
    w_up,
    w_down,
):
    block_rows = tokens.shape[1]
    model_width = tokens.shape[2]
    pool_half = REACH // 4
    score_scale = HEAD ** (-0.5)
    offset_tokens = lax.axis_index("seq") * block_rows
    outputs = []
    input_grads = []
    summed = None
    for micro_step in range(tokens.shape[0]):
        gathered = (
            lax.all_gather(ln1_gain, ("dp", "seq"), axis=0, tiled=True),
            lax.all_gather(ln1_bias, ("dp", "seq"), axis=0, tiled=True),
            lax.all_gather(w_qkv, ("dp", "seq"), axis=0, tiled=True),
            lax.all_gather(pool_taps, ("dp", "seq"), axis=1, tiled=True),
            lax.all_gather(w_out, ("dp", "seq"), axis=0, tiled=True),
            lax.all_gather(ln2_gain, ("dp", "seq"), axis=0, tiled=True),
            lax.all_gather(ln2_bias, ("dp", "seq"), axis=0, tiled=True),
            lax.all_gather(w_up, ("dp", "seq"), axis=0, tiled=True),
            lax.all_gather(w_down, ("dp", "seq"), axis=1, tiled=True),
        )
        gain_one, bias_one, proj_qkv, taps, proj_out, gain_two, bias_two, proj_up, proj_down = (
            gathered
        )
        seg_row = segments[micro_step]
        seg_padded = jnp.pad(seg_row, (REACH, REACH), constant_values=-1)
        seg_window = lax.dynamic_slice_in_dim(
            seg_padded, offset_tokens, block_rows + 2 * REACH, 0
        )
        near_mask, far_mask = window_masks(seg_window, block_rows)
        inputs = tokens[micro_step].astype(jnp.float32)
        gain_float = gain_one.astype(jnp.float32)
        bias_float = bias_one.astype(jnp.float32)
        gain_second = gain_two.astype(jnp.float32)
        bias_second = bias_two.astype(jnp.float32)
        normed = layer_norm(inputs, gain_float, bias_float).astype(jnp.bfloat16)
        projected = jnp.dot(normed, proj_qkv, preferred_element_type=jnp.float32).astype(
            jnp.bfloat16
        )
        queries = projected[:, :model_width].reshape(block_rows, HEADS, HEAD)
        key_value = projected[:, model_width:]
        extended = with_halo(key_value, (("seq", 0),), NEAR)
        ext_float = extended.astype(jnp.float32)
        taps_float = taps.astype(jnp.float32)
        pooled = pool_local(ext_float, taps_float, seg_window).astype(jnp.bfloat16)
        pool_ext = with_halo(pooled, (("seq", 0),), pool_half)
        near_keys = extended[:, :model_width].reshape(-1, HEADS, HEAD)
        near_values = extended[:, model_width:].reshape(-1, HEADS, HEAD)
        far_keys = pool_ext[:, :model_width].reshape(-1, HEADS, HEAD)
        far_values = pool_ext[:, model_width:].reshape(-1, HEADS, HEAD)
        near_scores, far_scores = scores_of(queries, near_keys, far_keys, near_mask, far_mask)
        row_max = jnp.maximum(
            jnp.max(near_scores, axis=2, keepdims=True), jnp.max(far_scores, axis=2, keepdims=True)
        )
        near_exp = jnp.where(near_mask[None], jnp.exp(near_scores - row_max), 0.0)
        far_exp = jnp.where(far_mask[None], jnp.exp(far_scores - row_max), 0.0)
        row_total = jnp.sum(near_exp, axis=2, keepdims=True) + jnp.sum(
            far_exp, axis=2, keepdims=True
        )
        near_low = (near_exp / row_total).astype(jnp.bfloat16)
        far_low = (far_exp / row_total).astype(jnp.bfloat16)
        mixed_sum = jnp.einsum(
            "hqk,khd->qhd", near_low, near_values, preferred_element_type=jnp.float32
        ) + jnp.einsum("hqk,khd->qhd", far_low, far_values, preferred_element_type=jnp.float32)
        attended = mixed_sum.reshape(block_rows, model_width).astype(jnp.bfloat16)
        branch = jnp.dot(attended, proj_out, preferred_element_type=jnp.float32)
        middle = inputs + branch
        normed_two = layer_norm(middle, gain_second, bias_second).astype(jnp.bfloat16)
        upward = jnp.dot(normed_two, proj_up, preferred_element_type=jnp.float32)
        activated = jax.nn.gelu(upward).astype(jnp.bfloat16)
        result = middle + jnp.dot(activated, proj_down, preferred_element_type=jnp.float32)
        outputs.append(result.astype(jnp.bfloat16))
        regathered = (
            lax.all_gather(ln1_gain, ("dp", "seq"), axis=0, tiled=True),
            lax.all_gather(ln1_bias, ("dp", "seq"), axis=0, tiled=True),
            lax.all_gather(w_qkv, ("dp", "seq"), axis=0, tiled=True),
            lax.all_gather(pool_taps, ("dp", "seq"), axis=1, tiled=True),
            lax.all_gather(w_out, ("dp", "seq"), axis=0, tiled=True),
            lax.all_gather(ln2_gain, ("dp", "seq"), axis=0, tiled=True),
            lax.all_gather(ln2_bias, ("dp", "seq"), axis=0, tiled=True),
            lax.all_gather(w_up, ("dp", "seq"), axis=0, tiled=True),
            lax.all_gather(w_down, ("dp", "seq"), axis=1, tiled=True),
        )
        back_qkv = regathered[2]
        back_out = regathered[4]
        back_up = regathered[7]
        back_down = regathered[8]
        grad_out = cotangent[micro_step]
        grad_act = jnp.dot(grad_out, back_down.T, preferred_element_type=jnp.float32)
        grad_down = jnp.dot(activated.T, grad_out, preferred_element_type=jnp.float32)
        gelu_value, gelu_back = jax.vjp(jax.nn.gelu, upward)
        grad_upin = gelu_back(grad_act)[0].astype(jnp.bfloat16)
        grad_upw = jnp.dot(normed_two.T, grad_upin, preferred_element_type=jnp.float32)
        grad_normed_two = jnp.dot(grad_upin, back_up.T, preferred_element_type=jnp.float32)
        norm_value_two, norm_back_two = jax.vjp(layer_norm, middle, gain_second, bias_second)
        grad_mid_part, grad_gain_two, grad_bias_two = norm_back_two(grad_normed_two)
        grad_middle = grad_out.astype(jnp.float32) + grad_mid_part
        grad_branch = grad_middle.astype(jnp.bfloat16)
        grad_outw = jnp.dot(attended.T, grad_branch, preferred_element_type=jnp.float32)
        grad_mixed = (
            jnp.dot(grad_branch, back_out.T, preferred_element_type=jnp.float32)
            .astype(jnp.bfloat16)
            .reshape(block_rows, HEADS, HEAD)
        )
        near_scores, far_scores = scores_of(queries, near_keys, far_keys, near_mask, far_mask)
        near_prob, far_prob = normalise(
            near_scores, far_scores, near_mask, far_mask, row_max, row_total
        )
        near_low = near_prob.astype(jnp.bfloat16)
        far_low = far_prob.astype(jnp.bfloat16)
        grad_near_values = jnp.einsum(
            "hqk,qhd->khd", near_low, grad_mixed, preferred_element_type=jnp.float32
        )
        grad_far_values = jnp.einsum(
            "hqk,qhd->khd", far_low, grad_mixed, preferred_element_type=jnp.float32
        )
        grad_near_prob = jnp.einsum(
            "qhd,khd->hqk", grad_mixed, near_values, preferred_element_type=jnp.float32
        )
        grad_far_prob = jnp.einsum(
            "qhd,khd->hqk", grad_mixed, far_values, preferred_element_type=jnp.float32
        )
        row_delta = jnp.sum(near_prob * grad_near_prob, axis=2, keepdims=True) + jnp.sum(
            far_prob * grad_far_prob, axis=2, keepdims=True
        )
        grad_near_scores = (near_prob * (grad_near_prob - row_delta)).astype(jnp.bfloat16)
        grad_far_scores = (far_prob * (grad_far_prob - row_delta)).astype(jnp.bfloat16)
        grad_queries = (
            jnp.einsum(
                "hqk,khd->qhd", grad_near_scores, near_keys, preferred_element_type=jnp.float32
            )
            + jnp.einsum(
                "hqk,khd->qhd", grad_far_scores, far_keys, preferred_element_type=jnp.float32
            )
        ) * score_scale
        grad_near_keys = (
            jnp.einsum(
                "hqk,qhd->khd", grad_near_scores, queries, preferred_element_type=jnp.float32
            )
            * score_scale
        )
        grad_far_keys = (
            jnp.einsum("hqk,qhd->khd", grad_far_scores, queries, preferred_element_type=jnp.float32)
            * score_scale
        )
        grad_extended = jnp.concatenate(
            [grad_near_keys.reshape(-1, model_width), grad_near_values.reshape(-1, model_width)],
            axis=1,
        )
        grad_pool_ext = jnp.concatenate(
            [grad_far_keys.reshape(-1, model_width), grad_far_values.reshape(-1, model_width)],
            axis=1,
        )
        pool_edges = jnp.concatenate(
            [grad_pool_ext[:pool_half], grad_pool_ext[-pool_half:]], axis=0
        )
        pool_returned = with_halo(pool_edges.astype(jnp.bfloat16), (("seq", 0),), pool_half).astype(
            pool_edges.dtype
        )
        grad_pooled = add_rims(grad_pool_ext[pool_half:-pool_half], pool_returned, pool_half)
        pool_value, pool_back = jax.vjp(
            lambda ext_in, taps_part: pool_local(ext_in, taps_part, seg_window),
            ext_float,
            taps_float,
        )
        grad_ext_pool, grad_taps = pool_back(grad_pooled)
        grad_extended = grad_extended + grad_ext_pool
        token_edges = jnp.concatenate(
            [grad_extended[:NEAR], grad_extended[-NEAR:]], axis=0
        )
        token_returned = with_halo(
            token_edges.astype(jnp.bfloat16), (("seq", 0),), NEAR
        ).astype(token_edges.dtype)
        grad_kv = add_rims(grad_extended[NEAR:-NEAR], token_returned, NEAR)
        grad_projected = jnp.concatenate(
            [grad_queries.reshape(block_rows, model_width), grad_kv], axis=1
        ).astype(jnp.bfloat16)
        grad_qkvw = jnp.dot(normed.T, grad_projected, preferred_element_type=jnp.float32)
        grad_normed = jnp.dot(grad_projected, back_qkv.T, preferred_element_type=jnp.float32)
        norm_value_one, norm_back_one = jax.vjp(layer_norm, inputs, gain_float, bias_float)
        grad_in_part, grad_gain_one, grad_bias_one = norm_back_one(grad_normed)
        input_grads.append(grad_middle + grad_in_part)
        shares = (
            lax.psum_scatter(grad_gain_one, ("dp", "seq"), scatter_dimension=0, tiled=True),
            lax.psum_scatter(grad_bias_one, ("dp", "seq"), scatter_dimension=0, tiled=True),
            lax.psum_scatter(grad_qkvw, ("dp", "seq"), scatter_dimension=0, tiled=True),
            lax.psum_scatter(grad_taps, ("dp", "seq"), scatter_dimension=1, tiled=True),
            lax.psum_scatter(grad_outw, ("dp", "seq"), scatter_dimension=0, tiled=True),
            lax.psum_scatter(grad_gain_two, ("dp", "seq"), scatter_dimension=0, tiled=True),
            lax.psum_scatter(grad_bias_two, ("dp", "seq"), scatter_dimension=0, tiled=True),
            lax.psum_scatter(grad_upw, ("dp", "seq"), scatter_dimension=0, tiled=True),
            lax.psum_scatter(grad_down, ("dp", "seq"), scatter_dimension=1, tiled=True),
        )
        if summed is None:
            summed = shares
        else:
            summed = jax.tree.map(jnp.add, summed, shares)
    return (
        jnp.stack(outputs),
        jnp.stack(input_grads),
        summed[0],
        summed[1],
        summed[2],
        summed[3],
        summed[4],
        summed[5],
        summed[6],
        summed[7],
        summed[8],
    )


def chained(
    tokens, segments, cotangent, ln1_gain, ln1_bias, w_qkv, pool_taps, w_out, ln2_gain, ln2_bias, w_up, w_down,
):
    small = small_share(pool_taps, ln1_gain, ln1_bias, ln2_gain, ln2_bias)
    wq, wo, wu, wd, taps, gains, h1, q, kv, pe, att, bias, lse, same = front(
        tokens, segments, w_qkv, w_out, w_up, w_down.T, small
    )
    flat, split = (1024, 768), (2, 512, 768)
    out, _, g_in, g_wq, g_wo, g_wu, g_wd, g_small = back_part(
        tokens.reshape(flat), att.reshape(flat), cotangent.reshape(flat), wo, wu, wd,
        q, kv, pe, bias, h1, wq, taps, gains, same, lse,
    )
    return (
        out.reshape(split), g_in.reshape(split), g_small[5, :24], g_small[6, :24], g_wq, g_small[0:5, :48], g_wo,
        g_small[7, :24], g_small[8, :24], g_wu, g_wd.T,
    )


def solution(mesh):
    both = ("dp", "seq")
    row, tok, first, second = P(both), P("dp", "seq", None), P(both, None), P(None, both)
    small_mesh = mesh.shape["dp"] == 2 and mesh.shape["seq"] == 16
    return jax.shard_map(
        chained if small_mesh else shards,
        mesh=mesh,
        in_specs=(tok, P("dp", None), tok, row, row, first, second, first, row, row, first, second),
        out_specs=(tok, tok, row, row, first, second, first, row, row, first, second),
        check_vma=False,
    )
```

```python
import functools

import jax
import jax.numpy as jnp
from jax import lax
from jax.experimental import pallas as pl
from jax.experimental.pallas import tpu as pltpu
from jax.sharding import PartitionSpec as P

HEADS = 12
HEAD = 64
NEAR = 64
REACH = 256
F32, BF = jnp.float32, jnp.bfloat16
NT = (((1,), (1,)), ((), ()))
TN = (((0,), (0,)), ((), ()))
NN = (((1,), (0,)), ((), ()))
MESH = pl.DeviceIdType.MESH
ANY = pl.BlockSpec(memory_space=pl.ANY)
VM = pl.BlockSpec(memory_space=pltpu.VMEM)
VMEM_LIMIT = 63 * 2**20
UNIT = 384
CLS = 3456
WIDE = 3584
PLACE = {"qkv": (0, 0, 2304), "out": (1, 0, 768), "up": (1, 3, 3072), "down": (1, 15, 3072)}


def dg(a, b, dims):
    return lax.dot_general(a, b, dims, preferred_element_type=F32)


def spot(name, unit):
    first, start, _ = PLACE[name]
    at = start + unit
    return first + at // 9, (at % 9) * UNIT


def units(name):
    return PLACE[name][2] // UNIT


def where_am_i():
    c = lax.axis_index("dp")
    s = lax.axis_index("seq")
    z, col = s // 4, s % 4
    x, y = col % 2, col // 2
    colx, coly, cold = y * 2 + (1 - x), (1 - y) * 2 + x, 3 - col
    return dict(
        c=c, s=s, z=z, col=col, colx=colx, coly=coly, cold=cold,
        px=(c, z * 4 + colx), py=(c, z * 4 + coly), pd=(1 - c, s),
    )


def greet(me):
    bar = pltpu.get_barrier_semaphore()
    who = [me["px"], me["py"], me["pd"]]
    who += [(me["c"], lax.rem(me["z"] + j, 4) * 4 + me["col"]) for j in (1, 2, 3)]
    for dev in who:
        pl.semaphore_signal(bar, inc=1, device_id=dev, device_id_type=MESH)
    last = lax.axis_size("seq") - 1

    @pl.when(me["s"] > 0)
    def _():
        pl.semaphore_signal(bar, inc=1, device_id=(me["c"], me["s"] - 1), device_id_type=MESH)

    @pl.when(me["s"] < last)
    def _():
        pl.semaphore_signal(bar, inc=1, device_id=(me["c"], me["s"] + 1), device_id_type=MESH)

    return 6 + (me["s"] > 0).astype(jnp.int32) + (me["s"] < last).astype(jnp.int32)


def all_here(count):
    pl.semaphore_wait(pltpu.get_barrier_semaphore(), count)


def greet_all(me):
    bar = pltpu.get_barrier_semaphore()
    pl.semaphore_signal(bar, inc=1, device_id=me["pd"], device_id_type=MESH)
    for d in range(1, 16):
        pl.semaphore_signal(bar, inc=1, device_id=(me["c"], lax.rem(me["s"] + d, 16)), device_id_type=MESH)


def lane_low():
    return lax.broadcasted_iota(jnp.int32, (128, 128), 1) < HEAD


def pair_rows(v):
    low = lane_low()
    zero = jnp.zeros_like(v)
    return jnp.concatenate([jnp.where(low, v, zero), jnp.where(low, zero, v)], axis=0)


def pair_out(t):
    return jnp.concatenate([t[:HEAD, :128], t[HEAD:, 128:]], axis=0).T


def softmax_block(q2, kn, kf, bias):
    st = jnp.concatenate([dg(kn, q2, NT), dg(kf, q2, NT)], axis=0)
    st = st + jnp.concatenate([bias, bias], axis=1)
    top = jnp.max(st, axis=0, keepdims=True)
    e = jnp.exp(st - top)
    total = jnp.sum(e, axis=0, keepdims=True)
    return e, 1.0 / total, top + jnp.log(total)


def fill_window(seg, winr, wcol, has_left, has_right, s):
    length, block = seg.shape[1], 512
    left = pl.multiple_of(jnp.maximum(s * block - REACH, 0), REACH)
    right = pl.multiple_of(jnp.minimum(s * block + block, length - REACH), REACH)
    before = seg[:, pl.ds(left, REACH)].astype(F32)
    after = seg[:, pl.ds(right, REACH)].astype(F32)
    winr[:, 0:REACH] = jnp.where(has_left, before, -1.0)
    winr[:, REACH : REACH + block] = seg[:, pl.ds(pl.multiple_of(s * block, block), block)].astype(F32)
    winr[:, REACH + block :] = jnp.where(has_right, after, -1.0)
    for r in range(2):
        for t in range(8):
            row = winr[r : r + 1, t * 128 : t * 128 + 128]
            wcol[r, t * 128 : t * 128 + 128] = jnp.broadcast_to(row, (128, 128)).T


def fill_masks(winr, wcol, bias, same):
    kk = lax.broadcasted_iota(jnp.int32, (256, 128), 0)
    ii = lax.broadcasted_iota(jnp.int32, (256, 128), 1)
    pp = lax.broadcasted_iota(jnp.int32, (160, 128), 0)
    qi = lax.broadcasted_iota(jnp.int32, (160, 128), 1)
    close = jnp.abs(kk - NEAR - ii) <= NEAR
    reach = jnp.abs(4 * pp - REACH - qi) <= REACH
    for r in range(2):
        for b in range(4):
            seg_q = winr[r : r + 1, 256 + 128 * b : 384 + 128 * b]
            near = close & (wcol[r, 192 + 128 * b : 448 + 128 * b] == seg_q)
            far = reach & (wcol[r, pl.ds(128 * b, 160, stride=4), :] == seg_q)
            bias[r * 4 + b, 0:256] = jnp.where(near, 0.0, -1e30)
            bias[r * 4 + b, 256:416] = jnp.where(far, 0.0, -1e30)
        anchor = wcol[r, pl.ds(REACH, 128, stride=4), :]
        for t in range(5):
            hit = wcol[r, pl.ds(REACH - 2 + t, 128, stride=4), :] == anchor
            same[r, t] = jnp.where(hit, 1.0, 0.0).astype(BF)


def head_lanes(h):
    return (
        pl.ds(pl.multiple_of(h * 128, 128), 128),
        pl.ds(pl.multiple_of(768 + h * 128, 128), 128),
    )


def attend(q, kv, pe, bias, att, lse, r, h):
    kl, vl = head_lanes(h)
    for b in range(4):
        n, f, i = slice(b * 128, b * 128 + 256), slice(b * 32, b * 32 + 160), slice(b * 128, b * 128 + 128)
        e, rt, lse[r * 6 + h, b : b + 1] = softmax_block(
            pair_rows(q[r, i, kl]), kv[r, n, kl], pe[r, f, kl], bias[r * 4 + b]
        )
        low = (e * rt).astype(BF)
        values = jnp.concatenate([kv[r, n, vl], pe[r, f, vl]], axis=0)
        att[r, i, kl] = pair_out(dg(values, low, TN)).astype(BF)


def attend_back(q, kv, pe, bias, lse, delta, g, gext, dkv, dpe, r, h):
    kl, vl = head_lanes(h)
    for part in (h, 6 + h):
        dkv[r, part] = jnp.zeros((640, 128), F32)
        dpe[r, part] = jnp.zeros((256, 128), F32)
    for b in range(4):
        n, f, i = slice(b * 128, b * 128 + 256), slice(b * 32, b * 32 + 160), slice(b * 128, b * 128 + 128)
        q2, g2 = pair_rows(q[r, i, kl]), pair_rows(g[r * 512 + b * 128 : r * 512 + b * 128 + 128, kl])
        kn, vn, kf, vf = kv[r, n, kl], kv[r, n, vl], pe[r, f, kl], pe[r, f, vl]
        st = jnp.concatenate([dg(kn, q2, NT), dg(kf, q2, NT)], axis=0) - lse[r * 6 + h, b : b + 1]
        p = jnp.exp(st + jnp.concatenate([bias[r * 4 + b], bias[r * 4 + b]], axis=1))
        dp = jnp.concatenate([dg(vn, g2, NT), dg(vf, g2, NT)], axis=0)
        at = slice(r * 512 + b * 128, r * 512 + b * 128 + 128)
        ds = (p * (dp - jnp.concatenate([delta[h, 0:1, at], delta[h, 1:2, at]], axis=1))).astype(BF)
        low = p.astype(BF)
        dv, dk = dg(low, g2, NN), dg(ds, q2, NN)
        dkv[r, h, n] += dk[:256]
        dkv[r, 6 + h, n] += dv[:256]
        dpe[r, h, f] += dk[256:]
        dpe[r, 6 + h, f] += dv[256:]
        dqt = dg(jnp.concatenate([kn, kf], axis=0), ds, TN)
        gext[r * 640 + 64 + b * 128 : r * 640 + 192 + b * 128, kl] = (pair_out(dqt) * HEAD**-0.5).astype(BF)


def norm_parts(v):
    mean = jnp.mean(v, axis=-1, keepdims=True)
    cen = v - mean
    var = jnp.mean(cen * cen, axis=-1, keepdims=True)
    rs = lax.rsqrt(var + 1e-05)
    return cen * rs, rs


LAST = 29


def pack_own(grab, put):
    for name in ("qkv", "out", "up", "down"):
        half = units(name) // 2
        for u in range(units(name)):
            k, lo = spot(name, u)
            put(k, lo, grab(name, 0, 16, u))
        for u in range(half):
            k, lo = spot(name, units(name) + u)
            put(k, lo, jnp.concatenate([grab(name, 16, 24, u), grab(name, 16, 24, u + half)], axis=0))


def hidden_place(n):
    half, r = divmod(n, 1536)
    return (r // 256) * 512 + half * 256 + r % 256


def unpack(name, got, dst):
    half = units(name) // 2

    def pair(p, carry):
        rows = pl.ds(pl.multiple_of(48 * p, 16), 48)
        for u in range(units(name)):
            k, lo = spot(name, u)
            kt, lt = spot(name, units(name) + u % half)
            cut = slice(0, 8) if u < half else slice(8, 16)
            hidden = name in ("up", "down")
            for i in range(0, UNIT, 128) if hidden else (0,):
                n = 128 if hidden else UNIT
                to = hidden_place(u * UNIT + i) if hidden else u * UNIT
                parts = []
                for j in (0, 1):
                    parts.append(got[k, 2 * p + j, :, lo + i : lo + i + n])
                    parts.append(got[kt, 2 * p + j, :, lt + i : lt + i + n][cut])
                dst[rows, to : to + n] = jnp.concatenate(parts, axis=0)
        return carry

    lax.fori_loop(0, 16, pair, 0)


def spread_small(got, taps, gains):
    lane = lax.broadcasted_iota(jnp.int32, (16, 128), 1)

    def place(width, tiles):
        acc = [jnp.zeros((16, 128), F32) for _ in range(tiles)]
        for s in range(32):
            at, off = divmod(width * s, 128)
            v = jnp.where(lane < width, got[0, s, :, CLS:WIDE].astype(F32), 0.0)
            v = pltpu.roll(v, off, 1) if off else v
            acc[at] = acc[at] + jnp.where(lane >= off, v, 0.0)
            if off + width > 128:
                acc[at + 1] = acc[at + 1] + jnp.where(lane < off, v, 0.0)
        return acc

    for i, v in enumerate(place(48, 12)):
        taps[:, i * 128 : (i + 1) * 128] = v
    for i, v in enumerate(place(24, 6)):
        gains[:, i * 128 : (i + 1) * 128] = v


def front_kernel(
    tok, seg, wq, wo, wu, wd, small,
    o_wq, o_wo, o_wu, o_wd, o_taps, o_gains, o_h1, o_q, o_kv, o_pe, o_att, o_bias, o_lse, o_same,
    G, Wq, Wo, Wu, Wd, taps, gains, xe, h1, q, kv, pe, att, bias, lse, same, chunk, winr, wcol,
    send_x, send_y, send_d, send_z, send_g, recv, hsend, hrecv, local,
):
    me = where_am_i()
    c, s, z, col = me["c"], me["s"], me["z"], me["col"]
    mine = c * 16 + s
    last = lax.axis_size("seq") - 1
    has_left, has_right = s > 0, s < last

    def cols(k):
        return WIDE if isinstance(k, int) and k == 0 else CLS

    def hop(k, slot, to, sem):
        part = G.at[k, slot, :, pl.ds(0, cols(k))]
        return pltpu.make_async_remote_copy(
            src_ref=part, dst_ref=part, send_sem=sem, recv_sem=recv.at[k, slot],
            device_id=to, device_id_type=MESH,
        )

    def to_x(k, at):
        return hop(k, c * 16 + at, me["px"], send_x.at[k, at])

    def to_y(k, at):
        return hop(k, c * 16 + at, me["py"], send_y.at[k, at])

    def to_d(k, at):
        return hop(k, c * 16 + at, me["pd"], send_d.at[k, at])

    def to_z(k, j):
        return hop(k, mine, (c, lax.rem(z + j, 4) * 4 + col), send_z.at[k, j - 1])

    def by_y(k, zz):
        return zz != 3

    def to_g(k, zz):
        over_y = by_y(k, zz)
        at = zz * 4 + jnp.where(over_y, me["colx"], me["coly"])
        to = (c, z * 4 + jnp.where(over_y, me["coly"], me["colx"]))
        return hop(k, c * 16 + at, to, send_g.at[k, zz])

    def got(k, slot):
        hop(k, slot, me["px"], send_x.at[k, 0]).wait_recv()

    def own(k):
        for j in (1, 2, 3):
            to_z(k, j).start()
        to_x(k, s).start()
        to_y(k, s).start()
        to_d(k, s).start()

    def column(k, j):
        at = lax.rem(z + j, 4) * 4 + col
        got(k, c * 16 + at)
        to_x(k, at).start()
        to_y(k, at).start()
        to_d(k, at).start()

    def plane(k, j):
        zz = lax.rem(z + j, 4)
        got(k, c * 16 + zz * 4 + me["colx"])
        to_d(k, zz * 4 + me["colx"]).start()
        got(k, c * 16 + zz * 4 + me["coly"])
        to_d(k, zz * 4 + me["coly"]).start()
        to_g(k, zz).start()

    def diag(k, j):
        at = lax.rem(z + j, 4) * 4 + me["cold"]
        got(k, c * 16 + at)
        to_d(k, at).start()

    def event(e):
        k, i = e // 11 + 1, lax.rem(e, 11)

        @pl.when(i < 4)
        def _():
            plane(k, i)

        @pl.when((i >= 4) & (i < 7) & (k < 3))
        def _():
            column(k + 1, i - 3)

        @pl.when(i >= 7)
        def _():
            diag(k, i - 7)

    def halo_tok(r, right):
        src = tok.at[r, pl.ds(448 if right else 0, 64)]
        dst = xe.at[r, pl.ds(0 if right else 576, 64)]
        i = r * 2 + int(right)
        return pltpu.make_async_remote_copy(
            src_ref=src, dst_ref=dst, send_sem=hsend.at[i], recv_sem=hrecv.at[i],
            device_id=(c, s + 1 if right else s - 1), device_id_type=MESH,
        )

    def halo_pool(r, right):
        src = pe.at[r, pl.ds(128 if right else 64, 64)]
        dst = pe.at[r, pl.ds(0 if right else 192, 64)]
        i = 4 + r * 2 + int(right)
        return pltpu.make_async_remote_copy(
            src_ref=src, dst_ref=dst, send_sem=hsend.at[i], recv_sem=hrecv.at[i],
            device_id=(c, s + 1 if right else s - 1), device_id_type=MESH,
        )

    def both(make, r, act):
        @pl.when(has_right)
        def _():
            act(make(r, True), True)

        @pl.when(has_left)
        def _():
            act(make(r, False), False)

    def arrived(make, r):
        @pl.when(has_left)
        def _():
            make(r, True).wait_recv()

        @pl.when(has_right)
        def _():
            make(r, False).wait_recv()

    expected = greet(me)
    load = [pltpu.make_async_copy(tok.at[r], xe.at[r, pl.ds(64, 512)], local.at[r]) for r in range(2)]
    for copy in load:
        copy.start()
    shares = {"qkv": wq, "out": wo, "up": wu, "down": wd}

    def grab(name, a, b, u):
        return shares[name][a:b, u * UNIT : (u + 1) * UNIT]

    def put(k, lo, v):
        G[k, mine, :, lo : lo + UNIT] = v

    pack_own(grab, put)
    G[0, mine, :, CLS:WIDE] = small[...]

    @pl.when(jnp.logical_not(has_left))
    def _():
        for r in range(2):
            xe[r, 0:64] = jnp.zeros((64, 768), BF)
            pe[r, 0:64] = jnp.zeros((64, 1536), BF)

    @pl.when(jnp.logical_not(has_right))
    def _():
        for r in range(2):
            xe[r, 576:640] = jnp.zeros((64, 768), BF)
            pe[r, 192:256] = jnp.zeros((64, 1536), BF)

    lse[...] = jnp.zeros((12, 8, 256), F32)
    all_here(expected)
    own(0)
    for r in range(2):
        both(halo_tok, r, lambda copy, right: copy.start())
    own(1)
    own(2)
    fill_window(seg, winr, wcol, has_left, has_right, s)
    fill_masks(winr, wcol, bias, same)
    for j in (1, 2, 3):
        column(0, j)
    for j in range(4):
        plane(0, j)
    own(3)
    for j in (1, 2, 3):
        column(1, j)
    for j in range(4):
        diag(0, j)

    def other(k):
        def body(i, carry):
            got(k, (1 - c) * 16 + i)
            return carry

        lax.fori_loop(0, 16, body, 0)

    other(0)
    unpack("qkv", G, Wq)
    spread_small(G, taps, gains)
    outs = [
        pltpu.make_async_copy(a, b, local.at[2 + i])
        for i, (a, b) in enumerate(
            [(Wq, o_wq), (taps, o_taps), (gains, o_gains), (h1, o_h1), (q, o_q), (kv, o_kv), (pe, o_pe),
             (att, o_att), (bias, o_bias), (Wo, o_wo), (Wu, o_wu), (Wd, o_wd), (lse, o_lse), (same, o_same)]
        )
    ]
    for i in (0, 1, 2, 8, 13):
        outs[i].start()
    for copy in load:
        copy.wait()
    for r in range(2):
        arrived(halo_tok, r)

    for r in range(2):
        def norm_rows(i, carry):
            rows = pl.ds(pl.multiple_of(i * 128, 128), 128)
            n, _ = norm_parts(xe[r, rows].astype(F32))
            h1[r, rows] = (n * gains[5:6] + gains[6:7]).astype(BF)
            return carry

        lax.fori_loop(0, 5, norm_rows, 0)
    outs[3].start()

    for r in range(2):
        def queries(j, carry):
            lanes = pl.ds(pl.multiple_of(j * 256, 256), 256)
            v = dg(h1[r, 64:576], Wq[:, lanes], NN)
            q[r, :, lanes] = v.astype(BF) * jnp.asarray(HEAD**-0.5, BF)
            return carry

        lax.fori_loop(0, 3, queries, 0)
        def keys(j, carry):
            event(r * 6 + j)
            lanes = pl.ds(pl.multiple_of(j * 128, 128), 128)
            from_lanes = pl.ds(pl.multiple_of(768 + j * 256, 256), 256)
            to_lanes = pl.ds(pl.multiple_of(j * 256, 256), 256)
            v = dg(h1[r], Wq[:, from_lanes], NN).astype(BF)
            kv[r, :, to_lanes] = v
            chunk[0] = v[:, :128].astype(F32)
            chunk[1] = v[:, 128:].astype(F32)
            for half in range(2):
                hl = pl.ds(pl.multiple_of(j * 256 + half * 128, 128), 128)
                acc = jnp.zeros((128, 128), F32)
                for t in range(5):
                    acc = acc + taps[t : t + 1, hl] * chunk[half, pl.ds(62 + t, 128, stride=4), :] * same[r, t].astype(F32)
                pe[r, 64:192, hl] = acc.astype(BF)
            return carry

        lax.fori_loop(0, 6, keys, 0)
        both(halo_pool, r, lambda copy, right: copy.start())
    outs[4].start()
    outs[5].start()
    for r in range(2):
        arrived(halo_pool, r)

        def heads_event(h, carry):
            attend(q, kv, pe, bias, att, lse, r, h)
            base = 12 + (r * 6 + h) * 2

            @pl.when(base < LAST)
            def _():
                event(base)

            @pl.when(base + 1 < LAST)
            def _():
                event(base + 1)

            return carry

        lax.fori_loop(0, 6, heads_event, 0)
    outs[6].start()
    outs[7].start()
    outs[12].start()
    for k in (1, 2):
        other(k)
    finish = (("out", Wo), ("up", Wu), ("down", Wd))
    for i in range(2):
        unpack(finish[i][0], G, finish[i][1])
        outs[9 + i].start()
    lax.fori_loop(LAST, 33, lambda e, carry: (event(e), carry)[1], 0)
    other(3)
    unpack("down", G, Wd)
    outs[11].start()
    for r in range(2):
        both(halo_tok, r, lambda copy, right: copy.wait_send())
        both(halo_pool, r, lambda copy, right: copy.wait_send())
    for k in range(4):
        def done(i, carry):
            to_x(k, i * 4 + col).wait_send()
            to_y(k, i * 4 + col).wait_send()
            to_g(k, i).wait_send()
            for j in range(4):
                to_d(k, i * 4 + j).wait_send()
            return carry

        lax.fori_loop(0, 4, done, 0)
        for j in (1, 2, 3):
            to_z(k, j).wait_send()
    for copy in outs:
        copy.wait()


def front(tok, seg, wq, wo, wu, wd, small):
    sds = jax.ShapeDtypeStruct
    shapes = [
        ((768, 2304), BF), ((768, 768), BF), ((768, 3072), BF), ((768, 3072), BF),
        ((16, 1536), F32), ((16, 768), F32),
        ((2, 640, 768), BF), ((2, 512, 768), BF), ((2, 640, 1536), BF), ((2, 256, 1536), BF),
        ((2, 512, 768), BF), ((8, 416, 128), F32), ((12, 8, 256), F32),
        ((2, 5, 128, 128), BF),
    ]
    scratch = [pltpu.VMEM((4, 32, 16, WIDE), BF)]
    scratch += [pltpu.VMEM(sh, dt) for sh, dt in shapes[:6]]
    scratch += [pltpu.VMEM((2, 640, 768), BF)]
    scratch += [pltpu.VMEM(sh, dt) for sh, dt in shapes[6:]]
    scratch += [pltpu.VMEM((2, 640, 128), F32), pltpu.VMEM((2, 1024), F32), pltpu.VMEM((2, 1024, 128), F32)]
    dma = pltpu.SemaphoreType.DMA
    scratch += [dma((4, 16)), dma((4, 16)), dma((4, 16)), dma((4, 3)), dma((4, 4)), dma((4, 32)), dma((8,)), dma((8,)), dma((16,))]
    return pl.pallas_call(
        front_kernel,
        out_shape=[sds(sh, dt) for sh, dt in shapes],
        in_specs=[ANY] + [VM] * 6,
        out_specs=[ANY] * len(shapes),
        scratch_shapes=scratch,
        compiler_params=pltpu.CompilerParams(collective_id=0, has_side_effects=True, vmem_limit_bytes=VMEM_LIMIT),
    )(tok, seg, wq, wo, wu, wd, small)


def small_share(pool_taps, ln1_gain, ln1_bias, ln2_gain, ln2_bias):
    rows = jnp.stack([ln1_gain, ln1_bias, ln2_gain, ln2_bias])
    return jnp.concatenate(
        [jnp.pad(pool_taps, ((0, 0), (0, 80))), jnp.pad(rows, ((0, 7), (0, 104)))], axis=0
    )


def gelu_both(u):
    a, b = 0.7978845608028654, 0.044715
    sq = u * u
    t = jnp.tanh(a * u * (1.0 + b * sq))
    half = 0.5 + 0.5 * t
    grad = half + 0.5 * u * (1.0 - t * t) * (a + (3.0 * a * b) * sq)
    return u * half, grad


def pack_pair(lo, hi):
    return jnp.concatenate([lo, hi], axis=0).astype(BF)


def pick_small(tg, lg, put):
    lane = lax.broadcasted_iota(jnp.int32, (16, 128), 1)

    def part(src, width, s):
        at, off = divmod(width * s, 128)
        v = src[:, at * 128 : at * 128 + 128]
        v = pltpu.roll(v, 128 - off, 1) if off else v
        if off + width > 128:
            w = pltpu.roll(src[:, at * 128 + 128 : at * 128 + 256], 128 - off, 1)
            v = jnp.where(lane < 128 - off, v, w)
        return jnp.where(lane < width, v, 0.0)

    for s in range(32):
        put(s, (part(tg, 48, s) + part(lg, 24, s)).astype(BF))


def back_kernel(
    tok_in, att_in, dy_in, wo_in, wu_in, wd_in,
    q_in, kv_in, pe_in, bias_in, h1_in, wq_in, taps, gains, same, lse,
    o_out, o_gmid, o_in, o_wq, o_wo, o_wu, o_wd, o_small,
    Sf, So, Ss, Rf, Ro, Rq, Rs, gatt, delta, pstage, precv, hstage, hrecv, tg, lg,
    send, recv, psend, prsem, local,
):
    me = where_am_i()
    greet_all(me)
    c, s, z, col = me["c"], me["s"], me["z"], me["col"]
    has_left, has_right = s > 0, s < lax.axis_size("seq") - 1

    def copy(i, a, b):
        return pltpu.make_async_copy(a, b, local.at[i])

    late = []

    def cls(k):
        if k < 3:
            return Sf.at[k, pl.ds(c * 16, 16)], Rf.at[k]
        if k == 3:
            return So.at[pl.ds(c * 16, 16)], Ro
        if k < 7:
            return late[0].at[k - 4, pl.ds(c * 16, 16)], Rq.at[k - 4]
        return Ss.at[pl.ds(c * 16, 16)], Rs

    def other(k):
        start = (1 - c) * 16
        if k < 3:
            return Sf.at[k, pl.ds(start, 16)]
        if k == 3 or k == 7:
            return (So if k == 3 else Ss).at[pl.ds(start, 16)]
        return late[0].at[k - 4, pl.ds(start, 16)]

    def remote(k, src, slot, i, to):
        return pltpu.make_async_remote_copy(
            src_ref=src, dst_ref=slot, send_sem=send.at[k, i], recv_sem=recv.at[k, i],
            device_id=to, device_id_type=MESH,
        )

    def swap(k):
        return remote(k, other(k), cls(k)[1].at[pl.ds(0, 16)], 0, me["pd"])

    def step_g(k, zz):
        S, R = cls(k)
        to = me["px"] if zz == 0 else me["py"]
        return remote(k, S.at[zz * 4 + me["cold"]], R.at[16 + zz], 1 + zz, to)

    def step_x(k, zz):
        S, R = cls(k)
        return remote(k, S.at[zz * 4 + me["colx"]], R.at[20 + zz], 5 + zz, me["px"])

    def step_y(k, zz):
        S, R = cls(k)
        return remote(k, S.at[zz * 4 + me["coly"]], R.at[24 + zz], 9 + zz, me["py"])

    def step_z(k, j):
        S, R = cls(k)
        zz = lax.rem(z + j, 4)
        return remote(k, S.at[zz * 4 + col], R.at[27 + j], 12 + j, (c, zz * 4 + col))

    def add(k, at, slots):
        S, R = cls(k)
        v = S[at].astype(F32) + R[at].astype(F32)
        for slot in slots:
            v = v + R[slot].astype(F32)
        return v

    def begin(k):
        swap(k).start()

    def do_g(k, zz):
        if zz == 0:
            swap(k).wait_recv()
        at = zz * 4 + me["cold"]
        cls(k)[0][at] = add(k, at, []).astype(BF)
        step_g(k, zz).start()

    def do_p(k, zz):
        step_g(k, zz).wait_recv()
        even = zz == 0
        for at, step, has in ((zz * 4 + me["colx"], step_x, not even), (zz * 4 + me["coly"], step_y, even)):
            cls(k)[0][at] = add(k, at, [16 + zz] if has else []).astype(BF)
            step(k, zz).start()

    def arrive(k, zz):
        S, R = cls(k)
        remote(k, S.at[0], R.at[20 + zz], 5 + zz, me["px"]).wait_recv()
        remote(k, S.at[0], R.at[24 + zz], 9 + zz, me["py"]).wait_recv()

    def do_c(k, j):
        zz = lax.rem(z + j, 4)
        arrive(k, zz)
        at = zz * 4 + col
        cls(k)[0][at] = add(k, at, [20 + zz, 24 + zz]).astype(BF)
        step_z(k, j).start()

    def total(k):
        arrive(k, z)
        for j in (1, 2, 3):
            step_z(k, j).wait_recv()
        return add(k, z * 4 + col, [20 + z, 24 + z, 28, 29, 30])

    def drain(k):
        swap(k).wait_send()
        for zz in range(4):
            step_g(k, zz).wait_send()
            step_x(k, zz).wait_send()
            step_y(k, zz).wait_send()
        for j in (1, 2, 3):
            step_z(k, j).wait_send()

    def finish(k):
        v = total(k)
        if k < 3:
            for i in range(2):
                for ref, base in ((o_wu, i * 1536), (o_wd, i * 1536 + 768)):
                    lo, hi = (2 * k + i) * 256, 1536 + (2 * k + i) * 256
                    ref[0:16, lo : lo + 256] = v[:, base : base + 256]
                    ref[0:16, hi : hi + 256] = v[:, base + 256 : base + 512]
                    ref[16:24, lo : lo + 256] = v[0:8, base + 512 : base + 768]
                    ref[16:24, hi : hi + 256] = v[8:16, base + 512 : base + 768]
        else:
            ref, at = (o_wo, 0) if k == 3 else (o_wq, (k - 4) * 768)
            ref[0:16, at : at + 768] = v[:, 0:768]
            ref[16:24, at : at + 384] = v[0:8, 768:1152]
            ref[16:24, at + 384 : at + 768] = v[8:16, 768:1152]
        drain(k)

    def to_owner(d):
        owner = lax.rem(s + d, 16)
        return remote(7, Ss.at[c * 16 + owner], Rs.at[16 + s], d, (c, owner))

    def from_peer(d):
        slot = 16 + lax.rem(s + 16 - d, 16)
        return remote(7, Ss.at[0], Rs.at[slot], d, me["px"])

    def small_out():
        swap(7).wait_recv()
        for i in range(16):
            Ss[c * 16 + i] = (Ss[c * 16 + i].astype(F32) + Rs[i].astype(F32)).astype(BF)
        for d in range(1, 16):
            to_owner(d).start()

    def small_in():
        v = Ss[c * 16 + s].astype(F32)
        for d in range(1, 16):
            from_peer(d).wait_recv()
            v = v + Rs[16 + lax.rem(s + 16 - d, 16)].astype(F32)
        o_small[...] = v
        swap(7).wait_send()
        for d in range(1, 16):
            to_owner(d).wait_send()

    def halo(src, dst, r, right, h):
        side = int(right)
        i = 24 + r * 2 + side if h is None else (r * 2 + side) * 6 + h
        at = (r, side) if h is None else (r, side, h)
        return pltpu.make_async_remote_copy(
            src_ref=src.at[at], dst_ref=dst.at[at], send_sem=psend.at[i], recv_sem=prsem.at[i],
            device_id=(c, s + 1 if right else s - 1), device_id_type=MESH,
        )

    def both(src, dst, r, h, act):
        @pl.when(has_right)
        def _():
            act(halo(src, dst, r, True, h))

        @pl.when(has_left)
        def _():
            act(halo(src, dst, r, False, h))

    def arrived(src, dst, r, h):
        @pl.when(has_left)
        def _():
            halo(src, dst, r, True, h).wait_recv()

        @pl.when(has_right)
        def _():
            halo(src, dst, r, False, h).wait_recv()

    @pl.when(jnp.logical_not(has_left))
    def _():
        precv[:, 1] = jnp.zeros((2, 6, 2, 64, 128), BF)
        hrecv[:, 1] = jnp.zeros((2, 64, 768), BF)

    @pl.when(jnp.logical_not(has_right))
    def _():
        precv[:, 0] = jnp.zeros((2, 6, 2, 64, 128), BF)
        hrecv[:, 0] = jnp.zeros((2, 64, 768), BF)

    tg[...] = jnp.zeros((16, 1536), F32)
    lg[...] = jnp.zeros((16, 768), F32)

    def perform(todo):
        for fn, k in todo:
            if fn is begin or fn is finish:
                fn(k)
            else:
                for j in (1, 2, 3) if fn is do_c else (0, 1, 2, 3):
                    fn(k, j)

    def run(plan, at):
        for i, todo in plan.items():
            @pl.when(at == i)
            def _():
                perform(todo)

    def feed_forward(Tok, Att, Dy, Wo, Wu, Wd, mid, h2, DyT, H2T, y, gh2, act, gu):
        loads = [
            copy(i, a, b)
            for i, (a, b) in enumerate(
                [(tok_in, Tok), (att_in, Att), (wo_in, Wo), (dy_in, Dy), (wu_in, Wu), (wd_in, Wd)]
            )
        ]
        for ld in loads:
            ld.start()
        y[...] = jnp.zeros((1024, 768), F32)
        gh2[...] = jnp.zeros((1024, 768), F32)
        for ld in loads[:3]:
            ld.wait()
        mid[...] = dg(Att[...], Wo[...], NN)

        def first(i, carry):
            rows = pl.ds(pl.multiple_of(i * 128, 128), 128)
            v = Tok[rows].astype(F32) + mid[rows]
            mid[rows] = v
            n, _ = norm_parts(v)
            h2[rows] = (n * gains[7:8] + gains[8:9]).astype(BF)
            return carry

        lax.fori_loop(0, 8, first, 0)
        loads[3].wait()

        def flip(i, carry):
            rows = pl.ds(pl.multiple_of(i * 128, 128), 128)
            for j in range(3):
                cols = slice(j * 256, j * 256 + 256)
                DyT[cols, rows] = Dy[rows, cols].T
                H2T[cols, rows] = h2[rows, cols].T
            return carry

        lax.fori_loop(0, 8, flip, 0)
        loads[4].wait()
        loads[5].wait()
        plan = {
            5: [(begin, 0)], 7: [(do_g, 0)], 11: [(do_p, 0), (begin, 1)], 13: [(do_g, 1)],
            17: [(do_c, 0), (begin, 2)],
        }

        all_here(16)

        def chunk(j, carry):
            lanes = [pl.ds(pl.multiple_of(j * 512 + h * 256, 256), 256) for h in range(2)]
            whole = pl.ds(pl.multiple_of(j * 512, 512), 512)
            for m in range(2):
                rows = slice(m * 512, m * 512 + 512)
                for h in range(2):
                    u = dg(h2[rows], Wu[:, lanes[h]], NN)
                    ga = dg(Dy[rows], Wd[:, lanes[h]], NN)
                    a, da = gelu_both(u)
                    act[rows, h * 256 : h * 256 + 256] = a.astype(BF)
                    gu[rows, h * 256 : h * 256 + 256] = (ga * da).astype(BF)
            run(plan, j * 3)
            y[...] += dg(act[...], Wd[:, whole], NT)
            gh2[...] += dg(gu[...], Wu[:, whole], NT)
            run(plan, j * 3 + 1)
            for which, (left, right) in enumerate(((H2T, gu), (DyT, act))):
                base = lax.rem(j, 2) * 1536 + which * 768
                at = [pl.ds(pl.multiple_of(base + i * 256, 256), 256) for i in range(3)]
                dws = dg(left[...], right[...], NN)
                for i in range(32):
                    head, tail = dws[i * 24 : i * 24 + 16].astype(BF), dws[i * 24 + 16 : i * 24 + 24]
                    Sf[j // 2, i, :, at[0]] = head[:, 0:256]
                    Sf[j // 2, i, :, at[1]] = head[:, 256:512]
                    Sf[j // 2, i, :, at[2]] = pack_pair(tail[:, 0:256], tail[:, 256:512])
            run(plan, j * 3 + 2)
            return carry

        lax.fori_loop(0, 6, chunk, 0)

        def last(i, carry):
            rows = pl.ds(pl.multiple_of(i * 128, 128), 128)
            v = mid[rows]
            Tok[rows] = (v + y[rows]).astype(BF)
            n, rs = norm_parts(v)
            g = gh2[rows]
            e = g * gains[7:8]
            gm = Dy[rows].astype(F32) + rs * (
                e - jnp.mean(e, axis=-1, keepdims=True) - n * jnp.mean(e * n, axis=-1, keepdims=True)
            )
            y[rows] = gm
            h2[rows] = gm.astype(BF)
            a, b = carry
            return a + jnp.sum((g * n).reshape(16, 8, 768), axis=0), b + jnp.sum(g.reshape(16, 8, 768), axis=0)

        zero = jnp.zeros((8, 768), F32)
        a, b = lax.fori_loop(0, 8, last, (zero, zero))
        perform([(do_p, 1)])
        lg[7:8] = jnp.sum(a, axis=0, keepdims=True)
        lg[8:9] = jnp.sum(b, axis=0, keepdims=True)
        store = [copy(6, Tok, o_out), copy(7, y, o_gmid)]
        for st in store:
            st.start()

        def flip_att(i, carry):
            rows = pl.ds(pl.multiple_of(i * 128, 128), 128)
            for j in range(3):
                DyT[j * 256 : j * 256 + 256, rows] = Att[rows, j * 256 : j * 256 + 256].T
            return carry

        lax.fori_loop(0, 8, flip_att, 0)
        gatt[...] = dg(h2[...], Wo[...], NT).astype(BF)
        dws = dg(DyT[...], h2[...], NN)
        for i in range(32):
            tail = dws[i * 24 + 16 : i * 24 + 24]
            So[i, :, 0:768] = dws[i * 24 : i * 24 + 16].astype(BF)
            So[i, :, 768:1152] = pack_pair(tail[:, 0:384], tail[:, 384:768])
        begin(3)
        perform([(do_g, 2)])

        def products(i, carry):
            rows = pl.ds(pl.multiple_of(i * 128, 128), 128)
            v = gatt[rows].astype(F32) * Att[rows].astype(F32)
            high = v.astype(BF)
            Dy[rows] = high
            Att[rows] = (v - high.astype(F32)).astype(BF)
            return carry

        lax.fori_loop(0, 8, products, 0)
        head = lax.broadcasted_iota(jnp.int32, (16, 768), 1) // HEAD
        pick = jnp.where(head == lax.broadcasted_iota(jnp.int32, (16, 768), 0), 1.0, 0.0).astype(BF)
        sums = dg(pick, Dy[...], NT) + dg(pick, Att[...], NT)
        for h in range(6):
            delta[h, 0:2] = sums[2 * h : 2 * h + 2]
        for st in store:
            st.wait()

    def weight_grad(gext, h1t, Sq, j):
        dws = dg(h1t[...], gext[:, j * 768 : j * 768 + 768], NN)
        for i in range(32):
            tail = dws[i * 24 + 16 : i * 24 + 24]
            Sq[j, i, :, 0:768] = dws[i * 24 : i * 24 + 16].astype(BF)
            Sq[j, i, :, 768:1152] = pack_pair(tail[:, 0:384], tail[:, 384:768])
        begin(4 + j)

    def attention(gext, h1, h1t, Sq, kv, dkv, dpe, chunk):
        late_load = copy(8, h1_in, h1)
        late_load.start()

        def scores(q, pe, bias):
            loads = [
                copy(4 + i, a, b)
                for i, (a, b) in enumerate([(q_in, q), (kv_in, kv), (pe_in, pe), (bias_in, bias)])
            ]
            for ld in loads:
                ld.start()
            for r in range(2):
                gext[r * 640 : r * 640 + 64, 0:768] = jnp.zeros((64, 768), BF)
                gext[r * 640 + 576 : r * 640 + 640, 0:768] = jnp.zeros((64, 768), BF)
            for ld in loads:
                ld.wait()
            plans = (
                {0: [(do_c, 1)], 2: [(do_p, 2)], 3: [(do_g, 3)], 5: [(do_p, 3)]},
                {0: [(finish, 0)], 2: [(do_c, 2)], 3: [(do_c, 3)], 4: [(finish, 1)]},
            )
            for r in range(2):
                def heads(h, carry):
                    attend_back(q, kv, pe, bias, lse, delta, gatt, gext, dkv, dpe, r, h)
                    for part in range(2):
                        pstage[r, 0, h, part] = dpe[r, part * 6 + h, 0:64].astype(BF)
                        pstage[r, 1, h, part] = dpe[r, part * 6 + h, 192:256].astype(BF)
                    both(pstage, precv, r, h, lambda cp: cp.start())
                    run(plans[r], h)
                    return carry

                lax.fori_loop(0, 6, heads, 0)

        pl.run_scoped(
            scores, vm((2, 512, 768), BF), vm((2, 256, 1536), BF), vm((8, 416, 128), F32)
        )
        late_load.wait()
        for r in range(2):
            def flip(i, carry):
                rows = pl.ds(pl.multiple_of(i * 128, 128), 128)
                for j in range(3):
                    to = pl.ds(pl.multiple_of(r * 640 + i * 128, 128), 128)
                    h1t[j * 256 : j * 256 + 256, to] = h1[r, rows, j * 256 : j * 256 + 256].T
                return carry

            lax.fori_loop(0, 5, flip, 0)
        weight_grad(gext, h1t, Sq, 0)
        for part in range(2):
            for r in range(2):
                def pool_back(h, carry):
                    t = part * 6 + h
                    lanes = pl.ds(pl.multiple_of(t * 128, 128), 128)
                    if part == 0:
                        arrived(pstage, precv, r, h)

                    low = dpe[r, t, 64:128] + precv[r, 1, h, part].astype(F32)
                    high = dpe[r, t, 128:192] + precv[r, 0, h, part].astype(F32)
                    gp = jnp.concatenate([low, high], axis=0)
                    chunk[...] = kv[r, :, lanes].astype(F32)
                    for i in range(5):
                        at = pl.ds(62 + i, 128, stride=4)
                        gm = gp * same[r, i].astype(F32)
                        tg[i : i + 1, lanes] += jnp.sum(gm * chunk[at, :], axis=0, keepdims=True)
                        dkv[r, t, at, :] += gm * taps[i : i + 1, lanes]
                    out_lanes = pl.ds(pl.multiple_of(768 + t * 128, 128), 128)
                    gext[r * 640 : r * 640 + 640, out_lanes] = dkv[r, t].astype(BF)
                    return carry

                lax.fori_loop(0, 6, pool_back, 0)
            weight_grad(gext, h1t, Sq, 1 + part)
            perform([(do_g, 4 + part)])

    def projection(gext, h1t, Sq, wq, tok, gmid, gh):
        loads = [
            copy(9 + i, a, b) for i, (a, b) in enumerate([(wq_in, wq), (tok_in, tok), (o_gmid, gmid)])
        ]
        for ld in loads:
            ld.start()
        perform([(do_p, 4)])
        for ld in loads:
            ld.wait()
        for r in range(2):
            gh[r] = dg(gext[r * 640 : r * 640 + 640], wq[...], NT)
            hstage[r, 0] = gh[r, 0:64].astype(BF)
            hstage[r, 1] = gh[r, 576:640].astype(BF)
            both(hstage, hrecv, r, None, lambda cp: cp.start())
            perform(([(do_g, 6), (do_p, 5)], [(do_p, 6), (do_c, 4)])[r])

        def rows_norm(r, i, carry):
            rows = pl.ds(pl.multiple_of(r * 512 + i * 128, 128), 128)
            n, rs = norm_parts(tok[rows].astype(F32))
            g = gh[r, pl.ds(pl.multiple_of(i * 128 + 64, 64), 128)]
            e = g * gains[5:6]
            gmid[rows] += rs * (
                e - jnp.mean(e, axis=-1, keepdims=True) - n * jnp.mean(e * n, axis=-1, keepdims=True)
            )
            a, b = carry
            return a + jnp.sum((g * n).reshape(16, 8, 768), axis=0), b + jnp.sum(g.reshape(16, 8, 768), axis=0)

        def add_halo(r):
            arrived(hstage, hrecv, r, None)
            gh[r, 64:128] += hrecv[r, 1].astype(F32)
            gh[r, 512:576] += hrecv[r, 0].astype(F32)

        zero = jnp.zeros((8, 768), F32)
        add_halo(0)
        acc = lax.fori_loop(0, 4, lambda i, cr: rows_norm(0, i, cr), (zero, zero))
        acc = lax.fori_loop(1, 3, lambda i, cr: rows_norm(1, i, cr), acc)
        add_halo(1)
        acc = lax.fori_loop(0, 2, lambda i, cr: rows_norm(1, 3 * i, cr), acc)
        out = copy(13, gmid, o_in)
        out.start()
        lg[5:6] = jnp.sum(acc[0], axis=0, keepdims=True)
        lg[6:7] = jnp.sum(acc[1], axis=0, keepdims=True)

        def put(i, v):
            Ss[i] = v

        pick_small(tg, lg, put)
        begin(7)
        perform([(do_c, 5)])
        small_out()
        perform([(finish, 2), (finish, 3), (do_c, 6), (finish, 4), (finish, 5)])
        small_in()
        perform([(finish, 6)])
        out.wait()

    vm = pltpu.VMEM
    tall, wide = (lambda dt: vm((1024, 768), dt)), (lambda dt: vm((768, 1024), dt))
    pl.run_scoped(
        feed_forward,
        tall(BF), tall(BF), tall(BF), vm((768, 768), BF), vm((768, 3072), BF), vm((768, 3072), BF),
        tall(F32), tall(BF), wide(BF), wide(BF), tall(F32), tall(F32), vm((1024, 512), BF), vm((1024, 512), BF),
    )

    def rest(gext, h1, h1t, Sq):
        late.append(Sq)
        pl.run_scoped(
            functools.partial(attention, gext, h1, h1t, Sq),
            vm((2, 640, 1536), BF), vm((2, 12, 640, 128), F32), vm((2, 12, 256, 128), F32), vm((640, 128), F32),
        )
        pl.run_scoped(
            functools.partial(projection, gext, h1t, Sq),
            vm((768, 2304), BF), tall(BF), tall(F32), vm((2, 640, 768), F32),
        )

    pl.run_scoped(
        rest, vm((1280, 2304), BF), vm((2, 640, 768), BF), vm((768, 1280), BF), vm((3, 32, 16, 1152), BF)
    )
    for r in range(2):
        for h in range(6):
            both(pstage, precv, r, h, lambda cp: cp.wait_send())
        both(hstage, hrecv, r, None, lambda cp: cp.wait_send())


def back_part(*args):
    sds = jax.ShapeDtypeStruct
    vm, dma = pltpu.VMEM, pltpu.SemaphoreType.DMA
    return pl.pallas_call(
        back_kernel,
        out_shape=[
            sds((1024, 768), BF), sds((1024, 768), F32), sds((1024, 768), F32),
            sds((24, 2304), F32), sds((24, 768), F32), sds((24, 3072), F32), sds((24, 3072), F32), sds((16, 128), F32),
        ],
        in_specs=[ANY] * 12 + [VM] * 4,
        out_specs=[ANY] * 3 + [VM] * 5,
        scratch_shapes=[
            vm((3, 32, 16, 3072), BF), vm((32, 16, 1152), BF), vm((32, 16, 128), BF),
            vm((3, 31, 16, 3072), BF), vm((31, 16, 1152), BF), vm((3, 31, 16, 1152), BF), vm((32, 16, 128), BF),
            vm((1024, 768), BF), vm((6, 8, 1024), F32),
            vm((2, 2, 6, 2, 64, 128), BF), vm((2, 2, 6, 2, 64, 128), BF), vm((2, 2, 64, 768), BF), vm((2, 2, 64, 768), BF),
            vm((16, 1536), F32), vm((16, 768), F32),
            dma((8, 16)), dma((8, 16)), dma((28,)), dma((28,)), dma((14,)),
        ],
        compiler_params=pltpu.CompilerParams(collective_id=1, has_side_effects=True, vmem_limit_bytes=VMEM_LIMIT),
    )(*args)


def with_halo(x, sides, width):
    for axis, dim in sides:
        size, length = (lax.axis_size(axis), x.shape[dim])
        up = [(i, (i + 1) % size) for i in range(size - 1)]
        down = [(j, i) for i, j in up]
        last = lax.slice_in_dim(x, length - width, length, axis=dim)
        first = lax.slice_in_dim(x, 0, width, axis=dim)
        before = lax.ppermute(last, axis, up)
        after = lax.ppermute(first, axis, down)
        x = jnp.concatenate([before, x, after], axis=dim)
    return x


def layer_norm(inputs, norm_gain, norm_bias):
    middle = jnp.mean(inputs, axis=-1, keepdims=True)
    centred = inputs - middle
    spread = jnp.mean(centred * centred, axis=-1, keepdims=True)
    return centred * lax.rsqrt(spread + 1e-05) * norm_gain + norm_bias


def pool_local(extended, taps_in, seg_window):
    block_rows = extended.shape[0] - 2 * NEAR
    anchors = seg_window[REACH : REACH + block_rows : 4]
    pooled = jnp.zeros((block_rows // 4, extended.shape[1]), jnp.float32)
    for offset in range(5):
        start_row = NEAR - 2 + offset
        picked = extended[start_row : start_row + block_rows : 4]
        seg_start = REACH - 2 + offset
        same_doc = (seg_window[seg_start : seg_start + block_rows : 4] == anchors).astype(
            jnp.float32
        )
        pooled = pooled + taps_in[offset] * picked * same_doc[:, None]
    return pooled


def window_masks(seg_window, block_rows):
    seg_query = seg_window[REACH : REACH + block_rows]
    seg_key = seg_window[REACH - NEAR : REACH + block_rows + NEAR]
    seg_pool = seg_window[0 : block_rows + 2 * REACH : 4]
    q_index = jnp.arange(block_rows, dtype=jnp.int32)
    k_index = jnp.arange(seg_key.shape[0], dtype=jnp.int32)
    p_index = jnp.arange(seg_pool.shape[0], dtype=jnp.int32)
    near_mask = (jnp.abs(q_index[:, None] - k_index[None, :] + NEAR) <= NEAR) & (
        seg_query[:, None] == seg_key[None, :]
    )
    far_mask = (jnp.abs(4 * p_index[None, :] - REACH - q_index[:, None]) <= REACH) & (
        seg_query[:, None] == seg_pool[None, :]
    )
    return (near_mask, far_mask)


def scores_of(queries, near_keys, far_keys, near_mask, far_mask):
    score_scale = HEAD ** (-0.5)
    near_scores = (
        jnp.einsum("qhd,khd->hqk", queries, near_keys, preferred_element_type=jnp.float32)
        * score_scale
    )
    far_scores = (
        jnp.einsum("qhd,khd->hqk", queries, far_keys, preferred_element_type=jnp.float32)
        * score_scale
    )
    return (
        jnp.where(near_mask[None], near_scores, -1e30),
        jnp.where(far_mask[None], far_scores, -1e30),
    )


def normalise(near_scores, far_scores, near_mask, far_mask, row_max, row_total):
    near_prob = jnp.where(near_mask[None], jnp.exp(near_scores - row_max), 0.0) / row_total
    far_prob = jnp.where(far_mask[None], jnp.exp(far_scores - row_max), 0.0) / row_total
    return (near_prob, far_prob)


def add_rims(middle_part, rim_values, rim_width):
    extra = middle_part.shape[0] - rim_width
    return (
        middle_part
        + jnp.pad(rim_values[:rim_width], ((0, extra), (0, 0)))
        + jnp.pad(rim_values[-rim_width:], ((extra, 0), (0, 0)))
    )


def shards(
    tokens,
    segments,
    cotangent,
    ln1_gain,
    ln1_bias,
    w_qkv,
    pool_taps,
    w_out,
    ln2_gain,
    ln2_bias,
    w_up,
    w_down,
):
    block_rows = tokens.shape[1]
    model_width = tokens.shape[2]
    pool_half = REACH // 4
    score_scale = HEAD ** (-0.5)
    offset_tokens = lax.axis_index("seq") * block_rows
    outputs = []
    input_grads = []
    summed = None
    for micro_step in range(tokens.shape[0]):
        gathered = (
            lax.all_gather(ln1_gain, ("dp", "seq"), axis=0, tiled=True),
            lax.all_gather(ln1_bias, ("dp", "seq"), axis=0, tiled=True),
            lax.all_gather(w_qkv, ("dp", "seq"), axis=0, tiled=True),
            lax.all_gather(pool_taps, ("dp", "seq"), axis=1, tiled=True),
            lax.all_gather(w_out, ("dp", "seq"), axis=0, tiled=True),
            lax.all_gather(ln2_gain, ("dp", "seq"), axis=0, tiled=True),
            lax.all_gather(ln2_bias, ("dp", "seq"), axis=0, tiled=True),
            lax.all_gather(w_up, ("dp", "seq"), axis=0, tiled=True),
            lax.all_gather(w_down, ("dp", "seq"), axis=1, tiled=True),
        )
        gain_one, bias_one, proj_qkv, taps, proj_out, gain_two, bias_two, proj_up, proj_down = (
            gathered
        )
        seg_row = segments[micro_step]
        seg_padded = jnp.pad(seg_row, (REACH, REACH), constant_values=-1)
        seg_window = lax.dynamic_slice_in_dim(
            seg_padded, offset_tokens, block_rows + 2 * REACH, 0
        )
        near_mask, far_mask = window_masks(seg_window, block_rows)
        inputs = tokens[micro_step].astype(jnp.float32)
        gain_float = gain_one.astype(jnp.float32)
        bias_float = bias_one.astype(jnp.float32)
        gain_second = gain_two.astype(jnp.float32)
        bias_second = bias_two.astype(jnp.float32)
        normed = layer_norm(inputs, gain_float, bias_float).astype(jnp.bfloat16)
        projected = jnp.dot(normed, proj_qkv, preferred_element_type=jnp.float32).astype(
            jnp.bfloat16
        )
        queries = projected[:, :model_width].reshape(block_rows, HEADS, HEAD)
        key_value = projected[:, model_width:]
        extended = with_halo(key_value, (("seq", 0),), NEAR)
        ext_float = extended.astype(jnp.float32)
        taps_float = taps.astype(jnp.float32)
        pooled = pool_local(ext_float, taps_float, seg_window).astype(jnp.bfloat16)
        pool_ext = with_halo(pooled, (("seq", 0),), pool_half)
        near_keys = extended[:, :model_width].reshape(-1, HEADS, HEAD)
        near_values = extended[:, model_width:].reshape(-1, HEADS, HEAD)
        far_keys = pool_ext[:, :model_width].reshape(-1, HEADS, HEAD)
        far_values = pool_ext[:, model_width:].reshape(-1, HEADS, HEAD)
        near_scores, far_scores = scores_of(queries, near_keys, far_keys, near_mask, far_mask)
        row_max = jnp.maximum(
            jnp.max(near_scores, axis=2, keepdims=True), jnp.max(far_scores, axis=2, keepdims=True)
        )
        near_exp = jnp.where(near_mask[None], jnp.exp(near_scores - row_max), 0.0)
        far_exp = jnp.where(far_mask[None], jnp.exp(far_scores - row_max), 0.0)
        row_total = jnp.sum(near_exp, axis=2, keepdims=True) + jnp.sum(
            far_exp, axis=2, keepdims=True
        )
        near_low = (near_exp / row_total).astype(jnp.bfloat16)
        far_low = (far_exp / row_total).astype(jnp.bfloat16)
        mixed_sum = jnp.einsum(
            "hqk,khd->qhd", near_low, near_values, preferred_element_type=jnp.float32
        ) + jnp.einsum("hqk,khd->qhd", far_low, far_values, preferred_element_type=jnp.float32)
        attended = mixed_sum.reshape(block_rows, model_width).astype(jnp.bfloat16)
        branch = jnp.dot(attended, proj_out, preferred_element_type=jnp.float32)
        middle = inputs + branch
        normed_two = layer_norm(middle, gain_second, bias_second).astype(jnp.bfloat16)
        upward = jnp.dot(normed_two, proj_up, preferred_element_type=jnp.float32)
        activated = jax.nn.gelu(upward).astype(jnp.bfloat16)
        result = middle + jnp.dot(activated, proj_down, preferred_element_type=jnp.float32)
        outputs.append(result.astype(jnp.bfloat16))
        regathered = (
            lax.all_gather(ln1_gain, ("dp", "seq"), axis=0, tiled=True),
            lax.all_gather(ln1_bias, ("dp", "seq"), axis=0, tiled=True),
            lax.all_gather(w_qkv, ("dp", "seq"), axis=0, tiled=True),
            lax.all_gather(pool_taps, ("dp", "seq"), axis=1, tiled=True),
            lax.all_gather(w_out, ("dp", "seq"), axis=0, tiled=True),
            lax.all_gather(ln2_gain, ("dp", "seq"), axis=0, tiled=True),
            lax.all_gather(ln2_bias, ("dp", "seq"), axis=0, tiled=True),
            lax.all_gather(w_up, ("dp", "seq"), axis=0, tiled=True),
            lax.all_gather(w_down, ("dp", "seq"), axis=1, tiled=True),
        )
        back_qkv = regathered[2]
        back_out = regathered[4]
        back_up = regathered[7]
        back_down = regathered[8]
        grad_out = cotangent[micro_step]
        grad_act = jnp.dot(grad_out, back_down.T, preferred_element_type=jnp.float32)
        grad_down = jnp.dot(activated.T, grad_out, preferred_element_type=jnp.float32)
        gelu_value, gelu_back = jax.vjp(jax.nn.gelu, upward)
        grad_upin = gelu_back(grad_act)[0].astype(jnp.bfloat16)
        grad_upw = jnp.dot(normed_two.T, grad_upin, preferred_element_type=jnp.float32)
        grad_normed_two = jnp.dot(grad_upin, back_up.T, preferred_element_type=jnp.float32)
        norm_value_two, norm_back_two = jax.vjp(layer_norm, middle, gain_second, bias_second)
        grad_mid_part, grad_gain_two, grad_bias_two = norm_back_two(grad_normed_two)
        grad_middle = grad_out.astype(jnp.float32) + grad_mid_part
        grad_branch = grad_middle.astype(jnp.bfloat16)
        grad_outw = jnp.dot(attended.T, grad_branch, preferred_element_type=jnp.float32)
        grad_mixed = (
            jnp.dot(grad_branch, back_out.T, preferred_element_type=jnp.float32)
            .astype(jnp.bfloat16)
            .reshape(block_rows, HEADS, HEAD)
        )
        near_scores, far_scores = scores_of(queries, near_keys, far_keys, near_mask, far_mask)
        near_prob, far_prob = normalise(
            near_scores, far_scores, near_mask, far_mask, row_max, row_total
        )
        near_low = near_prob.astype(jnp.bfloat16)
        far_low = far_prob.astype(jnp.bfloat16)
        grad_near_values = jnp.einsum(
            "hqk,qhd->khd", near_low, grad_mixed, preferred_element_type=jnp.float32
        )
        grad_far_values = jnp.einsum(
            "hqk,qhd->khd", far_low, grad_mixed, preferred_element_type=jnp.float32
        )
        grad_near_prob = jnp.einsum(
            "qhd,khd->hqk", grad_mixed, near_values, preferred_element_type=jnp.float32
        )
        grad_far_prob = jnp.einsum(
            "qhd,khd->hqk", grad_mixed, far_values, preferred_element_type=jnp.float32
        )
        row_delta = jnp.sum(near_prob * grad_near_prob, axis=2, keepdims=True) + jnp.sum(
            far_prob * grad_far_prob, axis=2, keepdims=True
        )
        grad_near_scores = (near_prob * (grad_near_prob - row_delta)).astype(jnp.bfloat16)
        grad_far_scores = (far_prob * (grad_far_prob - row_delta)).astype(jnp.bfloat16)
        grad_queries = (
            jnp.einsum(
                "hqk,khd->qhd", grad_near_scores, near_keys, preferred_element_type=jnp.float32
            )
            + jnp.einsum(
                "hqk,khd->qhd", grad_far_scores, far_keys, preferred_element_type=jnp.float32
            )
        ) * score_scale
        grad_near_keys = (
            jnp.einsum(
                "hqk,qhd->khd", grad_near_scores, queries, preferred_element_type=jnp.float32
            )
            * score_scale
        )
        grad_far_keys = (
            jnp.einsum("hqk,qhd->khd", grad_far_scores, queries, preferred_element_type=jnp.float32)
            * score_scale
        )
        grad_extended = jnp.concatenate(
            [grad_near_keys.reshape(-1, model_width), grad_near_values.reshape(-1, model_width)],
            axis=1,
        )
        grad_pool_ext = jnp.concatenate(
            [grad_far_keys.reshape(-1, model_width), grad_far_values.reshape(-1, model_width)],
            axis=1,
        )
        pool_edges = jnp.concatenate(
            [grad_pool_ext[:pool_half], grad_pool_ext[-pool_half:]], axis=0
        )
        pool_returned = with_halo(pool_edges.astype(jnp.bfloat16), (("seq", 0),), pool_half).astype(
            pool_edges.dtype
        )
        grad_pooled = add_rims(grad_pool_ext[pool_half:-pool_half], pool_returned, pool_half)
        pool_value, pool_back = jax.vjp(
            lambda ext_in, taps_part: pool_local(ext_in, taps_part, seg_window),
            ext_float,
            taps_float,
        )
        grad_ext_pool, grad_taps = pool_back(grad_pooled)
        grad_extended = grad_extended + grad_ext_pool
        token_edges = jnp.concatenate(
            [grad_extended[:NEAR], grad_extended[-NEAR:]], axis=0
        )
        token_returned = with_halo(
            token_edges.astype(jnp.bfloat16), (("seq", 0),), NEAR
        ).astype(token_edges.dtype)
        grad_kv = add_rims(grad_extended[NEAR:-NEAR], token_returned, NEAR)
        grad_projected = jnp.concatenate(
            [grad_queries.reshape(block_rows, model_width), grad_kv], axis=1
        ).astype(jnp.bfloat16)
        grad_qkvw = jnp.dot(normed.T, grad_projected, preferred_element_type=jnp.float32)
        grad_normed = jnp.dot(grad_projected, back_qkv.T, preferred_element_type=jnp.float32)
        norm_value_one, norm_back_one = jax.vjp(layer_norm, inputs, gain_float, bias_float)
        grad_in_part, grad_gain_one, grad_bias_one = norm_back_one(grad_normed)
        input_grads.append(grad_middle + grad_in_part)
        shares = (
            lax.psum_scatter(grad_gain_one, ("dp", "seq"), scatter_dimension=0, tiled=True),
            lax.psum_scatter(grad_bias_one, ("dp", "seq"), scatter_dimension=0, tiled=True),
            lax.psum_scatter(grad_qkvw, ("dp", "seq"), scatter_dimension=0, tiled=True),
            lax.psum_scatter(grad_taps, ("dp", "seq"), scatter_dimension=1, tiled=True),
            lax.psum_scatter(grad_outw, ("dp", "seq"), scatter_dimension=0, tiled=True),
            lax.psum_scatter(grad_gain_two, ("dp", "seq"), scatter_dimension=0, tiled=True),
            lax.psum_scatter(grad_bias_two, ("dp", "seq"), scatter_dimension=0, tiled=True),
            lax.psum_scatter(grad_upw, ("dp", "seq"), scatter_dimension=0, tiled=True),
            lax.psum_scatter(grad_down, ("dp", "seq"), scatter_dimension=1, tiled=True),
        )
        if summed is None:
            summed = shares
        else:
            summed = jax.tree.map(jnp.add, summed, shares)
    return (
        jnp.stack(outputs),
        jnp.stack(input_grads),
        summed[0],
        summed[1],
        summed[2],
        summed[3],
        summed[4],
        summed[5],
        summed[6],
        summed[7],
        summed[8],
    )


def chained(
    tokens, segments, cotangent, ln1_gain, ln1_bias, w_qkv, pool_taps, w_out, ln2_gain, ln2_bias, w_up, w_down,
):
    small = small_share(pool_taps, ln1_gain, ln1_bias, ln2_gain, ln2_bias)
    wq, wo, wu, wd, taps, gains, h1, q, kv, pe, att, bias, lse, same = front(
        tokens, segments, w_qkv, w_out, w_up, w_down.T, small
    )
    flat, split = (1024, 768), (2, 512, 768)
    out, _, g_in, g_wq, g_wo, g_wu, g_wd, g_small = back_part(
        tokens.reshape(flat), att.reshape(flat), cotangent.reshape(flat), wo, wu, wd,
        q, kv, pe, bias, h1, wq, taps, gains, same, lse,
    )
    return (
        out.reshape(split), g_in.reshape(split), g_small[5, :24], g_small[6, :24], g_wq, g_small[0:5, :48], g_wo,
        g_small[7, :24], g_small[8, :24], g_wu, g_wd.T,
    )


def solution(mesh):
    both = ("dp", "seq")
    row, tok, first, second = P(both), P("dp", "seq", None), P(both, None), P(None, both)
    small_mesh = mesh.shape["dp"] == 2 and mesh.shape["seq"] == 16
    return jax.shard_map(
        chained if small_mesh else shards,
        mesh=mesh,
        in_specs=(tok, P("dp", None), tok, row, row, first, second, first, row, row, first, second),
        out_specs=(tok, tok, row, row, first, second, first, row, row, first, second),
        check_vma=False,
    )
```
